256 devices in a mesh: row: 16 (over z, y_hi), col: 4 (over x), depth: 4 (over y_lo, core).
Axes of the slice: x: 4, y: 4 (y_hi: 2, y_lo: 2; y = y_hi * 2 + y_lo), z: 8, core: 2. Of those that a mesh axis runs over, the one named last changes fastest.
Arguments:
- integrals: bfloat16 [16384, 5120], P('row', 'depth'), may hold values from -0.25 to 0.25
- amplitudes: bfloat16 [160, 32, 10000], P('depth', 'row', 'col'), may hold values from -6 to 6
- ab_irrep: int32 [16384], P('row'), may hold values from 0 to 7
- cd_irrep: int32 [5120], P('depth'), may hold values from 0 to 7
Outputs:
- residual: bfloat16 [16384, 10000], P(('row', 'depth'), 'col')
The draws below stay inside these ranges and needn't reach their ends.
All inputs are finite; a program needn't handle non-finite values.
Results may differ from the reference program's by a relative error of at most 0.001.
Values may be sent and summed in bfloat16 or wider, within the bound.
A program may use at most 192 MiB of HBM per device.

```python
import jax
import jax.numpy as jnp

OCC = 100
SLAB = 256
SLABS = 20
KB = 32
CDK = 5120
CDB = 160
PAIRS = 10000
ABROWS = 16384


def set_ends(drawn, key, smallest, top_value):
    longest = drawn.shape.index(max(drawn.shape))
    spots = []
    for shift in (0, 1):
        where = [jax.random.randint(jax.random.fold_in(key, axis), (), 0, length) for axis, length in enumerate(drawn.shape)]
        where[longest] = (where[longest] + shift) % drawn.shape[longest]
        spots.append(tuple(where))
    return drawn.at[spots[0]].set(smallest).at[spots[1]].set(top_value)


def steps_of(stream_key, extent, shards, least, high):
    def one(position, shards_of):
        draws = jax.random.uniform(jax.random.fold_in(jax.random.fold_in(stream_key, 6), position), (shards_of,), jnp.float32, least / len(shards), high / len(shards))
        return jnp.repeat(jnp.exp(draws), extent[position] // shards_of).reshape((-1,) + (1,) * (len(extent) - position - 1))

    factor_of = one(*shards[0])
    for cut in shards[1:]:
        factor_of = factor_of * one(*cut)
    return factor_of


def scatter_about(stream_key, shape, scale, reach, cuts=(), held_as=jnp.bfloat16):
    values = scale * jax.random.normal(stream_key, shape, jnp.float32)
    if cuts:
        values = values * steps_of(stream_key, shape, cuts, -0.22, 0.18)
    return jnp.clip(values, -reach, reach).astype(held_as)


def setup_inputs(seed: int = 0) -> dict:
    key_list = jax.random.split(jax.random.key(seed), 5)
    return {
        "integrals": scatter_about(key_list[0], (ABROWS, CDK), (SLABS * SLAB // 8) ** -0.5, 0.25, ((0, 16), (1, 4))),
        "amplitudes": scatter_about(key_list[1], (CDB, KB, PAIRS), 1.0, 6.0, ((0, 4), (1, 16), (2, 4))),
        "ab_irrep": set_ends(jax.random.randint(key_list[2], (ABROWS,), 0, 8), jax.random.fold_in(key_list[2], 1), 0, 7).astype(jnp.int32),
        "cd_irrep": set_ends(jax.random.randint(key_list[3], (CDK,), 0, 8), jax.random.fold_in(key_list[3], 1), 0, 7).astype(jnp.int32),
    }


def reference(integrals, amplitudes, ab_irrep, cd_irrep):
    keep = ab_irrep[:, None] == cd_irrep[None, :]
    masked = jnp.where(keep, integrals, jnp.zeros_like(integrals))
    flat_amps = amplitudes.reshape(CDB * KB, OCC * OCC)
    ladder = jnp.dot(masked, flat_amps, preferred_element_type=jnp.float32)
    cube = ladder.reshape(ABROWS, OCC, OCC)
    result = cube - jnp.swapaxes(cube, 1, 2)
    return result.reshape(ABROWS, OCC * OCC).astype(jnp.bfloat16)
```

```python
import numpy as np

import jax
import jax.numpy as jnp
from jax import lax
from jax.experimental import pallas as pl
from jax.experimental.pallas import tpu as pltpu
from jax.sharding import PartitionSpec as P

OCC = 100
SUB = 25
NZ = 8
LANES = 128
CHUNKS = 10
HALF = 640
PAD = 15
PAIRS = CHUNKS * LANES
ROWS_T = 80
DEPTH = 1280
OUT_ROWS = 256
WIDE = 2560
MESH = pl.DeviceIdType.MESH


def iota(shape, dim):
    return lax.broadcasted_iota(jnp.int32, shape, dim)


def div25(v):
    return (v * 5243) >> 17


def div100(v):
    return (v * 5243) >> 19


def one_hot(cond):
    return jnp.where(cond, 1.0, 0.0).astype(jnp.bfloat16)


def dot(a, b):
    return jnp.dot(a, b, preferred_element_type=jnp.float32)


def band(n):
    lanes = np.arange(n * LANES, (n + 1) * LANES) - PAD
    lanes = lanes[(lanes >= 0) & (lanes < SUB * SUB)]
    first = 100 * (lanes // SUB) + lanes % SUB
    low = first.min() // LANES * LANES
    high = -(-(first.max() + 76) // LANES) * LANES
    return int(low), int(min(high, WIDE))


def kernel(
    t_ref, ab_ref, cd_ref, v_hbm, out_ref,
    v_ref, vp_ref, pk_ref, pt_ref, x_ref, wsend, wrecv, bq, sc_ref, bhl,
    csend, crecv, ysend, yrecv, own, r_own, r_recv, g_ref, src_ref, sgn_ref, acc_ref,
    v_sem, w_ss, w_rs, h_ss, h_rs, zr_ss, zr_rs, zl_ss, zl_rs, c_ss, c_rs, y_ss, y_rs, m_ss, m_rs,
):
    row, c, depth = lax.axis_index("row"), lax.axis_index("col"), lax.axis_index("depth")
    z, yh = row // 2, row % 2
    yl, core = depth // 2, depth % 2
    d_right = ((row + 2) % 16, c, depth)
    d_left = ((row + 14) % 16, c, depth)
    d_hi = (2 * z + 1 - yh, c, depth)
    d_core = (row, c, 2 * yl + 1 - core)
    d_lo = (row, c, 2 * (1 - yl) + core)
    x_next = (row, (c + 1) % 4, depth)
    x_opp = (row, (c + 2) % 4, depth)
    x_prev = (row, (c + 3) % 4, depth)

    def copy(src, dst, ss, rs, dev):
        return pltpu.make_async_remote_copy(
            src_ref=src, dst_ref=dst, send_sem=ss, recv_sem=rs, device_id=dev, device_id_type=MESH
        )

    v_copy = pltpu.make_async_copy(v_hbm, v_ref, v_sem)
    v_copy.start()

    barrier = pltpu.get_barrier_semaphore()
    for dev in (d_right, d_left, d_hi, d_core, d_lo, x_next, x_opp, x_prev):
        pl.semaphore_signal(barrier, inc=1, device_id=dev, device_id_type=MESH)

    u = iota((1, HALF), 1) - PAD
    a = div25(u)
    b = u - SUB * a
    flip = jnp.where(u >= 0, PAD + SUB * b + a, -1)
    lower = b <= a
    pt_ref[...] = one_hot(iota((HALF, HALF), 0) == flip)

    for n in range(HALF // LANES):
        low, high = band(n)
        u = iota((1, LANES), 1) + (n * LANES - PAD)
        a = div25(u)
        first = 100 * a + (u - SUB * a)
        r = iota((high - low, LANES), 0) + low
        mats = []
        for g in range(4):
            want = jnp.where((u >= 0), first + SUB * ((c + g) % 4), -1)
            mats.append(one_hot(r == want))
        got = dot(t_ref[:, low:high], jnp.concatenate(mats, axis=1)).astype(jnp.bfloat16)
        for g in range(4):
            x_ref[g, :, n * LANES:(n + 1) * LANES] = got[:, g * LANES:(g + 1) * LANES]

    wsend[0] = dot(x_ref[3], pt_ref[...]).astype(jnp.bfloat16)
    wsend[1] = dot(x_ref[2], pt_ref[...]).astype(jnp.bfloat16)
    pl.semaphore_wait(barrier, 8)
    w0 = copy(wsend.at[0], wrecv.at[0], w_ss.at[0], w_rs.at[0], x_prev)
    w1 = copy(wsend.at[1], wrecv.at[1], w_ss.at[1], w_rs.at[1], x_opp)
    w1.start()
    w0.start()
    x0 = x_ref[0]
    diag = x0.astype(jnp.float32) - dot(x0, pt_ref[...])

    k = iota((1, DEPTH), 1)
    zz = (k * 3277) >> 19
    rem = k - 160 * zz
    hh = jnp.where(rem >= 80, 1, 0)
    m = rem - 80 * hh
    from_k = 32 * (m >> 1) + 4 * zz + 2 * hh + (m & 1)

    def make_pk(i, _):
        base = pl.multiple_of(i * 256, 256)
        pk_ref[pl.ds(base, 256), :] = one_hot(iota((256, DEPTH), 0) + base == from_k)
        return 0

    lax.fori_loop(0, DEPTH // 256, make_pk, 0)
    v_copy.wait()

    def make_vp(i, _):
        base = pl.multiple_of(i * 128, 128)
        rows = pl.ds(base, 128)
        keep = ab_ref[rows, :] == cd_ref[...]
        masked = jnp.where(keep, v_ref[rows, :].astype(jnp.float32), 0.0).astype(jnp.bfloat16)
        vp_ref[rows, :] = dot(masked, pk_ref[...]).astype(jnp.bfloat16)
        return 0

    lax.fori_loop(0, 8, make_vp, 0)

    w0.wait_recv()
    w1.wait_recv()
    ta1 = x_ref[1].astype(jnp.float32) - wrecv[0].astype(jnp.float32)
    ta2 = jnp.where(lower, x_ref[2].astype(jnp.float32) - wrecv[1].astype(jnp.float32), diag)
    biggest = jnp.maximum(
        jnp.max(jnp.abs(ta1), axis=1, keepdims=True), jnp.max(jnp.abs(ta2), axis=1, keepdims=True)
    )
    exponent = jnp.ceil(jnp.log2(jnp.maximum(biggest, 1e-30))) - 15.0
    scale = jnp.exp2(-exponent)

    def coded(v):
        return jnp.clip(jnp.floor(v * scale + 0.5), -32767.0, 32767.0)

    q2 = coded(ta2)
    q1 = coded(ta1)
    q2 = jnp.where(iota((ROWS_T, HALF), 1) < PAD, jnp.broadcast_to(exponent, (ROWS_T, HALF)), q2)
    for n in range(CHUNKS):
        q = q2 if n < 5 else q1
        part = q[:, (n % 5) * LANES:(n % 5 + 1) * LANES]
        bq[n, z, yh] = part.astype(jnp.int32).astype(jnp.int16)

    def hi_copy(n):
        return copy(bq.at[n, z, yh], bq.at[n, z, yh], h_ss.at[n], h_rs.at[n], d_hi)

    def right_copy(n, s):
        at = (z - s + NZ) % NZ
        return copy(bq.at[n, at], bq.at[n, at], zr_ss.at[n, s], zr_rs.at[n, s], d_right)

    def left_copy(n, s):
        at = (z + s) % NZ
        return copy(bq.at[n, at], bq.at[n, at], zl_ss.at[n, s], zl_rs.at[n, s], d_left)

    def right_last(n):
        at = (z - 3 + NZ) % NZ
        return copy(bq.at[n, at, 0], bq.at[n, at, 0], zr_ss.at[n, 3], zr_rs.at[n, 3], d_right)

    def left_last(n):
        at = (z + 3) % NZ
        return copy(bq.at[n, at, 1], bq.at[n, at, 1], zl_ss.at[n, 3], zl_rs.at[n, 3], d_left)

    def core_copy(n, h):
        return copy(csend.at[n, h], crecv.at[n, h], c_ss.at[n, h], c_rs.at[n, h], d_core)

    def lo_copy(n):
        return copy(ysend.at[n], yrecv.at[n], y_ss.at[n], y_rs.at[n], d_lo)

    def mirror_copy(n):
        to = (row, (c + 2 - n // 5) % 4, depth)
        return copy(r_own.at[n], r_recv.at[n], m_ss.at[n], m_rs.at[n], to)

    hi_copy(0).start()
    hi_copy(1).start()

    lane = iota((1, WIDE), 1)
    a = div100(lane)
    j = lane - OCC * a
    grp = div25(j)
    b = j - SUB * grp
    rel = (grp - c + 4) % 4
    direct = PAD + SUB * a + b
    turned = PAD + SUB * b + a
    src = jnp.where(
        rel == 0,
        jnp.where(b > a, direct, jnp.where(b < a, turned, -1)),
        jnp.where(
            rel == 1,
            HALF + direct,
            jnp.where(rel == 2, jnp.where(b <= a, direct, 2048 + turned), 2048 + HALF + turned),
        ),
    )
    src_ref[...] = jnp.where(lane < OCC * SUB, src, -1)
    minus = ((rel == 0) & (b < a)) | ((rel == 2) & (b > a)) | (rel == 3)
    sgn_ref[...] = jnp.where(minus, -1.0, 1.0)
    acc_ref[...] = jnp.zeros_like(acc_ref)

    def block(yl_at, core_at):
        at = pl.multiple_of((2 * yl_at + core_at) * OUT_ROWS, OUT_ROWS)
        both = dot(vp_ref[pl.ds(at, OUT_ROWS), :], bhl[...])
        return both[:, :LANES] + both[:, LANES:]

    def step(t, _):
        n4 = t - 3

        @pl.when((n4 >= 0) & (n4 < CHUNKS))
        def _():
            right_copy(n4, 2).wait_recv()
            right_last(n4).start()
            left_copy(n4, 2).wait_recv()
            left_last(n4).start()

        n3 = t - 2

        @pl.when((n3 >= 0) & (n3 < CHUNKS))
        def _():
            right_copy(n3, 1).wait_recv()
            right_copy(n3, 2).start()
            left_copy(n3, 1).wait_recv()
            left_copy(n3, 2).start()

        n2 = t - 1

        @pl.when((n2 >= 0) & (n2 < CHUNKS))
        def _():
            right_copy(n2, 0).wait_recv()
            right_copy(n2, 1).start()
            left_copy(n2, 0).wait_recv()
            left_copy(n2, 1).start()

        @pl.when(t + 2 < CHUNKS)
        def _():
            hi_copy(t + 2).start()

        @pl.when(t < CHUNKS)
        def _():
            hi_copy(t).wait_recv()
            right_copy(t, 0).start()
            left_copy(t, 0).start()

        n = t - 4

        @pl.when((n >= 0) & (n < CHUNKS))
        def _():
            right_last(n).wait_recv()
            left_last(n).wait_recv()
            q = bq[n].reshape(DEPTH, LANES).astype(jnp.int32)

            @pl.when(n == 0)
            def _():
                sc_ref[...] = jnp.broadcast_to(jnp.exp2(q[:, 0:1].astype(jnp.float32)), (DEPTH, LANES))

            s = sc_ref[...]
            hi = (q + 128) >> 8
            lo = q - (hi << 8)
            bhl[:, :LANES] = (hi.astype(jnp.float32) * (s * 256.0)).astype(jnp.bfloat16)
            bhl[:, LANES:] = (lo.astype(jnp.float32) * s).astype(jnp.bfloat16)
            csend[n, 0] = block(1 - yl, 1 - core)
            core_copy(n, 0).start()
            csend[n, 1] = block(yl, 1 - core)
            core_copy(n, 1).start()
            part = block(1 - yl, core)
            core_copy(n, 0).wait_recv()
            ysend[n] = part + crecv[n, 0]
            lo_copy(n).start()
            part = block(yl, core)
            core_copy(n, 1).wait_recv()
            own[n] = part + crecv[n, 1]

        f = t - 5

        @pl.when((f >= 0) & (f < CHUNKS))
        def _():
            lo_copy(f).wait_recv()
            r_own[f] = (own[f] + yrecv[f]).astype(jnp.bfloat16)
            mirror_copy(f).start()

        @pl.when(t < CHUNKS)
        def _():
            r = iota((2 * LANES, 512), 0)
            r = r + (t * LANES + jnp.where(r >= LANES, 2048 - LANES, 0))
            for w in range(WIDE // 512):
                at = slice(w * 512, (w + 1) * 512)
                g_ref[t, :, at] = jnp.where(r == src_ref[:, at], sgn_ref[:, at], 0.0).astype(jnp.bfloat16)

        h = t - 6

        @pl.when((h >= 0) & (h < CHUNKS))
        def _():
            mirror_copy(h).wait_recv()
            both = jnp.concatenate([r_own[h], r_recv[h]], axis=1)
            for w in range(WIDE // 512):
                at = slice(w * 512, (w + 1) * 512)
                acc_ref[:, at] += dot(both, g_ref[h, :, at])

        return 0

    lax.fori_loop(0, CHUNKS + 6, step, 0)
    out_ref[...] = acc_ref[:, : OCC * SUB].astype(jnp.bfloat16)

    w0.wait_send()
    w1.wait_send()

    def drain(n, _):
        hi_copy(n).wait_send()
        for s in range(3):
            right_copy(n, s).wait_send()
            left_copy(n, s).wait_send()
        right_last(n).wait_send()
        left_last(n).wait_send()
        core_copy(n, 0).wait_send()
        core_copy(n, 1).wait_send()
        lo_copy(n).wait_send()
        mirror_copy(n).wait_send()
        return 0

    lax.fori_loop(0, CHUNKS, drain, 0)


def local(integrals, amplitudes, ab_irrep, cd_irrep):
    amps = jnp.pad(amplitudes.reshape(ROWS_T, OCC * SUB), ((0, 0), (0, WIDE - OCC * SUB)))
    vmem = pl.BlockSpec(memory_space=pltpu.VMEM)
    bf, f32 = jnp.bfloat16, jnp.float32
    dma = pltpu.SemaphoreType.DMA
    n = CHUNKS
    scratch = [
        pltpu.VMEM((1024, DEPTH), bf),
        pltpu.VMEM((1024, DEPTH), bf),
        pltpu.VMEM((DEPTH, DEPTH), bf),
        pltpu.VMEM((HALF, HALF), bf),
        pltpu.VMEM((4, ROWS_T, HALF), bf),
        pltpu.VMEM((2, ROWS_T, HALF), bf),
        pltpu.VMEM((2, ROWS_T, HALF), bf),
        pltpu.VMEM((n, NZ, 2, ROWS_T, LANES), jnp.int16),
        pltpu.VMEM((DEPTH, LANES), f32),
        pltpu.VMEM((DEPTH, 2 * LANES), bf),
        pltpu.VMEM((n, 2, OUT_ROWS, LANES), f32),
        pltpu.VMEM((n, 2, OUT_ROWS, LANES), f32),
        pltpu.VMEM((n, OUT_ROWS, LANES), f32),
        pltpu.VMEM((n, OUT_ROWS, LANES), f32),
        pltpu.VMEM((n, OUT_ROWS, LANES), f32),
        pltpu.VMEM((n, OUT_ROWS, LANES), bf),
        pltpu.VMEM((n, OUT_ROWS, LANES), bf),
        pltpu.VMEM((n, 2 * LANES, WIDE), bf),
        pltpu.VMEM((1, WIDE), jnp.int32),
        pltpu.VMEM((1, WIDE), f32),
        pltpu.VMEM((OUT_ROWS, WIDE), f32),
        dma,
        dma((2,)), dma((2,)),
        dma((n,)), dma((n,)),
        dma((n, 4)), dma((n, 4)),
        dma((n, 4)), dma((n, 4)),
        dma((n, 2)), dma((n, 2)),
        dma((n,)), dma((n,)),
        dma((n,)), dma((n,)),
    ]
    return pl.pallas_call(
        kernel,
        out_shape=jax.ShapeDtypeStruct((OUT_ROWS, OCC * SUB), bf),
        in_specs=[vmem, vmem, vmem, pl.BlockSpec(memory_space=pl.ANY)],
        out_specs=vmem,
        scratch_shapes=scratch,
        compiler_params=pltpu.CompilerParams(
            collective_id=0, has_side_effects=True, vmem_limit_bytes=58 * 2**20
        ),
        name="ladder",
    )(amps, ab_irrep.reshape(1024, 1), cd_irrep.reshape(1, DEPTH), integrals)


def solution(mesh):
    in_specs = (P("row", "depth"), P("depth", "row", "col"), P("row"), P("depth"))
    out_specs = P(("row", "depth"), "col")
    return jax.shard_map(local, mesh=mesh, in_specs=in_specs, out_specs=out_specs, check_vma=False)
```

```python
import numpy as np

import jax
import jax.numpy as jnp
from jax import lax
from jax.experimental import pallas as pl
from jax.experimental.pallas import tpu as pltpu
from jax.sharding import PartitionSpec as P

OCC = 100
SUB = 25
NZ = 8
LANES = 128
CHUNKS = 10
HALF = 640
PAD = 15
PAIRS = CHUNKS * LANES
ROWS_T = 80
DEPTH = 1280
OUT_ROWS = 256
WIDE = 2560
MESH = pl.DeviceIdType.MESH


def iota(shape, dim):
    return lax.broadcasted_iota(jnp.int32, shape, dim)


def div25(v):
    return (v * 5243) >> 17


def div100(v):
    return (v * 5243) >> 19


def one_hot(cond):
    return jnp.where(cond, 1.0, 0.0).astype(jnp.bfloat16)


def dot(a, b):
    return jnp.dot(a, b, preferred_element_type=jnp.float32)


def band(n):
    lanes = np.arange(n * LANES, (n + 1) * LANES) - PAD
    lanes = lanes[(lanes >= 0) & (lanes < SUB * SUB)]
    first = 100 * (lanes // SUB) + lanes % SUB
    low = first.min() // LANES * LANES
    high = -(-(first.max() + 76) // LANES) * LANES
    return int(low), int(min(high, WIDE))


def kernel(
    amp_ref, ab_ref, cd_ref, v_hbm, out_ref,
    t_ref, v_ref, vp_ref, pk_ref, pt_ref, x_ref, wsend, wrecv, bq, sc_ref, bhl,
    csend, crecv, ysend, ycode, yrecv, own, r_own, r_recv, g_ref, src_ref, sgn_ref, acc_ref,
    v_sem, w_ss, w_rs, h_ss, h_rs, zr_ss, zr_rs, zl_ss, zl_rs, c_ss, c_rs, y_ss, y_rs, m_ss, m_rs,
):
    row, c, depth = lax.axis_index("row"), lax.axis_index("col"), lax.axis_index("depth")
    z, yh = row // 2, row % 2
    yl, core = depth // 2, depth % 2
    d_right = ((row + 2) % 16, c, depth)
    d_left = ((row + 14) % 16, c, depth)
    d_hi = (2 * z + 1 - yh, c, depth)
    d_core = (row, c, 2 * yl + 1 - core)
    d_lo = (row, c, 2 * (1 - yl) + core)
    x_next = (row, (c + 1) % 4, depth)
    x_opp = (row, (c + 2) % 4, depth)
    x_prev = (row, (c + 3) % 4, depth)

    def copy(src, dst, ss, rs, dev):
        return pltpu.make_async_remote_copy(
            src_ref=src, dst_ref=dst, send_sem=ss, recv_sem=rs, device_id=dev, device_id_type=MESH
        )

    v_copy = pltpu.make_async_copy(v_hbm, v_ref, v_sem)
    v_copy.start()

    barrier = pltpu.get_barrier_semaphore()
    for dev in (d_right, d_left, d_hi, d_core, d_lo, x_next, x_opp, x_prev):
        pl.semaphore_signal(barrier, inc=1, device_id=dev, device_id_type=MESH)

    t_ref[:, 2432:] = jnp.zeros((ROWS_T, LANES), jnp.bfloat16)
    t_ref[:, : OCC * SUB] = amp_ref[...]

    u = iota((1, HALF), 1) - PAD
    a = div25(u)
    b = u - SUB * a
    flip = jnp.where(u >= 0, PAD + SUB * b + a, -1)
    lower = b <= a
    pt_ref[...] = one_hot(iota((HALF, HALF), 0) == flip)

    for n in range(HALF // LANES):
        low, high = band(n)
        u = iota((1, LANES), 1) + (n * LANES - PAD)
        a = div25(u)
        first = 100 * a + (u - SUB * a)
        r = iota((high - low, LANES), 0) + low
        mats = []
        for g in range(4):
            want = jnp.where((u >= 0), first + SUB * ((c + g) % 4), -1)
            mats.append(one_hot(r == want))
        got = dot(t_ref[:, low:high], jnp.concatenate(mats, axis=1)).astype(jnp.bfloat16)
        for g in range(4):
            x_ref[g, :, n * LANES:(n + 1) * LANES] = got[:, g * LANES:(g + 1) * LANES]

    wsend[0] = dot(x_ref[3], pt_ref[...]).astype(jnp.bfloat16)
    wsend[1] = dot(x_ref[2], pt_ref[...]).astype(jnp.bfloat16)
    pl.semaphore_wait(barrier, 8)
    w0 = copy(wsend.at[0], wrecv.at[0], w_ss.at[0], w_rs.at[0], x_prev)
    w1 = copy(wsend.at[1], wrecv.at[1], w_ss.at[1], w_rs.at[1], x_opp)
    w1.start()
    w0.start()
    x0 = x_ref[0]
    diag = x0.astype(jnp.float32) - dot(x0, pt_ref[...])

    k = iota((1, DEPTH), 1)
    zz = (k * 3277) >> 19
    rem = k - 160 * zz
    hh = jnp.where(rem >= 80, 1, 0)
    m = rem - 80 * hh
    from_k = 32 * (m >> 1) + 4 * zz + 2 * hh + (m & 1)

    def make_pk(i, _):
        base = pl.multiple_of(i * 256, 256)
        pk_ref[pl.ds(base, 256), :] = one_hot(iota((256, DEPTH), 0) + base == from_k)
        return 0

    lax.fori_loop(0, DEPTH // 256, make_pk, 0)
    v_copy.wait()

    def make_vp(i, _):
        base = pl.multiple_of(i * 128, 128)
        rows = pl.ds(base, 128)
        label = jnp.broadcast_to(ab_ref[rows].reshape(1, 128), (128, 128)).T
        keep = jnp.concatenate([label] * 10, axis=1) == cd_ref[...].reshape(1, DEPTH)
        masked = jnp.where(keep, v_ref[rows, :].astype(jnp.float32), 0.0).astype(jnp.bfloat16)
        vp_ref[rows, :] = dot(masked, pk_ref[...]).astype(jnp.bfloat16)
        return 0

    lax.fori_loop(0, 4, make_vp, 0)

    w0.wait_recv()
    w1.wait_recv()
    ta1 = x_ref[1].astype(jnp.float32) - wrecv[0].astype(jnp.float32)
    ta2 = jnp.where(lower, x_ref[2].astype(jnp.float32) - wrecv[1].astype(jnp.float32), diag)
    biggest = jnp.maximum(
        jnp.max(jnp.abs(ta1), axis=1, keepdims=True), jnp.max(jnp.abs(ta2), axis=1, keepdims=True)
    )
    exponent = jnp.ceil(jnp.log2(jnp.maximum(biggest, 1e-30))) - 15.0
    scale = jnp.exp2(-exponent)

    def coded(v):
        return jnp.clip(jnp.floor(v * scale + 0.5), -32767.0, 32767.0)

    q2 = coded(ta2)
    q1 = coded(ta1)
    q2 = jnp.where(iota((ROWS_T, HALF), 1) < PAD, jnp.broadcast_to(exponent, (ROWS_T, HALF)), q2)
    for n in range(CHUNKS):
        q = q2 if n < 5 else q1
        part = q[:, (n % 5) * LANES:(n % 5 + 1) * LANES]
        bq[n, z, yh] = part.astype(jnp.int32).astype(jnp.int16)

    def hi_copy(n):
        return copy(bq.at[n, z, yh], bq.at[n, z, yh], h_ss.at[n], h_rs.at[n], d_hi)

    def first_copies(n, side):
        at = yh if side == 0 else 1 - yh
        ref = bq.at[n, z, at]
        sem = 4 * side
        return (
            copy(ref, ref, zr_ss.at[n, sem], zr_rs.at[n, sem], d_right),
            copy(ref, ref, zl_ss.at[n, sem], zl_rs.at[n, sem], d_left),
        )

    def right_copy(n, s):
        at = (z - s + NZ) % NZ
        return copy(bq.at[n, at], bq.at[n, at], zr_ss.at[n, s], zr_rs.at[n, s], d_right)

    def left_copy(n, s):
        at = (z + s) % NZ
        return copy(bq.at[n, at], bq.at[n, at], zl_ss.at[n, s], zl_rs.at[n, s], d_left)

    def right_last(n):
        at = (z - 3 + NZ) % NZ
        return copy(bq.at[n, at, 0], bq.at[n, at, 0], zr_ss.at[n, 3], zr_rs.at[n, 3], d_right)

    def left_last(n):
        at = (z + 3) % NZ
        return copy(bq.at[n, at, 1], bq.at[n, at, 1], zl_ss.at[n, 3], zl_rs.at[n, 3], d_left)

    def core_copy(n, h):
        return copy(csend.at[n, h], crecv.at[n, h], c_ss.at[n, h], c_rs.at[n, h], d_core)

    def lo_copy(n):
        return copy(ycode.at[n], yrecv.at[n], y_ss.at[n], y_rs.at[n], d_lo)

    def mirror_copy(n):
        to = (row, (c + 2 - n // 5) % 4, depth)
        return copy(r_own.at[n], r_recv.at[n], m_ss.at[n], m_rs.at[n], to)

    def start_both(pair):
        for one in pair:
            one.start()

    def own_start(n, _):
        hi_copy(n).start()
        start_both(first_copies(n, 0))
        return 0

    lax.fori_loop(0, CHUNKS, own_start, 0)
    lax.fori_loop(4, 8, make_vp, 0)

    lane = iota((1, WIDE), 1)
    a = div100(lane)
    j = lane - OCC * a
    grp = div25(j)
    b = j - SUB * grp
    rel = (grp - c + 4) % 4
    direct = PAD + SUB * a + b
    turned = PAD + SUB * b + a
    src = jnp.where(
        rel == 0,
        jnp.where(b > a, direct, jnp.where(b < a, turned, -1)),
        jnp.where(
            rel == 1,
            HALF + direct,
            jnp.where(rel == 2, jnp.where(b <= a, direct, 2048 + turned), 2048 + HALF + turned),
        ),
    )
    src_ref[...] = jnp.where(lane < OCC * SUB, src, -1)
    minus = ((rel == 0) & (b < a)) | ((rel == 2) & (b > a)) | (rel == 3)
    sgn_ref[...] = jnp.where(minus, -1.0, 1.0)
    acc_ref[...] = jnp.zeros_like(acc_ref)

    def block(yl_at, core_at):
        at = pl.multiple_of((2 * yl_at + core_at) * OUT_ROWS, OUT_ROWS)
        both = dot(vp_ref[pl.ds(at, OUT_ROWS), :], bhl[...])
        return both[:, :LANES] + both[:, LANES:]

    def part_start(n):
        hi_copy(n).wait_recv()
        start_both(first_copies(n, 1))

    def forward(n, s):
        before = [(right_copy(n, s - 1), left_copy(n, s - 1))] if s > 1 else [first_copies(n, 0), first_copies(n, 1)]
        after = (right_last(n), left_last(n)) if s == 3 else (right_copy(n, s), left_copy(n, s))
        for side in range(2):
            for pair in before:
                pair[side].wait_recv()
            after[side].start()

    def make_g(n):
        r = iota((2 * LANES, 512), 0)
        r = r + (n * LANES + jnp.where(r >= LANES, 2048 - LANES, 0))
        for w in range(WIDE // 512):
            at = slice(w * 512, (w + 1) * 512)
            g_ref[n, :, at] = jnp.where(r == src_ref[:, at], sgn_ref[:, at], 0.0).astype(jnp.bfloat16)

    def expand(n):
        right_last(n).wait_recv()
        left_last(n).wait_recv()
        q = bq[n].reshape(DEPTH, LANES).astype(jnp.int32)

        @pl.when(n == 0)
        def _():
            sc_ref[...] = jnp.broadcast_to(jnp.exp2(q[:, 0:1].astype(jnp.float32)), (DEPTH, LANES))

        s = sc_ref[...]
        hi = (q + 128) >> 8
        lo = q - (hi << 8)
        bhl[:, :LANES] = (hi.astype(jnp.float32) * (s * 256.0)).astype(jnp.bfloat16)
        bhl[:, LANES:] = (lo.astype(jnp.float32) * s).astype(jnp.bfloat16)

    def to_core(n, h):
        csend[n, h] = block(yl if h else 1 - yl, 1 - core)
        core_copy(n, h).start()

    def core_sum(n):
        core_copy(n, 0).wait_recv()
        part = ysend[n] + crecv[n, 0]
        biggest = jnp.max(jnp.abs(part), axis=1, keepdims=True)
        ex = jnp.ceil(jnp.log2(jnp.maximum(biggest, 1e-30))) - 15.0
        ex = jnp.broadcast_to(ex, (OUT_ROWS, LANES))
        q = jnp.clip(jnp.floor(part * jnp.exp2(-ex) + 0.5), -32767.0, 32767.0)
        ycode[n, :OUT_ROWS] = q.astype(jnp.int32).astype(jnp.int16)
        turned = jnp.concatenate([ex[:LANES].T[:8], ex[LANES:].T[:8]], axis=0)
        ycode[n, OUT_ROWS:] = turned.astype(jnp.int32).astype(jnp.int16)
        lo_copy(n).start()
        core_copy(n, 1).wait_recv()
        own[n] += crecv[n, 1]

    def finish(n):
        lo_copy(n).wait_recv()
        ex = yrecv[n, OUT_ROWS:].astype(jnp.int32).astype(jnp.float32)
        for k in range(2):
            rows = slice(k * LANES, (k + 1) * LANES)
            scale = jnp.exp2(jnp.broadcast_to(ex[8 * k:8 * k + 1], (LANES, LANES)).T)
            got = yrecv[n, rows].astype(jnp.int32).astype(jnp.float32) * scale
            r_own[n, rows] = (own[n, rows] + got).astype(jnp.bfloat16)
        mirror_copy(n).start()

    def place(n):
        mirror_copy(n).wait_recv()
        both = jnp.concatenate([r_own[n], r_recv[n]], axis=1)
        for w in range(WIDE // 512):
            at = slice(w * 512, (w + 1) * 512)
            acc_ref[:, at] += dot(both, g_ref[n, :, at])

    def first_part(n, _):
        part_start(n)
        return 0

    lax.fori_loop(0, 5, first_part, 0)

    def early(n, _):
        forward(n, 1)
        make_g(n)
        return 0

    def middle(n, _):
        forward(n, 2)
        make_g(n + 5)
        return 0

    def late(n, _):
        forward(n, 3)
        part_start(n + 5)
        return 0

    lax.fori_loop(0, 5, early, 0)
    lax.fori_loop(0, 5, middle, 0)
    lax.fori_loop(0, 5, late, 0)

    def event(i):
        n = 5 + i % 5
        for s in range(1, 4):

            @pl.when(i // 5 == s - 1)
            def _():
                forward(n, s)

    def body(t, _):
        @pl.when(t < 5)
        def _():
            event(3 * t)

        expand(t)
        to_core(t, 0)
        to_core(t, 1)

        @pl.when(t < 5)
        def _():
            event(3 * t + 1)

        @pl.when(t >= 1)
        def _():
            core_sum(t - 1)

        ysend[t] = block(1 - yl, core)
        own[t] = block(yl, core)

        @pl.when(t < 5)
        def _():
            event(3 * t + 2)

        @pl.when(t >= 3)
        def _():
            finish(t - 3)

        return 0

    lax.fori_loop(0, CHUNKS, body, 0)

    def place_some(n, _):
        place(n)
        return 0

    def finish_some(n, _):
        finish(n)
        return 0

    lax.fori_loop(0, 3, place_some, 0)
    core_sum(9)
    lax.fori_loop(7, 9, finish_some, 0)
    lax.fori_loop(3, 6, place_some, 0)
    finish(9)
    lax.fori_loop(6, 10, place_some, 0)
    out_ref[...] = acc_ref[:, : OCC * SUB].astype(jnp.bfloat16)

    w0.wait_send()
    w1.wait_send()

    def drain(n, _):
        hi_copy(n).wait_send()
        for side in range(2):
            for one in first_copies(n, side):
                one.wait_send()
        for s in range(1, 3):
            right_copy(n, s).wait_send()
            left_copy(n, s).wait_send()
        right_last(n).wait_send()
        left_last(n).wait_send()
        core_copy(n, 0).wait_send()
        core_copy(n, 1).wait_send()
        lo_copy(n).wait_send()
        mirror_copy(n).wait_send()
        return 0

    lax.fori_loop(0, CHUNKS, drain, 0)


def local(integrals, amplitudes, ab_irrep, cd_irrep):
    amps = amplitudes.reshape(ROWS_T, OCC * SUB)
    vmem = pl.BlockSpec(memory_space=pltpu.VMEM)
    bf, f32 = jnp.bfloat16, jnp.float32
    dma = pltpu.SemaphoreType.DMA
    n = CHUNKS
    scratch = [
        pltpu.VMEM((ROWS_T, WIDE), bf),
        pltpu.VMEM((1024, DEPTH), bf),
        pltpu.VMEM((1024, DEPTH), bf),
        pltpu.VMEM((DEPTH, DEPTH), bf),
        pltpu.VMEM((HALF, HALF), bf),
        pltpu.VMEM((4, ROWS_T, HALF), bf),
        pltpu.VMEM((2, ROWS_T, HALF), bf),
        pltpu.VMEM((2, ROWS_T, HALF), bf),
        pltpu.VMEM((n, NZ, 2, ROWS_T, LANES), jnp.int16),
        pltpu.VMEM((DEPTH, LANES), f32),
        pltpu.VMEM((DEPTH, 2 * LANES), bf),
        pltpu.VMEM((n, 2, OUT_ROWS, LANES), f32),
        pltpu.VMEM((n, 2, OUT_ROWS, LANES), f32),
        pltpu.VMEM((n, OUT_ROWS, LANES), f32),
        pltpu.VMEM((n, OUT_ROWS + 16, LANES), jnp.int16),
        pltpu.VMEM((n, OUT_ROWS + 16, LANES), jnp.int16),
        pltpu.VMEM((n, OUT_ROWS, LANES), f32),
        pltpu.VMEM((n, OUT_ROWS, LANES), bf),
        pltpu.VMEM((n, OUT_ROWS, LANES), bf),
        pltpu.VMEM((n, 2 * LANES, WIDE), bf),
        pltpu.VMEM((1, WIDE), jnp.int32),
        pltpu.VMEM((1, WIDE), f32),
        pltpu.VMEM((OUT_ROWS, WIDE), f32),
        dma,
        dma((2,)), dma((2,)),
        dma((n,)), dma((n,)),
        dma((n, 5)), dma((n, 5)),
        dma((n, 5)), dma((n, 5)),
        dma((n, 2)), dma((n, 2)),
        dma((n,)), dma((n,)),
        dma((n,)), dma((n,)),
    ]
    return pl.pallas_call(
        kernel,
        out_shape=jax.ShapeDtypeStruct((OUT_ROWS, OCC * SUB), bf),
        in_specs=[vmem, vmem, vmem, pl.BlockSpec(memory_space=pl.ANY)],
        out_specs=vmem,
        scratch_shapes=scratch,
        compiler_params=pltpu.CompilerParams(
            collective_id=0, has_side_effects=True, vmem_limit_bytes=58 * 2**20
        ),
        name="ladder",
    )(amps, ab_irrep, cd_irrep, integrals)


def solution(mesh):
    in_specs = (P("row", "depth"), P("depth", "row", "col"), P("row"), P("depth"))
    out_specs = P(("row", "depth"), "col")
    return jax.shard_map(local, mesh=mesh, in_specs=in_specs, out_specs=out_specs, check_vma=False)
```

```python
import numpy as np

import jax
import jax.numpy as jnp
from jax import lax
from jax.experimental import pallas as pl
from jax.experimental.pallas import tpu as pltpu
from jax.sharding import PartitionSpec as P

OCC = 100
SUB = 25
NZ = 8
LANES = 128
CHUNKS = 10
HALF = 640
PAD = 15
FIRST = 6
LAST = CHUNKS - FIRST
ROWS_T = 80
DEPTH = 1280
OUT_ROWS = 256
WIDE = 2560
MESH = pl.DeviceIdType.MESH


def iota(shape, dim):
    return lax.broadcasted_iota(jnp.int32, shape, dim)


def div25(v):
    return (v * 5243) >> 17


def div100(v):
    return (v * 5243) >> 19


def one_hot(cond):
    return jnp.where(cond, 1.0, 0.0).astype(jnp.bfloat16)


def dot(a, b):
    return jnp.dot(a, b, preferred_element_type=jnp.float32)


def band(n):
    lanes = np.arange(n * LANES, (n + 1) * LANES) - PAD
    lanes = lanes[(lanes >= 0) & (lanes < SUB * SUB)]
    first = 100 * (lanes // SUB) + lanes % SUB
    low = first.min() // LANES * LANES
    high = -(-(first.max() + 76) // LANES) * LANES
    return int(low), int(min(high, WIDE))


def kernel(
    amp_ref, ab_ref, cd_ref, v_hbm, out_ref,
    t_ref, v_ref, vp_ref, pk_ref, pt_ref, x_ref, wsend, wrecv, bq, sc_ref, bhl,
    csend, crecv, ysend, ycode, yrecv, own, r_own, r_recv, g_ref, src_ref, sgn_ref, acc_ref,
    v_sem, w_ss, w_rs, h_ss, h_rs, zr_ss, zr_rs, zl_ss, zl_rs, c_ss, c_rs, y_ss, y_rs, m_ss, m_rs,
):
    row, c, depth = lax.axis_index("row"), lax.axis_index("col"), lax.axis_index("depth")
    z, yh = row // 2, row % 2
    yl, core = depth // 2, depth % 2
    d_right = ((row + 2) % 16, c, depth)
    d_left = ((row + 14) % 16, c, depth)
    d_hi = (2 * z + 1 - yh, c, depth)
    d_core = (row, c, 2 * yl + 1 - core)
    d_lo = (row, c, 2 * (1 - yl) + core)
    x_next = (row, (c + 1) % 4, depth)
    x_opp = (row, (c + 2) % 4, depth)
    x_prev = (row, (c + 3) % 4, depth)

    def copy(src, dst, ss, rs, dev):
        return pltpu.make_async_remote_copy(
            src_ref=src, dst_ref=dst, send_sem=ss, recv_sem=rs, device_id=dev, device_id_type=MESH
        )

    v_copy = pltpu.make_async_copy(v_hbm, v_ref, v_sem)
    v_copy.start()

    barrier = pltpu.get_barrier_semaphore()
    for dev in (d_right, d_left, d_hi, d_core, d_lo, x_next, x_opp, x_prev):
        pl.semaphore_signal(barrier, inc=1, device_id=dev, device_id_type=MESH)

    t_ref[:, 2432:] = jnp.zeros((ROWS_T, LANES), jnp.bfloat16)
    t_ref[:, : OCC * SUB] = amp_ref[...].reshape(ROWS_T, OCC * SUB)

    u = iota((1, HALF), 1) - PAD
    a = div25(u)
    b = u - SUB * a
    flip = jnp.where(u >= 0, PAD + SUB * b + a, -1)
    lower = b <= a
    pt_ref[...] = one_hot(iota((HALF, HALF), 0) == flip)

    for n in range(HALF // LANES):
        low, high = band(n)
        u = iota((1, LANES), 1) + (n * LANES - PAD)
        a = div25(u)
        first = 100 * a + (u - SUB * a)
        r = iota((high - low, LANES), 0) + low
        mats = []
        for g in range(4):
            want = jnp.where((u >= 0), first + SUB * ((c + g) % 4), -1)
            mats.append(one_hot(r == want))
        got = dot(t_ref[:, low:high], jnp.concatenate(mats, axis=1)).astype(jnp.bfloat16)
        for g in range(4):
            x_ref[g, :, n * LANES:(n + 1) * LANES] = got[:, g * LANES:(g + 1) * LANES]

    wsend[0] = dot(x_ref[3], pt_ref[...]).astype(jnp.bfloat16)
    wsend[1] = dot(x_ref[2], pt_ref[...]).astype(jnp.bfloat16)
    pl.semaphore_wait(barrier, 8)
    w0 = copy(wsend.at[0], wrecv.at[0], w_ss.at[0], w_rs.at[0], x_prev)
    w1 = copy(wsend.at[1], wrecv.at[1], w_ss.at[1], w_rs.at[1], x_opp)
    w1.start()
    w0.start()
    x0 = x_ref[0]
    diag = x0.astype(jnp.float32) - dot(x0, pt_ref[...])

    k = iota((1, DEPTH), 1)
    zz = (k * 3277) >> 19
    rem = k - 160 * zz
    hh = jnp.where(rem >= 80, 1, 0)
    m = rem - 80 * hh
    from_k = 32 * (m >> 1) + 4 * zz + 2 * hh + (m & 1)

    def make_pk(i, _):
        base = pl.multiple_of(i * 256, 256)
        pk_ref[pl.ds(base, 256), :] = one_hot(iota((256, DEPTH), 0) + base == from_k)
        return 0

    lax.fori_loop(0, DEPTH // 256, make_pk, 0)
    v_copy.wait()

    def make_vp(i, _):
        base = pl.multiple_of(i * 128, 128)
        rows = pl.ds(base, 128)
        label = jnp.broadcast_to(ab_ref[rows].reshape(1, 128), (128, 128)).T
        keep = jnp.concatenate([label] * 10, axis=1) == cd_ref[...].reshape(1, DEPTH)
        masked = jnp.where(keep, v_ref[rows, :].astype(jnp.float32), 0.0).astype(jnp.bfloat16)
        vp_ref[rows, :] = dot(masked, pk_ref[...]).astype(jnp.bfloat16)
        return 0

    lax.fori_loop(0, 4, make_vp, 0)

    w0.wait_recv()
    w1.wait_recv()
    ta1 = x_ref[1].astype(jnp.float32) - wrecv[0].astype(jnp.float32)
    ta2 = jnp.where(lower, x_ref[2].astype(jnp.float32) - wrecv[1].astype(jnp.float32), diag)
    biggest = jnp.maximum(
        jnp.max(jnp.abs(ta1), axis=1, keepdims=True), jnp.max(jnp.abs(ta2), axis=1, keepdims=True)
    )
    exponent = jnp.ceil(jnp.log2(jnp.maximum(biggest, 1e-30))) - 15.0
    scale = jnp.exp2(-exponent)

    def coded(v):
        return jnp.clip(jnp.floor(v * scale + 0.5), -32767.0, 32767.0)

    q2 = coded(ta2)
    q1 = coded(ta1)
    q2 = jnp.where(iota((ROWS_T, HALF), 1) < PAD, jnp.broadcast_to(exponent, (ROWS_T, HALF)), q2)
    for n in range(CHUNKS):
        q = q2 if n < 5 else q1
        part = q[:, (n % 5) * LANES:(n % 5 + 1) * LANES]
        bq[n, z, yh] = part.astype(jnp.int32).astype(jnp.int16)

    def hi_copy(n):
        return copy(bq.at[n, z, yh], bq.at[n, z, yh], h_ss.at[n], h_rs.at[n], d_hi)

    def first_copies(n, side):
        at = yh if side == 0 else 1 - yh
        ref = bq.at[n, z, at]
        sem = 4 * side
        return (
            copy(ref, ref, zr_ss.at[n, sem], zr_rs.at[n, sem], d_right),
            copy(ref, ref, zl_ss.at[n, sem], zl_rs.at[n, sem], d_left),
        )

    def right_copy(n, s):
        at = (z - s + NZ) % NZ
        return copy(bq.at[n, at], bq.at[n, at], zr_ss.at[n, s], zr_rs.at[n, s], d_right)

    def left_copy(n, s):
        at = (z + s) % NZ
        return copy(bq.at[n, at], bq.at[n, at], zl_ss.at[n, s], zl_rs.at[n, s], d_left)

    def right_last(n):
        at = (z - 3 + NZ) % NZ
        return copy(bq.at[n, at, 0], bq.at[n, at, 0], zr_ss.at[n, 3], zr_rs.at[n, 3], d_right)

    def left_last(n):
        at = (z + 3) % NZ
        return copy(bq.at[n, at, 1], bq.at[n, at, 1], zl_ss.at[n, 3], zl_rs.at[n, 3], d_left)

    def core_copy(n, h):
        return copy(csend.at[n, h], crecv.at[n, h], c_ss.at[n, h], c_rs.at[n, h], d_core)

    def lo_copy(n):
        return copy(ycode.at[n], yrecv.at[n], y_ss.at[n], y_rs.at[n], d_lo)

    def mirror_copy(n):
        to = (row, (c + 2 - n // 5) % 4, depth)
        return copy(r_own.at[n], r_recv.at[n], m_ss.at[n], m_rs.at[n], to)

    def start_both(pair):
        for one in pair:
            one.start()

    def own_start(n, _):
        hi_copy(n).start()
        start_both(first_copies(n, 0))
        return 0

    lax.fori_loop(0, CHUNKS, own_start, 0)
    lax.fori_loop(4, 8, make_vp, 0)

    lane = iota((WIDE, LANES), 0)
    a = div100(lane)
    j = lane - OCC * a
    grp = div25(j)
    b = j - SUB * grp
    rel = (grp - c + 4) % 4
    direct = PAD + SUB * a + b
    turned = PAD + SUB * b + a
    src = jnp.where(
        rel == 0,
        jnp.where(b > a, direct, jnp.where(b < a, turned, -1)),
        jnp.where(
            rel == 1,
            HALF + direct,
            jnp.where(rel == 2, jnp.where(b <= a, direct, 2048 + turned), 2048 + HALF + turned),
        ),
    )
    src_ref[...] = jnp.where(lane < OCC * SUB, src, -1)
    minus = ((rel == 0) & (b < a)) | ((rel == 2) & (b > a)) | (rel == 3)
    sgn_ref[...] = jnp.where(minus, -1.0, 1.0)
    acc_ref[...] = jnp.zeros_like(acc_ref)

    def block(yl_at, core_at):
        at = pl.multiple_of((2 * yl_at + core_at) * OUT_ROWS, OUT_ROWS)
        both = dot(vp_ref[pl.ds(at, OUT_ROWS), :], bhl[...])
        return both[:, :LANES] + both[:, LANES:]

    def part_start(n):
        hi_copy(n).wait_recv()
        start_both(first_copies(n, 1))

    def forward(n, s):
        before = [(right_copy(n, s - 1), left_copy(n, s - 1))] if s > 1 else [first_copies(n, 0), first_copies(n, 1)]
        after = (right_last(n), left_last(n)) if s == 3 else (right_copy(n, s), left_copy(n, s))
        for side in range(2):
            for pair in before:
                pair[side].wait_recv()
            after[side].start()

    def make_g(n):
        col = iota((512, LANES), 1) + n * LANES
        for w in range(WIDE // 512):
            at = slice(w * 512, (w + 1) * 512)
            for side in range(2):
                hit = src_ref[at] == col + 2048 * side
                g_ref[n, at, side * LANES:(side + 1) * LANES] = jnp.where(hit, sgn_ref[at], 0.0).astype(jnp.bfloat16)

    def expand(n):
        right_last(n).wait_recv()
        left_last(n).wait_recv()
        q = bq[n].reshape(DEPTH, LANES).astype(jnp.int32)

        @pl.when(n == 0)
        def _():
            sc_ref[...] = jnp.broadcast_to(jnp.exp2(q[:, 0:1].astype(jnp.float32)), (DEPTH, LANES))

        s = sc_ref[...]
        hi = (q + 128) >> 8
        lo = q - (hi << 8)
        bhl[:, :LANES] = (hi.astype(jnp.float32) * (s * 256.0)).astype(jnp.bfloat16)
        bhl[:, LANES:] = (lo.astype(jnp.float32) * s).astype(jnp.bfloat16)

    def to_core(n, h):
        csend[n, h] = block(yl if h else 1 - yl, 1 - core)
        core_copy(n, h).start()

    def core_sum(n):
        core_copy(n, 0).wait_recv()
        part = ysend[n] + crecv[n, 0]
        biggest = jnp.max(jnp.abs(part), axis=1, keepdims=True)
        ex = jnp.ceil(jnp.log2(jnp.maximum(biggest, 1e-30))) - 15.0
        ex = jnp.broadcast_to(ex, (OUT_ROWS, LANES))
        q = jnp.clip(jnp.floor(part * jnp.exp2(-ex) + 0.5), -32767.0, 32767.0)
        ycode[n, :OUT_ROWS] = q.astype(jnp.int32).astype(jnp.int16)
        turned = jnp.concatenate([ex[:LANES].T[:8], ex[LANES:].T[:8]], axis=0)
        ycode[n, OUT_ROWS:] = turned.astype(jnp.int32).astype(jnp.int16)
        lo_copy(n).start()
        core_copy(n, 1).wait_recv()
        own[n] += crecv[n, 1]

    def finish(n):
        lo_copy(n).wait_recv()
        ex = yrecv[n, OUT_ROWS:].astype(jnp.int32).astype(jnp.float32)
        for k in range(2):
            rows = slice(k * LANES, (k + 1) * LANES)
            scale = jnp.exp2(jnp.broadcast_to(ex[8 * k:8 * k + 1], (LANES, LANES)).T)
            got = yrecv[n, rows].astype(jnp.int32).astype(jnp.float32) * scale
            r_own[n, rows] = (own[n, rows] + got).astype(jnp.bfloat16)
        mirror_copy(n).start()

    def place(n):
        mirror_copy(n).wait_recv()
        both = jnp.concatenate([r_own[n], r_recv[n]], axis=1)
        for w in range(WIDE // 512):
            at = slice(w * 512, (w + 1) * 512)
            acc_ref[at] += lax.dot_general(
                g_ref[n, at], both, (((1,), (1,)), ((), ())), preferred_element_type=jnp.float32
            )

    def first_part(n, _):
        part_start(n)
        return 0

    lax.fori_loop(0, FIRST, first_part, 0)

    def early(n, _):
        forward(n, 1)
        make_g(n)
        return 0

    def middle(n, _):
        forward(n, 2)

        @pl.when(n < LAST)
        def _():
            make_g(n + FIRST)

        return 0

    def late(n, _):
        forward(n, 3)

        @pl.when(n < LAST)
        def _():
            part_start(n + FIRST)

        return 0

    lax.fori_loop(0, FIRST, early, 0)
    lax.fori_loop(0, FIRST, middle, 0)
    lax.fori_loop(0, FIRST, late, 0)

    def event(i):
        n = FIRST + i % LAST
        for s in range(1, 4):

            @pl.when(i // LAST == s - 1)
            def _():
                forward(n, s)

    def body(t, _):
        @pl.when(t < FIRST)
        def _():
            event(2 * t)

        expand(t)
        to_core(t, 0)
        to_core(t, 1)

        @pl.when(t >= 1)
        def _():
            core_sum(t - 1)

        ysend[t] = block(1 - yl, core)
        own[t] = block(yl, core)

        @pl.when(t < FIRST)
        def _():
            event(2 * t + 1)

        @pl.when(t >= 3)
        def _():
            finish(t - 3)

        return 0

    lax.fori_loop(0, CHUNKS, body, 0)

    def place_some(n, _):
        place(n)
        return 0

    def finish_some(n, _):
        finish(n)
        return 0

    lax.fori_loop(0, 3, place_some, 0)
    core_sum(9)
    lax.fori_loop(7, 9, finish_some, 0)
    lax.fori_loop(3, 6, place_some, 0)
    finish(9)
    lax.fori_loop(6, 10, place_some, 0)
    out_ref[...] = acc_ref[: OCC * SUB].astype(jnp.bfloat16)

    w0.wait_send()
    w1.wait_send()

    def drain(n, _):
        hi_copy(n).wait_send()
        for side in range(2):
            for one in first_copies(n, side):
                one.wait_send()
        for s in range(1, 3):
            right_copy(n, s).wait_send()
            left_copy(n, s).wait_send()
        right_last(n).wait_send()
        left_last(n).wait_send()
        core_copy(n, 0).wait_send()
        core_copy(n, 1).wait_send()
        lo_copy(n).wait_send()
        mirror_copy(n).wait_send()
        return 0

    lax.fori_loop(0, CHUNKS, drain, 0)


def local(integrals, amplitudes, ab_irrep, cd_irrep):
    vmem = pl.BlockSpec(memory_space=pltpu.VMEM)
    bf, f32 = jnp.bfloat16, jnp.float32
    dma = pltpu.SemaphoreType.DMA
    n = CHUNKS
    scratch = [
        pltpu.VMEM((ROWS_T, WIDE), bf),
        pltpu.VMEM((1024, DEPTH), bf),
        pltpu.VMEM((1024, DEPTH), bf),
        pltpu.VMEM((DEPTH, DEPTH), bf),
        pltpu.VMEM((HALF, HALF), bf),
        pltpu.VMEM((4, ROWS_T, HALF), bf),
        pltpu.VMEM((2, ROWS_T, HALF), bf),
        pltpu.VMEM((2, ROWS_T, HALF), bf),
        pltpu.VMEM((n, NZ, 2, ROWS_T, LANES), jnp.int16),
        pltpu.VMEM((DEPTH, LANES), f32),
        pltpu.VMEM((DEPTH, 2 * LANES), bf),
        pltpu.VMEM((n, 2, OUT_ROWS, LANES), f32),
        pltpu.VMEM((n, 2, OUT_ROWS, LANES), f32),
        pltpu.VMEM((n, OUT_ROWS, LANES), f32),
        pltpu.VMEM((n, OUT_ROWS + 16, LANES), jnp.int16),
        pltpu.VMEM((n, OUT_ROWS + 16, LANES), jnp.int16),
        pltpu.VMEM((n, OUT_ROWS, LANES), f32),
        pltpu.VMEM((n, OUT_ROWS, LANES), bf),
        pltpu.VMEM((n, OUT_ROWS, LANES), bf),
        pltpu.VMEM((n, WIDE, 2 * LANES), bf),
        pltpu.VMEM((WIDE, LANES), jnp.int32),
        pltpu.VMEM((WIDE, LANES), f32),
        pltpu.VMEM((WIDE, OUT_ROWS), f32),
        dma,
        dma((2,)), dma((2,)),
        dma((n,)), dma((n,)),
        dma((n, 5)), dma((n, 5)),
        dma((n, 5)), dma((n, 5)),
        dma((n, 2)), dma((n, 2)),
        dma((n,)), dma((n,)),
        dma((n,)), dma((n,)),
    ]
    turned = pl.pallas_call(
        kernel,
        out_shape=jax.ShapeDtypeStruct((OCC * SUB, OUT_ROWS), bf),
        in_specs=[vmem, vmem, vmem, pl.BlockSpec(memory_space=pl.ANY)],
        out_specs=vmem,
        scratch_shapes=scratch,
        compiler_params=pltpu.CompilerParams(
            collective_id=0, has_side_effects=True, vmem_limit_bytes=58 * 2**20
        ),
        name="ladder",
    )(amplitudes, ab_irrep, cd_irrep, integrals)
    return turned.T


def solution(mesh):
    in_specs = (P("row", "depth"), P("depth", "row", "col"), P("row"), P("depth"))
    out_specs = P(("row", "depth"), "col")
    return jax.shard_map(local, mesh=mesh, in_specs=in_specs, out_specs=out_specs, check_vma=False)
```

```python
import numpy as np

import jax
import jax.numpy as jnp
from jax import lax
from jax.experimental import pallas as pl
from jax.experimental.pallas import tpu as pltpu
from jax.sharding import PartitionSpec as P

OCC = 100
SUB = 25
NZ = 8
LANES = 128
CHUNKS = 10
HALF = 640
PAD = 15
FIRST = 6
LAST = CHUNKS - FIRST
THIN = 3
FULL = FIRST - THIN
CUT = 48
ROWS_T = 80
DEPTH = 1280
OUT_ROWS = 256
WIDE = 2560
MESH = pl.DeviceIdType.MESH


def iota(shape, dim):
    return lax.broadcasted_iota(jnp.int32, shape, dim)


def div25(v):
    return (v * 5243) >> 17


def div100(v):
    return (v * 5243) >> 19


def one_hot(cond):
    return jnp.where(cond, 1.0, 0.0).astype(jnp.bfloat16)


def dot(a, b):
    return jnp.dot(a, b, preferred_element_type=jnp.float32)


def band(n):
    lanes = np.arange(n * LANES, (n + 1) * LANES) - PAD
    lanes = lanes[(lanes >= 0) & (lanes < SUB * SUB)]
    first = 100 * (lanes // SUB) + lanes % SUB
    low = first.min() // LANES * LANES
    high = -(-(first.max() + 76) // LANES) * LANES
    return int(low), int(min(high, WIDE))


def kernel(
    amp_ref, ab_ref, cd_ref, v_hbm, out_ref,
    t_ref, v_ref, vp_ref, pk_ref, pt_ref, x_ref, wsend, wrecv, bq, sc_ref, bhl,
    csend, crecv, ysend, ycode, yrecv, own, r_own, r_recv, g_ref, src_ref, sgn_ref, acc_ref,
    v_sem, w_ss, w_rs, h_ss, h_rs, t_ss, t_rs, zr_ss, zr_rs, zl_ss, zl_rs, c_ss, c_rs, y_ss, y_rs, m_ss, m_rs,
):
    row, c, depth = lax.axis_index("row"), lax.axis_index("col"), lax.axis_index("depth")
    z, yh = row // 2, row % 2
    yl, core = depth // 2, depth % 2
    d_right = ((row + 2) % 16, c, depth)
    d_left = ((row + 14) % 16, c, depth)
    d_hi = (2 * z + 1 - yh, c, depth)
    d_core = (row, c, 2 * yl + 1 - core)
    d_lo = (row, c, 2 * (1 - yl) + core)
    x_next = (row, (c + 1) % 4, depth)
    x_opp = (row, (c + 2) % 4, depth)
    x_prev = (row, (c + 3) % 4, depth)

    def copy(src, dst, ss, rs, dev):
        return pltpu.make_async_remote_copy(
            src_ref=src, dst_ref=dst, send_sem=ss, recv_sem=rs, device_id=dev, device_id_type=MESH
        )

    v_copy = pltpu.make_async_copy(v_hbm, v_ref, v_sem)
    v_copy.start()

    barrier = pltpu.get_barrier_semaphore()
    for dev in (d_right, d_left, d_hi, d_core, d_lo, x_next, x_opp, x_prev):
        pl.semaphore_signal(barrier, inc=1, device_id=dev, device_id_type=MESH)

    t_ref[:, 2432:] = jnp.zeros((ROWS_T, LANES), jnp.bfloat16)
    t_ref[:, : OCC * SUB] = amp_ref[...].reshape(ROWS_T, OCC * SUB)

    u = iota((1, HALF), 1) - PAD
    a = div25(u)
    b = u - SUB * a
    flip = jnp.where(u >= 0, PAD + SUB * b + a, -1)
    lower = b <= a
    pt_ref[...] = one_hot(iota((HALF, HALF), 0) == flip)

    for n in range(HALF // LANES):
        low, high = band(n)
        u = iota((1, LANES), 1) + (n * LANES - PAD)
        a = div25(u)
        first = 100 * a + (u - SUB * a)
        r = iota((high - low, LANES), 0) + low
        mats = []
        for g in range(4):
            want = jnp.where((u >= 0), first + SUB * ((c + g) % 4), -1)
            mats.append(one_hot(r == want))
        got = dot(t_ref[:, low:high], jnp.concatenate(mats, axis=1)).astype(jnp.bfloat16)
        for g in range(4):
            x_ref[g, :, n * LANES:(n + 1) * LANES] = got[:, g * LANES:(g + 1) * LANES]

    wsend[0] = dot(x_ref[3], pt_ref[...]).astype(jnp.bfloat16)
    wsend[1] = dot(x_ref[2], pt_ref[...]).astype(jnp.bfloat16)
    pl.semaphore_wait(barrier, 8)
    w0 = copy(wsend.at[0], wrecv.at[0], w_ss.at[0], w_rs.at[0], x_prev)
    w1 = copy(wsend.at[1], wrecv.at[1], w_ss.at[1], w_rs.at[1], x_opp)
    w1.start()
    w0.start()
    x0 = x_ref[0]
    diag = x0.astype(jnp.float32) - dot(x0, pt_ref[...])

    k = iota((1, DEPTH), 1)
    zz = (k * 3277) >> 19
    rem = k - 160 * zz
    hh = jnp.where(rem >= 80, 1, 0)
    m = rem - 80 * hh
    from_k = 32 * (m >> 1) + 4 * zz + 2 * hh + (m & 1)

    def make_pk(i, _):
        base = pl.multiple_of(i * 256, 256)
        pk_ref[pl.ds(base, 256), :] = one_hot(iota((256, DEPTH), 0) + base == from_k)
        return 0

    lax.fori_loop(0, DEPTH // 256, make_pk, 0)
    v_copy.wait()

    def make_vp(i, _):
        base = pl.multiple_of(i * 128, 128)
        rows = pl.ds(base, 128)
        label = jnp.broadcast_to(ab_ref[rows].reshape(1, 128), (128, 128)).T
        keep = jnp.concatenate([label] * 10, axis=1) == cd_ref[...].reshape(1, DEPTH)
        masked = jnp.where(keep, v_ref[rows, :].astype(jnp.float32), 0.0).astype(jnp.bfloat16)
        vp_ref[rows, :] = dot(masked, pk_ref[...]).astype(jnp.bfloat16)
        return 0

    lax.fori_loop(0, 4, make_vp, 0)

    w0.wait_recv()
    w1.wait_recv()
    ta1 = x_ref[1].astype(jnp.float32) - wrecv[0].astype(jnp.float32)
    ta2 = jnp.where(lower, x_ref[2].astype(jnp.float32) - wrecv[1].astype(jnp.float32), diag)
    biggest = jnp.maximum(
        jnp.max(jnp.abs(ta1), axis=1, keepdims=True), jnp.max(jnp.abs(ta2), axis=1, keepdims=True)
    )
    exponent = jnp.ceil(jnp.log2(jnp.maximum(biggest, 1e-30))) - 15.0
    scale = jnp.exp2(-exponent)

    def coded(v):
        return jnp.clip(jnp.floor(v * scale + 0.5), -32767.0, 32767.0)

    q2 = coded(ta2)
    q1 = coded(ta1)
    q2 = jnp.where(iota((ROWS_T, HALF), 1) < PAD, jnp.broadcast_to(exponent, (ROWS_T, HALF)), q2)
    for n in range(CHUNKS):
        q = q2 if n < 5 else q1
        part = q[:, (n % 5) * LANES:(n % 5 + 1) * LANES]
        bq[n, z, yh] = part.astype(jnp.int32).astype(jnp.int16)

    def hi_copy(n):
        return copy(bq.at[n, z, yh], bq.at[n, z, yh], h_ss.at[n], h_rs.at[n], d_hi)

    def first_copies(n, side):
        at = yh if side == 0 else 1 - yh
        ref = bq.at[n, z, at]
        sem = 4 * side
        return (
            copy(ref, ref, zr_ss.at[n, sem], zr_rs.at[n, sem], d_right),
            copy(ref, ref, zl_ss.at[n, sem], zl_rs.at[n, sem], d_left),
        )

    def right_copy(n, s):
        at = (z - s + NZ) % NZ
        return copy(bq.at[n, at], bq.at[n, at], zr_ss.at[n, s], zr_rs.at[n, s], d_right)

    def left_copy(n, s):
        at = (z + s) % NZ
        return copy(bq.at[n, at], bq.at[n, at], zl_ss.at[n, s], zl_rs.at[n, s], d_left)

    def thin_copies(n, s):
        near, far = (z - s + NZ) % NZ, (z + s) % NZ
        right, left = bq.at[n, near, yh], bq.at[n, far, yh]
        if s == 3:
            right, left = right.at[pl.ds(0, CUT)], left.at[pl.ds(CUT, ROWS_T - CUT)]
        return (
            copy(right, right, zr_ss.at[n, s], zr_rs.at[n, s], d_right),
            copy(left, left, zl_ss.at[n, s], zl_rs.at[n, s], d_left),
        )

    def slot_copies(n, s):
        near, far = bq.at[n, (z - s + NZ) % NZ, yh], bq.at[n, (z + s) % NZ, yh]
        first = copy(near, near, t_ss.at[n - FULL, s - 1], t_rs.at[n - FULL, s - 1], d_hi)
        if s == 4:
            return (first,)
        return first, copy(far, far, t_ss.at[n - FULL, s + 3], t_rs.at[n - FULL, s + 3], d_hi)

    def right_last(n):
        at = (z - 3 + NZ) % NZ
        return copy(bq.at[n, at, 0], bq.at[n, at, 0], zr_ss.at[n, 3], zr_rs.at[n, 3], d_right)

    def left_last(n):
        at = (z + 3) % NZ
        return copy(bq.at[n, at, 1], bq.at[n, at, 1], zl_ss.at[n, 3], zl_rs.at[n, 3], d_left)

    def core_copy(n, h):
        return copy(csend.at[n, h], crecv.at[n, h], c_ss.at[n, h], c_rs.at[n, h], d_core)

    def lo_copy(n):
        return copy(ycode.at[n], yrecv.at[n], y_ss.at[n], y_rs.at[n], d_lo)

    def mirror_copy(n):
        to = (row, (c + 2 - n // 5) % 4, depth)
        return copy(r_own.at[n], r_recv.at[n], m_ss.at[n], m_rs.at[n], to)

    def start_both(pair):
        for one in pair:
            one.start()

    def own_start(n, _):
        hi_copy(n).start()
        start_both(first_copies(n, 0))
        return 0

    lax.fori_loop(0, CHUNKS, own_start, 0)
    lax.fori_loop(4, 8, make_vp, 0)

    lane = iota((WIDE, LANES), 0)
    a = div100(lane)
    j = lane - OCC * a
    grp = div25(j)
    b = j - SUB * grp
    rel = (grp - c + 4) % 4
    direct = PAD + SUB * a + b
    turned = PAD + SUB * b + a
    src = jnp.where(
        rel == 0,
        jnp.where(b > a, direct, jnp.where(b < a, turned, -1)),
        jnp.where(
            rel == 1,
            HALF + direct,
            jnp.where(rel == 2, jnp.where(b <= a, direct, 2048 + turned), 2048 + HALF + turned),
        ),
    )
    src_ref[...] = jnp.where(lane < OCC * SUB, src, -1)
    minus = ((rel == 0) & (b < a)) | ((rel == 2) & (b > a)) | (rel == 3)
    sgn_ref[...] = jnp.where(minus, -1.0, 1.0)
    acc_ref[...] = jnp.zeros_like(acc_ref)

    def block(yl_at, core_at):
        at = pl.multiple_of((2 * yl_at + core_at) * OUT_ROWS, OUT_ROWS)
        both = dot(vp_ref[pl.ds(at, OUT_ROWS), :], bhl[...])
        return both[:, :LANES] + both[:, LANES:]

    def part_start(n):
        hi_copy(n).wait_recv()
        start_both(first_copies(n, 1))

    def forward(n, s):
        before = [(right_copy(n, s - 1), left_copy(n, s - 1))] if s > 1 else [first_copies(n, 0), first_copies(n, 1)]
        after = (right_last(n), left_last(n)) if s == 3 else (right_copy(n, s), left_copy(n, s))
        for side in range(2):
            for pair in before:
                pair[side].wait_recv()
            after[side].start()

    def forward_thin(n, s):
        before = thin_copies(n, s - 1) if s > 1 else first_copies(n, 0)
        after = thin_copies(n, s)
        for side in range(2):
            before[side].wait_recv()
            after[side].start()
        start_both(slot_copies(n, s))

    def end_thin(n):
        for one in thin_copies(n, 3):
            one.wait_recv()
        start_both(slot_copies(n, 4))

    def make_g(n):
        col = iota((512, LANES), 1) + n * LANES
        for w in range(WIDE // 512):
            at = slice(w * 512, (w + 1) * 512)
            for side in range(2):
                hit = src_ref[at] == col + 2048 * side
                g_ref[n, at, side * LANES:(side + 1) * LANES] = jnp.where(hit, sgn_ref[at], 0.0).astype(jnp.bfloat16)

    def is_thin(n):
        return (n >= FULL) & (n < FIRST)

    def expand(n):
        @pl.when(is_thin(n))
        def _():
            hi_copy(n).wait_recv()
            for s in range(1, 5):
                for one in slot_copies(n, s):
                    one.wait_recv()

        @pl.when(jnp.logical_not(is_thin(n)))
        def _():
            right_last(n).wait_recv()
            left_last(n).wait_recv()

        q = bq[n].reshape(DEPTH, LANES).astype(jnp.int32)

        @pl.when(n == 0)
        def _():
            sc_ref[...] = jnp.broadcast_to(jnp.exp2(q[:, 0:1].astype(jnp.float32)), (DEPTH, LANES))

        s = sc_ref[...]
        hi = (q + 128) >> 8
        lo = q - (hi << 8)
        bhl[:, :LANES] = (hi.astype(jnp.float32) * (s * 256.0)).astype(jnp.bfloat16)
        bhl[:, LANES:] = (lo.astype(jnp.float32) * s).astype(jnp.bfloat16)

    def to_core(n, h):
        csend[n, h] = block(yl if h else 1 - yl, 1 - core)
        core_copy(n, h).start()

    def core_sum(n):
        core_copy(n, 0).wait_recv()
        part = ysend[n] + crecv[n, 0]
        biggest = jnp.max(jnp.abs(part), axis=1, keepdims=True)
        ex = jnp.ceil(jnp.log2(jnp.maximum(biggest, 1e-30))) - 15.0
        ex = jnp.broadcast_to(ex, (OUT_ROWS, LANES))
        q = jnp.clip(jnp.floor(part * jnp.exp2(-ex) + 0.5), -32767.0, 32767.0)
        ycode[n, :OUT_ROWS] = q.astype(jnp.int32).astype(jnp.int16)
        turned = jnp.concatenate([ex[:LANES].T[:8], ex[LANES:].T[:8]], axis=0)
        ycode[n, OUT_ROWS:] = turned.astype(jnp.int32).astype(jnp.int16)
        lo_copy(n).start()
        core_copy(n, 1).wait_recv()
        own[n] += crecv[n, 1]

    def finish(n):
        lo_copy(n).wait_recv()
        ex = yrecv[n, OUT_ROWS:].astype(jnp.int32).astype(jnp.float32)
        for k in range(2):
            rows = slice(k * LANES, (k + 1) * LANES)
            scale = jnp.exp2(jnp.broadcast_to(ex[8 * k:8 * k + 1], (LANES, LANES)).T)
            got = yrecv[n, rows].astype(jnp.int32).astype(jnp.float32) * scale
            r_own[n, rows] = (own[n, rows] + got).astype(jnp.bfloat16)
        mirror_copy(n).start()

    def place(n):
        mirror_copy(n).wait_recv()
        both = jnp.concatenate([r_own[n], r_recv[n]], axis=1)
        for w in range(WIDE // 512):
            at = slice(w * 512, (w + 1) * 512)
            acc_ref[at] += lax.dot_general(
                g_ref[n, at], both, (((1,), (1,)), ((), ())), preferred_element_type=jnp.float32
            )

    def first_part(n, _):
        part_start(n)
        return 0

    lax.fori_loop(0, FULL, first_part, 0)

    def early(n, _):
        forward(n, 1)
        make_g(n)
        return 0

    def early_thin(n, _):
        forward_thin(n, 1)
        make_g(n)
        return 0

    def middle(n, _):
        forward(n, 2)
        make_g(n + FIRST)
        return 0

    def middle_thin(n, _):
        forward_thin(n, 2)
        return 0

    def late(n, _):
        forward(n, 3)
        part_start(n + FIRST)
        return 0

    def late_thin(n, _):
        forward_thin(n, 3)
        return 0

    lax.fori_loop(0, FULL, early, 0)
    lax.fori_loop(FULL, FIRST, early_thin, 0)
    lax.fori_loop(0, FULL, middle, 0)
    lax.fori_loop(FULL, FIRST, middle_thin, 0)
    lax.fori_loop(0, FULL, late, 0)
    lax.fori_loop(FULL, FIRST, late_thin, 0)
    part_start(CHUNKS - 1)
    make_g(CHUNKS - 1)

    def event(i):
        n = FIRST + i % LAST
        for s in range(1, 4):

            @pl.when(i // LAST == s - 1)
            def _():
                forward(n, s)

    def body(t, _):
        @pl.when(t < FIRST)
        def _():
            event(2 * t)

        expand(t)
        to_core(t, 0)
        to_core(t, 1)

        @pl.when(t >= 1)
        def _():
            core_sum(t - 1)

        ysend[t] = block(1 - yl, core)
        own[t] = block(yl, core)

        @pl.when(t < FIRST)
        def _():
            event(2 * t + 1)

        @pl.when(t == 0)
        def _():
            for n in range(FULL, FIRST):
                end_thin(n)

        @pl.when(t >= 3)
        def _():
            finish(t - 3)

        return 0

    lax.fori_loop(0, CHUNKS, body, 0)

    def place_some(n, _):
        place(n)
        return 0

    def finish_some(n, _):
        finish(n)
        return 0

    def drain(n, _):
        hi_copy(n).wait_send()
        for one in first_copies(n, 0):
            one.wait_send()

        @pl.when(is_thin(n))
        def _():
            for s in range(1, 4):
                for one in thin_copies(n, s):
                    one.wait_send()
            for s in range(1, 5):
                for one in slot_copies(n, s):
                    one.wait_send()

        @pl.when(jnp.logical_not(is_thin(n)))
        def _():
            for one in first_copies(n, 1):
                one.wait_send()
            for s in range(1, 3):
                right_copy(n, s).wait_send()
                left_copy(n, s).wait_send()
            right_last(n).wait_send()
            left_last(n).wait_send()

        return 0

    def drain_sums(n, _):
        core_copy(n, 0).wait_send()
        core_copy(n, 1).wait_send()
        lo_copy(n).wait_send()
        return 0

    def drain_mirror(n, _):
        mirror_copy(n).wait_send()
        return 0

    lax.fori_loop(0, 3, place_some, 0)
    core_sum(9)
    lax.fori_loop(7, 9, finish_some, 0)
    lax.fori_loop(0, CHUNKS, drain, 0)
    lax.fori_loop(3, 5, place_some, 0)
    finish(9)
    w0.wait_send()
    w1.wait_send()
    lax.fori_loop(0, CHUNKS, drain_sums, 0)
    lax.fori_loop(5, 10, place_some, 0)
    out_ref[...] = acc_ref[: OCC * SUB].astype(jnp.bfloat16)
    lax.fori_loop(0, CHUNKS, drain_mirror, 0)


def pass_on(src, dst, sem):
    whole = pltpu.make_async_copy(src, dst, sem)
    whole.start()
    whole.wait()


def local(integrals, amplitudes, ab_irrep, cd_irrep):
    vmem = pl.BlockSpec(memory_space=pltpu.VMEM)
    bf, f32 = jnp.bfloat16, jnp.float32
    dma = pltpu.SemaphoreType.DMA
    n = CHUNKS
    scratch = [
        pltpu.VMEM((ROWS_T, WIDE), bf),
        pltpu.VMEM((1024, DEPTH), bf),
        pltpu.VMEM((1024, DEPTH), bf),
        pltpu.VMEM((DEPTH, DEPTH), bf),
        pltpu.VMEM((HALF, HALF), bf),
        pltpu.VMEM((4, ROWS_T, HALF), bf),
        pltpu.VMEM((2, ROWS_T, HALF), bf),
        pltpu.VMEM((2, ROWS_T, HALF), bf),
        pltpu.VMEM((n, NZ, 2, ROWS_T, LANES), jnp.int16),
        pltpu.VMEM((DEPTH, LANES), f32),
        pltpu.VMEM((DEPTH, 2 * LANES), bf),
        pltpu.VMEM((n, 2, OUT_ROWS, LANES), f32),
        pltpu.VMEM((n, 2, OUT_ROWS, LANES), f32),
        pltpu.VMEM((n, OUT_ROWS, LANES), f32),
        pltpu.VMEM((n, OUT_ROWS + 16, LANES), jnp.int16),
        pltpu.VMEM((n, OUT_ROWS + 16, LANES), jnp.int16),
        pltpu.VMEM((n, OUT_ROWS, LANES), f32),
        pltpu.VMEM((n, OUT_ROWS, LANES), bf),
        pltpu.VMEM((n, OUT_ROWS, LANES), bf),
        pltpu.VMEM((n, WIDE, 2 * LANES), bf),
        pltpu.VMEM((WIDE, LANES), jnp.int32),
        pltpu.VMEM((WIDE, LANES), f32),
        pltpu.VMEM((WIDE, OUT_ROWS), f32),
        dma,
        dma((2,)), dma((2,)),
        dma((n,)), dma((n,)),
        dma((THIN, 7)), dma((THIN, 7)),
        dma((n, 5)), dma((n, 5)),
        dma((n, 5)), dma((n, 5)),
        dma((n, 2)), dma((n, 2)),
        dma((n,)), dma((n,)),
        dma((n,)), dma((n,)),
    ]
    turned = pl.pallas_call(
        kernel,
        out_shape=jax.ShapeDtypeStruct((OCC * SUB, OUT_ROWS), bf),
        in_specs=[vmem, vmem, vmem, pl.BlockSpec(memory_space=pl.ANY)],
        out_specs=vmem,
        scratch_shapes=scratch,
        compiler_params=pltpu.CompilerParams(
            collective_id=0, has_side_effects=True, vmem_limit_bytes=58 * 2**20
        ),
        name="ladder",
    )(amplitudes, ab_irrep, cd_irrep, integrals)
    any_space = pl.BlockSpec(memory_space=pl.ANY)
    final = pl.pallas_call(
        pass_on,
        out_shape=jax.ShapeDtypeStruct(turned.shape, turned.dtype),
        in_specs=[any_space],
        out_specs=any_space,
        scratch_shapes=[dma],
        name="pass_on",
    )(turned)
    return final.T


def solution(mesh):
    in_specs = (P("row", "depth"), P("depth", "row", "col"), P("row"), P("depth"))
    out_specs = P(("row", "depth"), "col")
    return jax.shard_map(local, mesh=mesh, in_specs=in_specs, out_specs=out_specs, check_vma=False)
```

```python
import numpy as np

import jax
import jax.numpy as jnp
from jax import lax
from jax.experimental import pallas as pl
from jax.experimental.pallas import tpu as pltpu
from jax.sharding import PartitionSpec as P

OCC = 100
SUB = 25
NZ = 8
LANES = 128
CHUNKS = 10
HALF = 640
PAD = 15
FIRST = 6
LAST = CHUNKS - FIRST
THIN = 3
FULL = FIRST - THIN
CUT = 48
ROWS_T = 80
DEPTH = 1280
OUT_ROWS = 256
WIDE = 2560
MESH = pl.DeviceIdType.MESH


def iota(shape, dim):
    return lax.broadcasted_iota(jnp.int32, shape, dim)


def div25(v):
    return (v * 5243) >> 17


def one_hot(cond):
    return jnp.where(cond, 1.0, 0.0).astype(jnp.bfloat16)


def dot(a, b):
    return jnp.dot(a, b, preferred_element_type=jnp.float32)


def band(n):
    lanes = np.arange(n * LANES, (n + 1) * LANES) - PAD
    lanes = lanes[(lanes >= 0) & (lanes < SUB * SUB)]
    first = 100 * (lanes // SUB) + lanes % SUB
    low = first.min() // LANES * LANES
    high = -(-(first.max() + 76) // LANES) * LANES
    return int(low), int(min(high, WIDE))


def kernel(
    amp_ref, ab_ref, cd_ref, v_hbm, out_ref,
    t_ref, v_ref, vp_ref, pk_ref, pt_ref, x_ref, wsend, wrecv, bq, sc_ref, bhl,
    csend, crecv, ysend, ycode, yrecv, own, r_own, r_recv, tmp_ref, acc_ref,
    v_sem, w_ss, w_rs, h_ss, h_rs, t_ss, t_rs, zr_ss, zr_rs, zl_ss, zl_rs, c_ss, c_rs, y_ss, y_rs, m_ss, m_rs,
):
    row, c, depth = lax.axis_index("row"), lax.axis_index("col"), lax.axis_index("depth")
    z, yh = row // 2, row % 2
    yl, core = depth // 2, depth % 2
    d_right = ((row + 2) % 16, c, depth)
    d_left = ((row + 14) % 16, c, depth)
    d_hi = (2 * z + 1 - yh, c, depth)
    d_core = (row, c, 2 * yl + 1 - core)
    d_lo = (row, c, 2 * (1 - yl) + core)
    x_next = (row, (c + 1) % 4, depth)
    x_opp = (row, (c + 2) % 4, depth)
    x_prev = (row, (c + 3) % 4, depth)

    def copy(src, dst, ss, rs, dev):
        return pltpu.make_async_remote_copy(
            src_ref=src, dst_ref=dst, send_sem=ss, recv_sem=rs, device_id=dev, device_id_type=MESH
        )

    v_copy = pltpu.make_async_copy(v_hbm, v_ref, v_sem)
    v_copy.start()

    barrier = pltpu.get_barrier_semaphore()
    for dev in (d_right, d_left, d_hi, d_core, d_lo, x_next, x_opp, x_prev):
        pl.semaphore_signal(barrier, inc=1, device_id=dev, device_id_type=MESH)

    t_ref[:, 2432:] = jnp.zeros((ROWS_T, LANES), jnp.bfloat16)
    t_ref[:, : OCC * SUB] = amp_ref[...].reshape(ROWS_T, OCC * SUB)

    u = iota((1, HALF), 1) - PAD
    a = div25(u)
    b = u - SUB * a
    flip = jnp.where(u >= 0, PAD + SUB * b + a, -1)
    lower = b <= a
    pt_ref[...] = one_hot(iota((HALF, HALF), 0) == flip)

    for n in range(HALF // LANES):
        low, high = band(n)
        u = iota((1, LANES), 1) + (n * LANES - PAD)
        a = div25(u)
        first = 100 * a + (u - SUB * a)
        r = iota((high - low, LANES), 0) + low
        mats = []
        for g in range(4):
            want = jnp.where((u >= 0), first + SUB * ((c + g) % 4), -1)
            mats.append(one_hot(r == want))
        got = dot(t_ref[:, low:high], jnp.concatenate(mats, axis=1)).astype(jnp.bfloat16)
        for g in range(4):
            x_ref[g, :, n * LANES:(n + 1) * LANES] = got[:, g * LANES:(g + 1) * LANES]

    wsend[0] = dot(x_ref[3], pt_ref[...]).astype(jnp.bfloat16)
    wsend[1] = dot(x_ref[2], pt_ref[...]).astype(jnp.bfloat16)
    pl.semaphore_wait(barrier, 8)
    w0 = copy(wsend.at[0], wrecv.at[0], w_ss.at[0], w_rs.at[0], x_prev)
    w1 = copy(wsend.at[1], wrecv.at[1], w_ss.at[1], w_rs.at[1], x_opp)
    w1.start()
    w0.start()
    x0 = x_ref[0]
    diag = x0.astype(jnp.float32) - dot(x0, pt_ref[...])

    k = iota((1, DEPTH), 1)
    zz = (k * 3277) >> 19
    rem = k - 160 * zz
    hh = jnp.where(rem >= 80, 1, 0)
    m = rem - 80 * hh
    from_k = 32 * (m >> 1) + 4 * zz + 2 * hh + (m & 1)

    def make_pk(i, _):
        base = pl.multiple_of(i * 256, 256)
        pk_ref[pl.ds(base, 256), :] = one_hot(iota((256, DEPTH), 0) + base == from_k)
        return 0

    lax.fori_loop(0, DEPTH // 256, make_pk, 0)
    v_copy.wait()

    def make_vp(i, _):
        base = pl.multiple_of(i * 128, 128)
        rows = pl.ds(base, 128)
        label = jnp.broadcast_to(ab_ref[rows].reshape(1, 128), (128, 128)).T
        keep = jnp.concatenate([label] * 10, axis=1) == cd_ref[...].reshape(1, DEPTH)
        masked = jnp.where(keep, v_ref[rows, :].astype(jnp.float32), 0.0).astype(jnp.bfloat16)
        vp_ref[rows, :] = dot(masked, pk_ref[...]).astype(jnp.bfloat16)
        return 0

    lax.fori_loop(0, 4, make_vp, 0)

    w0.wait_recv()
    w1.wait_recv()
    ta1 = x_ref[1].astype(jnp.float32) - wrecv[0].astype(jnp.float32)
    ta2 = jnp.where(lower, x_ref[2].astype(jnp.float32) - wrecv[1].astype(jnp.float32), diag)
    biggest = jnp.maximum(
        jnp.max(jnp.abs(ta1), axis=1, keepdims=True), jnp.max(jnp.abs(ta2), axis=1, keepdims=True)
    )
    exponent = jnp.ceil(jnp.log2(jnp.maximum(biggest, 1e-30))) - 15.0
    scale = jnp.exp2(-exponent)

    def coded(v):
        return jnp.clip(jnp.floor(v * scale + 0.5), -32767.0, 32767.0)

    q2 = coded(ta2)
    q1 = coded(ta1)
    q2 = jnp.where(iota((ROWS_T, HALF), 1) < PAD, jnp.broadcast_to(exponent, (ROWS_T, HALF)), q2)
    for n in range(CHUNKS):
        q = q2 if n < 5 else q1
        part = q[:, (n % 5) * LANES:(n % 5 + 1) * LANES]
        bq[n, z, yh] = part.astype(jnp.int32).astype(jnp.int16)

    def hi_copy(n):
        return copy(bq.at[n, z, yh], bq.at[n, z, yh], h_ss.at[n], h_rs.at[n], d_hi)

    def first_copies(n, side):
        at = yh if side == 0 else 1 - yh
        ref = bq.at[n, z, at]
        sem = 4 * side
        return (
            copy(ref, ref, zr_ss.at[n, sem], zr_rs.at[n, sem], d_right),
            copy(ref, ref, zl_ss.at[n, sem], zl_rs.at[n, sem], d_left),
        )

    def right_copy(n, s):
        at = (z - s + NZ) % NZ
        return copy(bq.at[n, at], bq.at[n, at], zr_ss.at[n, s], zr_rs.at[n, s], d_right)

    def left_copy(n, s):
        at = (z + s) % NZ
        return copy(bq.at[n, at], bq.at[n, at], zl_ss.at[n, s], zl_rs.at[n, s], d_left)

    def thin_copies(n, s):
        near, far = (z - s + NZ) % NZ, (z + s) % NZ
        right, left = bq.at[n, near, yh], bq.at[n, far, yh]
        if s == 3:
            right, left = right.at[pl.ds(0, CUT)], left.at[pl.ds(CUT, ROWS_T - CUT)]
        return (
            copy(right, right, zr_ss.at[n, s], zr_rs.at[n, s], d_right),
            copy(left, left, zl_ss.at[n, s], zl_rs.at[n, s], d_left),
        )

    def slot_copies(n, s):
        near, far = bq.at[n, (z - s + NZ) % NZ, yh], bq.at[n, (z + s) % NZ, yh]
        first = copy(near, near, t_ss.at[n - FULL, s - 1], t_rs.at[n - FULL, s - 1], d_hi)
        if s == 4:
            return (first,)
        return first, copy(far, far, t_ss.at[n - FULL, s + 3], t_rs.at[n - FULL, s + 3], d_hi)

    def right_last(n):
        at = (z - 3 + NZ) % NZ
        return copy(bq.at[n, at, 0], bq.at[n, at, 0], zr_ss.at[n, 3], zr_rs.at[n, 3], d_right)

    def left_last(n):
        at = (z + 3) % NZ
        return copy(bq.at[n, at, 1], bq.at[n, at, 1], zl_ss.at[n, 3], zl_rs.at[n, 3], d_left)

    def core_copy(n, h):
        return copy(csend.at[n, h], crecv.at[n, h], c_ss.at[n, h], c_rs.at[n, h], d_core)

    def lo_copy(n):
        return copy(ycode.at[n], yrecv.at[n], y_ss.at[n], y_rs.at[n], d_lo)

    def mirror_copy(n):
        to = (row, (c + 2 - n // 5) % 4, depth)
        return copy(r_own.at[n], r_recv.at[n], m_ss.at[n], m_rs.at[n], to)

    def start_both(pair):
        for one in pair:
            one.start()

    def own_start(n, _):
        hi_copy(n).start()
        start_both(first_copies(n, 0))
        return 0

    lax.fori_loop(0, CHUNKS, own_start, 0)
    lax.fori_loop(4, 8, make_vp, 0)

    def block(yl_at, core_at):
        at = pl.multiple_of((2 * yl_at + core_at) * OUT_ROWS, OUT_ROWS)
        both = dot(vp_ref[pl.ds(at, OUT_ROWS), :], bhl[...])
        return both[:, :LANES] + both[:, LANES:]

    def part_start(n):
        hi_copy(n).wait_recv()
        start_both(first_copies(n, 1))

    def forward(n, s):
        before = [(right_copy(n, s - 1), left_copy(n, s - 1))] if s > 1 else [first_copies(n, 0), first_copies(n, 1)]
        after = (right_last(n), left_last(n)) if s == 3 else (right_copy(n, s), left_copy(n, s))
        for side in range(2):
            for pair in before:
                pair[side].wait_recv()
            after[side].start()

    def forward_thin(n, s):
        before = thin_copies(n, s - 1) if s > 1 else first_copies(n, 0)
        after = thin_copies(n, s)
        for side in range(2):
            before[side].wait_recv()
            after[side].start()
        start_both(slot_copies(n, s))

    def end_thin(n):
        for one in thin_copies(n, 3):
            one.wait_recv()
        start_both(slot_copies(n, 4))

    def is_thin(n):
        return (n >= FULL) & (n < FIRST)

    def arrive(n):
        @pl.when(is_thin(n))
        def _():
            hi_copy(n).wait_recv()
            for s in range(1, 5):
                for one in slot_copies(n, s):
                    one.wait_recv()

        @pl.when(jnp.logical_not(is_thin(n)))
        def _():
            right_last(n).wait_recv()
            left_last(n).wait_recv()

    def expand(n):
        q = bq[n].reshape(DEPTH, LANES).astype(jnp.int32)

        @pl.when(n == 0)
        def _():
            sc_ref[...] = jnp.broadcast_to(jnp.exp2(q[:, 0:1].astype(jnp.float32)), (DEPTH, LANES))

        s = sc_ref[...]
        hi = (q + 128) >> 8
        lo = q - (hi << 8)
        bhl[:, :LANES] = (hi.astype(jnp.float32) * (s * 256.0)).astype(jnp.bfloat16)
        bhl[:, LANES:] = (lo.astype(jnp.float32) * s).astype(jnp.bfloat16)

    def to_core(n, h):
        csend[n, h] = block(yl if h else 1 - yl, 1 - core)
        core_copy(n, h).start()

    def core_sum(n):
        core_copy(n, 0).wait_recv()
        part = ysend[n] + crecv[n, 0]
        biggest = jnp.max(jnp.abs(part), axis=1, keepdims=True)
        ex = jnp.ceil(jnp.log2(jnp.maximum(biggest, 1e-30))) - 15.0
        ex = jnp.broadcast_to(ex, (OUT_ROWS, LANES))
        q = jnp.clip(jnp.floor(part * jnp.exp2(-ex) + 0.5), -32767.0, 32767.0)
        ycode[n, :OUT_ROWS] = q.astype(jnp.int32).astype(jnp.int16)
        turned = jnp.concatenate([ex[:LANES].T[:8], ex[LANES:].T[:8]], axis=0)
        ycode[n, OUT_ROWS:] = turned.astype(jnp.int32).astype(jnp.int16)
        lo_copy(n).start()
        core_copy(n, 1).wait_recv()
        own[n] += crecv[n, 1]

    def finish(n):
        lo_copy(n).wait_recv()
        ex = yrecv[n, OUT_ROWS:].astype(jnp.int32).astype(jnp.float32)
        for k in range(2):
            rows = slice(k * LANES, (k + 1) * LANES)
            scale = jnp.exp2(jnp.broadcast_to(ex[8 * k:8 * k + 1], (LANES, LANES)).T)
            got = yrecv[n, rows].astype(jnp.int32).astype(jnp.float32) * scale
            r_own[n, :, rows] = (own[n, rows] + got).T.astype(jnp.bfloat16)
        mirror_copy(n).start()

    def place(block_ref, group):
        for q in range(4):

            @pl.when((c + group) % 4 == q)
            def _():
                for a in range(SUB):
                    at, to = PAD + SUB * a, OCC * a + SUB * q
                    acc_ref[to:to + SUB, :] = block_ref[at:at + SUB, :]

    def mirror_wait(n, _):
        mirror_copy(n).wait_recv()
        return 0

    def place_opposite():
        rows = iota((HALF, 1), 0) - PAD
        ia = div25(rows)
        ib = rows - SUB * ia
        mine = r_own[0:5].reshape(HALF, OUT_ROWS)
        direct = mine.astype(jnp.float32)
        turned = dot(pt_ref[...], mine)
        tmp_ref[...] = jnp.where(ib > ia, direct, jnp.where(ib < ia, -turned, 0.0))
        place(tmp_ref, 0)
        tmp_ref[...] = jnp.where(ib <= ia, direct, -dot(pt_ref[...], r_recv[0:5].reshape(HALF, OUT_ROWS)))
        place(tmp_ref, 2)

    def place_next():
        tmp_ref[...] = r_own[5:10].reshape(HALF, OUT_ROWS).astype(jnp.float32)
        place(tmp_ref, 1)

    def place_previous():
        tmp_ref[...] = -dot(pt_ref[...], r_recv[5:10].reshape(HALF, OUT_ROWS))
        place(tmp_ref, 3)

    def first_part(n, _):
        part_start(n)
        return 0

    lax.fori_loop(0, FULL, first_part, 0)

    def early(n, _):
        forward(n, 1)
        return 0

    def early_thin(n, _):
        forward_thin(n, 1)
        return 0

    def middle(n, _):
        forward(n, 2)
        return 0

    def middle_thin(n, _):
        forward_thin(n, 2)
        return 0

    def late(n, _):
        forward(n, 3)
        part_start(n + FIRST)
        return 0

    def late_thin(n, _):
        forward_thin(n, 3)
        return 0

    lax.fori_loop(0, FULL, early, 0)
    lax.fori_loop(FULL, FIRST, early_thin, 0)
    lax.fori_loop(0, FULL, middle, 0)
    lax.fori_loop(FULL, FIRST, middle_thin, 0)
    lax.fori_loop(0, FULL, late, 0)
    lax.fori_loop(FULL, FIRST, late_thin, 0)
    part_start(CHUNKS - 1)

    def event(i):
        n = FIRST + i % LAST
        for s in range(1, 4):

            @pl.when(i // LAST == s - 1)
            def _():
                forward(n, s)

    def body(t, _):
        @pl.when(t < FIRST)
        def _():
            event(2 * t)

        arrive(t)
        expand(t)
        to_core(t, 0)
        to_core(t, 1)

        @pl.when(t >= 1)
        def _():
            core_sum(t - 1)

        ysend[t] = block(1 - yl, core)
        own[t] = block(yl, core)

        @pl.when(t < FIRST)
        def _():
            event(2 * t + 1)

        @pl.when(t == 0)
        def _():
            for n in range(FULL, FIRST):
                end_thin(n)

        @pl.when(t >= 3)
        def _():
            finish(t - 3)

        return 0

    lax.fori_loop(0, CHUNKS, body, 0)

    def finish_some(n, _):
        finish(n)
        return 0

    def drain(n, _):
        hi_copy(n).wait_send()
        for one in first_copies(n, 0):
            one.wait_send()

        @pl.when(is_thin(n))
        def _():
            for s in range(1, 4):
                for one in thin_copies(n, s):
                    one.wait_send()
            for s in range(1, 5):
                for one in slot_copies(n, s):
                    one.wait_send()

        @pl.when(jnp.logical_not(is_thin(n)))
        def _():
            for one in first_copies(n, 1):
                one.wait_send()
            for s in range(1, 3):
                right_copy(n, s).wait_send()
                left_copy(n, s).wait_send()
            right_last(n).wait_send()
            left_last(n).wait_send()

        return 0

    def drain_sums(n, _):
        core_copy(n, 0).wait_send()
        core_copy(n, 1).wait_send()
        lo_copy(n).wait_send()
        return 0

    def drain_mirror(n, _):
        mirror_copy(n).wait_send()
        return 0

    core_sum(9)
    lax.fori_loop(7, 9, finish_some, 0)
    lax.fori_loop(0, CHUNKS, drain, 0)
    lax.fori_loop(0, 5, mirror_wait, 0)
    place_opposite()
    finish(9)
    w0.wait_send()
    w1.wait_send()
    lax.fori_loop(0, CHUNKS, drain_sums, 0)
    place_next()
    lax.fori_loop(5, CHUNKS, mirror_wait, 0)
    place_previous()
    out_ref[...] = acc_ref[...].astype(jnp.bfloat16)
    lax.fori_loop(0, CHUNKS, drain_mirror, 0)


def pass_on(src, dst):
    dst[...] = src[...]


def local(integrals, amplitudes, ab_irrep, cd_irrep):
    vmem = pl.BlockSpec(memory_space=pltpu.VMEM)
    bf, f32 = jnp.bfloat16, jnp.float32
    dma = pltpu.SemaphoreType.DMA
    n = CHUNKS
    scratch = [
        pltpu.VMEM((ROWS_T, WIDE), bf),
        pltpu.VMEM((1024, DEPTH), bf),
        pltpu.VMEM((1024, DEPTH), bf),
        pltpu.VMEM((DEPTH, DEPTH), bf),
        pltpu.VMEM((HALF, HALF), bf),
        pltpu.VMEM((4, ROWS_T, HALF), bf),
        pltpu.VMEM((2, ROWS_T, HALF), bf),
        pltpu.VMEM((2, ROWS_T, HALF), bf),
        pltpu.VMEM((n, NZ, 2, ROWS_T, LANES), jnp.int16),
        pltpu.VMEM((DEPTH, LANES), f32),
        pltpu.VMEM((DEPTH, 2 * LANES), bf),
        pltpu.VMEM((n, 2, OUT_ROWS, LANES), f32),
        pltpu.VMEM((n, 2, OUT_ROWS, LANES), f32),
        pltpu.VMEM((n, OUT_ROWS, LANES), f32),
        pltpu.VMEM((n, OUT_ROWS + 16, LANES), jnp.int16),
        pltpu.VMEM((n, OUT_ROWS + 16, LANES), jnp.int16),
        pltpu.VMEM((n, OUT_ROWS, LANES), f32),
        pltpu.VMEM((n, LANES, OUT_ROWS), bf),
        pltpu.VMEM((n, LANES, OUT_ROWS), bf),
        pltpu.VMEM((HALF, OUT_ROWS), f32),
        pltpu.VMEM((OCC * SUB, OUT_ROWS), f32),
        dma,
        dma((2,)), dma((2,)),
        dma((n,)), dma((n,)),
        dma((THIN, 7)), dma((THIN, 7)),
        dma((n, 5)), dma((n, 5)),
        dma((n, 5)), dma((n, 5)),
        dma((n, 2)), dma((n, 2)),
        dma((n,)), dma((n,)),
        dma((n,)), dma((n,)),
    ]
    turned = pl.pallas_call(
        kernel,
        out_shape=jax.ShapeDtypeStruct((OCC * SUB, OUT_ROWS), bf),
        in_specs=[vmem, vmem, vmem, pl.BlockSpec(memory_space=pl.ANY)],
        out_specs=vmem,
        scratch_shapes=scratch,
        compiler_params=pltpu.CompilerParams(
            collective_id=0, has_side_effects=True, vmem_limit_bytes=58 * 2**20
        ),
        name="ladder",
    )(amplitudes, ab_irrep, cd_irrep, integrals)
    final = pl.pallas_call(
        pass_on,
        out_shape=jax.ShapeDtypeStruct(turned.shape, turned.dtype),
        in_specs=[vmem],
        out_specs=vmem,
        name="pass_on",
    )(turned)
    return final.T


def solution(mesh):
    in_specs = (P("row", "depth"), P("depth", "row", "col"), P("row"), P("depth"))
    out_specs = P(("row", "depth"), "col")
    return jax.shard_map(local, mesh=mesh, in_specs=in_specs, out_specs=out_specs, check_vma=False)
```

```python
import numpy as np

import jax
import jax.numpy as jnp
from jax import lax
from jax.experimental import pallas as pl
from jax.experimental.pallas import tpu as pltpu
from jax.sharding import PartitionSpec as P

OCC = 100
SUB = 25
NZ = 8
LANES = 128
CHUNKS = 10
HALF = 640
PAD = 15
FIRST = 6
LAST = CHUNKS - FIRST
THIN = 3
FULL = FIRST - THIN
CUT = 48
ROWS_T = 80
DEPTH = 1280
OUT_ROWS = 256
WIDE = 2560
MESH = pl.DeviceIdType.MESH


def iota(shape, dim):
    return lax.broadcasted_iota(jnp.int32, shape, dim)


def div25(v):
    return (v * 5243) >> 17


def one_hot(cond):
    return jnp.where(cond, 1.0, 0.0).astype(jnp.bfloat16)


def dot(a, b):
    return jnp.dot(a, b, preferred_element_type=jnp.float32)


def band(n):
    lanes = np.arange(n * LANES, (n + 1) * LANES) - PAD
    lanes = lanes[(lanes >= 0) & (lanes < SUB * SUB)]
    first = 100 * (lanes // SUB) + lanes % SUB
    low = first.min() // LANES * LANES
    high = -(-(first.max() + 76) // LANES) * LANES
    return int(low), int(min(high, WIDE))


def kernel(
    amp_ref, ab_ref, cd_ref, v_hbm, out_ref,
    t_ref, v_ref, vp_ref, pk_ref, pt_ref, x_ref, diag_ref, wsend, wrecv, bq, sc_ref, bhl,
    csend, crecv, ysend, ycode, yrecv, own, r_own, r_recv, tmp_ref, acc_ref,
    v_sem, w_ss, w_rs, h_ss, h_rs, t_ss, t_rs, zr_ss, zr_rs, zl_ss, zl_rs, c_ss, c_rs, y_ss, y_rs, m_ss, m_rs,
):
    row, c, depth = lax.axis_index("row"), lax.axis_index("col"), lax.axis_index("depth")
    z, yh = row // 2, row % 2
    yl, core = depth // 2, depth % 2
    d_right = ((row + 2) % 16, c, depth)
    d_left = ((row + 14) % 16, c, depth)
    d_hi = (2 * z + 1 - yh, c, depth)
    d_core = (row, c, 2 * yl + 1 - core)
    d_lo = (row, c, 2 * (1 - yl) + core)
    x_next = (row, (c + 1) % 4, depth)
    x_opp = (row, (c + 2) % 4, depth)
    x_prev = (row, (c + 3) % 4, depth)

    def copy(src, dst, ss, rs, dev):
        return pltpu.make_async_remote_copy(
            src_ref=src, dst_ref=dst, send_sem=ss, recv_sem=rs, device_id=dev, device_id_type=MESH
        )

    v_copy = pltpu.make_async_copy(v_hbm, v_ref, v_sem)
    v_copy.start()

    barrier = pltpu.get_barrier_semaphore()
    for dev in (d_right, d_left, d_hi, d_core, d_lo, x_next, x_opp, x_prev):
        pl.semaphore_signal(barrier, inc=1, device_id=dev, device_id_type=MESH)

    t_ref[:, 2432:] = jnp.zeros((ROWS_T, LANES), jnp.bfloat16)
    t_ref[:, : OCC * SUB] = amp_ref[...].reshape(ROWS_T, OCC * SUB)

    u = iota((1, HALF), 1) - PAD
    a = div25(u)
    b = u - SUB * a
    flip = jnp.where(u >= 0, PAD + SUB * b + a, -1)
    lower = b <= a
    pt_ref[...] = one_hot(iota((HALF, HALF), 0) == flip)

    for n in range(HALF // LANES):
        low, high = band(n)
        u = iota((1, LANES), 1) + (n * LANES - PAD)
        a = div25(u)
        first = 100 * a + (u - SUB * a)
        r = iota((high - low, LANES), 0) + low
        mats = []
        for g in range(4):
            want = jnp.where((u >= 0), first + SUB * ((c + g) % 4), -1)
            mats.append(one_hot(r == want))
        got = dot(t_ref[:, low:high], jnp.concatenate(mats, axis=1)).astype(jnp.bfloat16)
        for g in range(4):
            x_ref[g, :, n * LANES:(n + 1) * LANES] = got[:, g * LANES:(g + 1) * LANES]

    wsend[1] = dot(x_ref[2], pt_ref[...]).astype(jnp.bfloat16)
    pl.semaphore_wait(barrier, 8)
    w0 = copy(wsend.at[0], wrecv.at[0], w_ss.at[0], w_rs.at[0], x_prev)
    w1 = copy(wsend.at[1], wrecv.at[1], w_ss.at[1], w_rs.at[1], x_opp)
    w1.start()
    wsend[0] = dot(x_ref[3], pt_ref[...]).astype(jnp.bfloat16)
    x0 = x_ref[0]
    diag_ref[...] = x0.astype(jnp.float32) - dot(x0, pt_ref[...])

    k = iota((1, DEPTH), 1)
    zz = (k * 3277) >> 19
    rem = k - 160 * zz
    hh = jnp.where(rem >= 80, 1, 0)
    m = rem - 80 * hh
    from_k = 32 * (m >> 1) + 4 * zz + 2 * hh + (m & 1)

    def make_pk(i, _):
        base = pl.multiple_of(i * 256, 256)
        pk_ref[pl.ds(base, 256), :] = one_hot(iota((256, DEPTH), 0) + base == from_k)
        return 0

    lax.fori_loop(0, DEPTH // 256, make_pk, 0)
    w1.wait_send()
    w0.start()
    v_copy.wait()

    def make_vp(i, _):
        to = 512 * jnp.where(i // 2 % 2 == core, 1, 0) + 256 * jnp.where(i // 4 == yl, 1, 0) + 128 * (i % 2)
        base = pl.multiple_of(i * 128, 128)
        rows = pl.ds(base, 128)
        label = jnp.broadcast_to(ab_ref[rows].reshape(1, 128), (128, 128)).T
        keep = jnp.concatenate([label] * 10, axis=1) == cd_ref[...].reshape(1, DEPTH)
        masked = jnp.where(keep, v_ref[rows, :].astype(jnp.float32), 0.0).astype(jnp.bfloat16)
        vp_ref[pl.ds(pl.multiple_of(to, 128), 128), :] = dot(masked, pk_ref[...]).astype(jnp.bfloat16)
        return 0

    lax.fori_loop(0, 2, make_vp, 0)

    def encode(values, chunk):
        biggest = jnp.max(jnp.abs(values), axis=1, keepdims=True)
        exponent = jnp.ceil(jnp.log2(jnp.maximum(biggest, 1e-30))) - 15.0
        q = jnp.clip(jnp.floor(values * jnp.exp2(-exponent) + 0.5), -32767.0, 32767.0)
        q = jnp.where(iota((ROWS_T, HALF), 1) < PAD, jnp.broadcast_to(exponent, (ROWS_T, HALF)), q)
        for n in range(5):
            part = q[:, n * LANES:(n + 1) * LANES]
            bq[chunk + n, z, yh] = part.astype(jnp.int32).astype(jnp.int16)

    def hi_copy(n):
        return copy(bq.at[n, z, yh], bq.at[n, z, yh], h_ss.at[n], h_rs.at[n], d_hi)

    def first_copies(n, side):
        at = yh if side == 0 else 1 - yh
        ref = bq.at[n, z, at]
        sem = 4 * side
        return (
            copy(ref, ref, zr_ss.at[n, sem], zr_rs.at[n, sem], d_right),
            copy(ref, ref, zl_ss.at[n, sem], zl_rs.at[n, sem], d_left),
        )

    def right_copy(n, s):
        at = (z - s + NZ) % NZ
        return copy(bq.at[n, at], bq.at[n, at], zr_ss.at[n, s], zr_rs.at[n, s], d_right)

    def left_copy(n, s):
        at = (z + s) % NZ
        return copy(bq.at[n, at], bq.at[n, at], zl_ss.at[n, s], zl_rs.at[n, s], d_left)

    def thin_copies(n, s):
        near, far = (z - s + NZ) % NZ, (z + s) % NZ
        right, left = bq.at[n, near, yh], bq.at[n, far, yh]
        if s == 3:
            right, left = right.at[pl.ds(0, CUT)], left.at[pl.ds(CUT, ROWS_T - CUT)]
        return (
            copy(right, right, zr_ss.at[n, s], zr_rs.at[n, s], d_right),
            copy(left, left, zl_ss.at[n, s], zl_rs.at[n, s], d_left),
        )

    def slot_copies(n, s):
        near, far = bq.at[n, (z - s + NZ) % NZ, yh], bq.at[n, (z + s) % NZ, yh]
        first = copy(near, near, t_ss.at[n - FULL, s - 1], t_rs.at[n - FULL, s - 1], d_hi)
        if s == 4:
            return (first,)
        return first, copy(far, far, t_ss.at[n - FULL, s + 3], t_rs.at[n - FULL, s + 3], d_hi)

    def right_last(n):
        at = (z - 3 + NZ) % NZ
        return copy(bq.at[n, at, 0], bq.at[n, at, 0], zr_ss.at[n, 3], zr_rs.at[n, 3], d_right)

    def left_last(n):
        at = (z + 3) % NZ
        return copy(bq.at[n, at, 1], bq.at[n, at, 1], zl_ss.at[n, 3], zl_rs.at[n, 3], d_left)

    def core_copy(n, h):
        return copy(csend.at[n, h], crecv.at[n, h], c_ss.at[n, h], c_rs.at[n, h], d_core)

    def lo_copy(n):
        return copy(ycode.at[n], yrecv.at[n], y_ss.at[n], y_rs.at[n], d_lo)

    def mirror_copy(n):
        to = (row, (c + 2 - n // 5) % 4, depth)
        return copy(r_own.at[n], r_recv.at[n], m_ss.at[n], m_rs.at[n], to)

    def start_both(pair):
        for one in pair:
            one.start()

    def own_start(n, _):
        hi_copy(n).start()
        start_both(first_copies(n, 0))
        return 0

    w1.wait_recv()
    opposite = x_ref[2].astype(jnp.float32) - wrecv[1].astype(jnp.float32)
    encode(jnp.where(lower, opposite, diag_ref[...]), 0)
    lax.fori_loop(0, 5, own_start, 0)
    make_vp(2, 0)
    w0.wait_recv()
    encode(x_ref[1].astype(jnp.float32) - wrecv[0].astype(jnp.float32), 5)
    lax.fori_loop(5, CHUNKS, own_start, 0)
    make_vp(3, 0)

    def products(half):
        both = dot(vp_ref[512 * half:512 * half + 512, :], bhl[...])
        return both[:, :LANES] + both[:, LANES:]

    def part_start(n):
        hi_copy(n).wait_recv()
        start_both(first_copies(n, 1))

    def forward(n, s):
        before = [(right_copy(n, s - 1), left_copy(n, s - 1))] if s > 1 else [first_copies(n, 0), first_copies(n, 1)]
        after = (right_last(n), left_last(n)) if s == 3 else (right_copy(n, s), left_copy(n, s))
        for side in range(2):
            for pair in before:
                pair[side].wait_recv()
            after[side].start()

    def forward_thin(n, s):
        before = thin_copies(n, s - 1) if s > 1 else first_copies(n, 0)
        after = thin_copies(n, s)
        for side in range(2):
            before[side].wait_recv()
            after[side].start()
        start_both(slot_copies(n, s))

    def end_thin(n):
        for one in thin_copies(n, 3):
            one.wait_recv()
        start_both(slot_copies(n, 4))

    def is_thin(n):
        return (n >= FULL) & (n < FIRST)

    def arrive(n):
        @pl.when(is_thin(n))
        def _():
            hi_copy(n).wait_recv()
            for s in range(1, 5):
                for one in slot_copies(n, s):
                    one.wait_recv()

        @pl.when(jnp.logical_not(is_thin(n)))
        def _():
            right_last(n).wait_recv()
            left_last(n).wait_recv()

    def expand(n):
        q = bq[n].reshape(DEPTH, LANES).astype(jnp.int32)

        @pl.when((n == 0) | (n == 5))
        def _():
            sc_ref[...] = jnp.broadcast_to(jnp.exp2(q[:, 0:1].astype(jnp.float32)), (DEPTH, LANES))

        s = sc_ref[...]
        hi = (q + 128) >> 8
        lo = q - (hi << 8)
        bhl[:, :LANES] = (hi.astype(jnp.float32) * (s * 256.0)).astype(jnp.bfloat16)
        bhl[:, LANES:] = (lo.astype(jnp.float32) * s).astype(jnp.bfloat16)

    def to_core(n):
        csend[n] = products(0).reshape(2, OUT_ROWS, LANES)
        core_copy(n, 0).start()
        core_copy(n, 1).start()

    def keep(n):
        both = products(1)
        ysend[n] = both[:OUT_ROWS]
        own[n] = both[OUT_ROWS:]

    def core_sum(n):
        core_copy(n, 0).wait_recv()
        part = ysend[n] + crecv[n, 0]
        biggest = jnp.max(jnp.abs(part), axis=0, keepdims=True)
        ex = jnp.ceil(jnp.log2(jnp.maximum(biggest, 1e-30))) - 15.0
        q = jnp.clip(jnp.floor(part * jnp.exp2(-ex) + 0.5), -32767.0, 32767.0)
        ycode[n, :OUT_ROWS] = q.astype(jnp.int32).astype(jnp.int16)
        ycode[n, OUT_ROWS:] = jnp.broadcast_to(ex, (16, LANES)).astype(jnp.int32).astype(jnp.int16)
        lo_copy(n).start()
        core_copy(n, 1).wait_recv()
        own[n] += crecv[n, 1]

    def finish(n):
        lo_copy(n).wait_recv()
        ex = yrecv[n, OUT_ROWS:].astype(jnp.int32).astype(jnp.float32)
        got = yrecv[n, :OUT_ROWS].astype(jnp.int32).astype(jnp.float32) * jnp.exp2(ex[0:1])
        r_own[n] = (own[n] + got).T.astype(jnp.bfloat16)
        mirror_copy(n).start()

    def place(block_ref, group):
        for q in range(4):

            @pl.when((c + group) % 4 == q)
            def _():
                for a in range(SUB):
                    at, to = PAD + SUB * a, OCC * a + SUB * q
                    acc_ref[to:to + SUB, :] = block_ref[at:at + SUB, :]

    def mirror_wait(n, _):
        mirror_copy(n).wait_recv()
        return 0

    def place_opposite():
        rows = iota((HALF, 1), 0) - PAD
        ia = div25(rows)
        ib = rows - SUB * ia
        mine = r_own[0:5].reshape(HALF, OUT_ROWS)
        direct = mine.astype(jnp.float32)
        turned = dot(pt_ref[...], mine)
        tmp_ref[...] = jnp.where(ib > ia, direct, jnp.where(ib < ia, -turned, 0.0))
        place(tmp_ref, 0)
        tmp_ref[...] = jnp.where(ib <= ia, direct, -dot(pt_ref[...], r_recv[0:5].reshape(HALF, OUT_ROWS)))
        place(tmp_ref, 2)

    def place_next():
        tmp_ref[...] = r_own[5:10].reshape(HALF, OUT_ROWS).astype(jnp.float32)
        place(tmp_ref, 1)

    def place_previous():
        tmp_ref[...] = -dot(pt_ref[...], r_recv[5:10].reshape(HALF, OUT_ROWS))
        place(tmp_ref, 3)

    def first_part(n, _):
        part_start(n)
        return 0

    lax.fori_loop(0, FULL, first_part, 0)
    lax.fori_loop(4, 8, make_vp, 0)

    def early(n, _):
        forward(n, 1)
        return 0

    def early_thin(n, _):
        forward_thin(n, 1)
        return 0

    def middle(n, _):
        forward(n, 2)
        return 0

    def middle_thin(n, _):
        forward_thin(n, 2)
        return 0

    def late(n, _):
        forward(n, 3)
        part_start(n + FIRST)
        return 0

    def late_thin(n, _):
        forward_thin(n, 3)
        return 0

    lax.fori_loop(0, FULL, early, 0)
    lax.fori_loop(FULL, FIRST, early_thin, 0)
    lax.fori_loop(0, FULL, middle, 0)
    lax.fori_loop(FULL, FIRST, middle_thin, 0)
    lax.fori_loop(0, FULL, late, 0)
    lax.fori_loop(FULL, FIRST, late_thin, 0)
    part_start(CHUNKS - 1)

    def event(i):
        n = FIRST + i % LAST
        for s in range(1, 4):

            @pl.when(i // LAST == s - 1)
            def _():
                forward(n, s)

    def body(t, _):
        @pl.when(t < FIRST)
        def _():
            event(2 * t)

        arrive(t)
        expand(t)
        to_core(t)

        @pl.when(t >= 1)
        def _():
            core_sum(t - 1)

        keep(t)

        @pl.when(t < FIRST)
        def _():
            event(2 * t + 1)

        @pl.when(t == 0)
        def _():
            for n in range(FULL, FIRST):
                end_thin(n)

        @pl.when(t >= 3)
        def _():
            finish(t - 3)

        return 0

    lax.fori_loop(0, CHUNKS, body, 0)

    def finish_some(n, _):
        finish(n)
        return 0

    def drain(n, _):
        hi_copy(n).wait_send()
        for one in first_copies(n, 0):
            one.wait_send()

        @pl.when(is_thin(n))
        def _():
            for s in range(1, 4):
                for one in thin_copies(n, s):
                    one.wait_send()
            for s in range(1, 5):
                for one in slot_copies(n, s):
                    one.wait_send()

        @pl.when(jnp.logical_not(is_thin(n)))
        def _():
            for one in first_copies(n, 1):
                one.wait_send()
            for s in range(1, 3):
                right_copy(n, s).wait_send()
                left_copy(n, s).wait_send()
            right_last(n).wait_send()
            left_last(n).wait_send()

        return 0

    def drain_sums(n, _):
        core_copy(n, 0).wait_send()
        core_copy(n, 1).wait_send()
        lo_copy(n).wait_send()
        return 0

    def drain_mirror(n, _):
        mirror_copy(n).wait_send()
        return 0

    core_sum(9)
    lax.fori_loop(7, 9, finish_some, 0)
    lax.fori_loop(0, CHUNKS, drain, 0)
    lax.fori_loop(0, 5, mirror_wait, 0)
    place_opposite()
    finish(9)
    w0.wait_send()
    lax.fori_loop(0, CHUNKS, drain_sums, 0)
    place_next()
    lax.fori_loop(5, CHUNKS, mirror_wait, 0)
    place_previous()
    out_ref[...] = acc_ref[...].astype(jnp.bfloat16)
    lax.fori_loop(0, CHUNKS, drain_mirror, 0)


def local(integrals, amplitudes, ab_irrep, cd_irrep):
    vmem = pl.BlockSpec(memory_space=pltpu.VMEM)
    bf, f32 = jnp.bfloat16, jnp.float32
    dma = pltpu.SemaphoreType.DMA
    n = CHUNKS
    scratch = [
        pltpu.VMEM((ROWS_T, WIDE), bf),
        pltpu.VMEM((1024, DEPTH), bf),
        pltpu.VMEM((1024, DEPTH), bf),
        pltpu.VMEM((DEPTH, DEPTH), bf),
        pltpu.VMEM((HALF, HALF), bf),
        pltpu.VMEM((4, ROWS_T, HALF), bf),
        pltpu.VMEM((ROWS_T, HALF), f32),
        pltpu.VMEM((2, ROWS_T, HALF), bf),
        pltpu.VMEM((2, ROWS_T, HALF), bf),
        pltpu.VMEM((n, NZ, 2, ROWS_T, LANES), jnp.int16),
        pltpu.VMEM((DEPTH, LANES), f32),
        pltpu.VMEM((DEPTH, 2 * LANES), bf),
        pltpu.VMEM((n, 2, OUT_ROWS, LANES), f32),
        pltpu.VMEM((n, 2, OUT_ROWS, LANES), f32),
        pltpu.VMEM((n, OUT_ROWS, LANES), f32),
        pltpu.VMEM((n, OUT_ROWS + 16, LANES), jnp.int16),
        pltpu.VMEM((n, OUT_ROWS + 16, LANES), jnp.int16),
        pltpu.VMEM((n, OUT_ROWS, LANES), f32),
        pltpu.VMEM((n, LANES, OUT_ROWS), bf),
        pltpu.VMEM((n, LANES, OUT_ROWS), bf),
        pltpu.VMEM((HALF, OUT_ROWS), f32),
        pltpu.VMEM((OCC * SUB, OUT_ROWS), f32),
        dma,
        dma((2,)), dma((2,)),
        dma((n,)), dma((n,)),
        dma((THIN, 7)), dma((THIN, 7)),
        dma((n, 5)), dma((n, 5)),
        dma((n, 5)), dma((n, 5)),
        dma((n, 2)), dma((n, 2)),
        dma((n,)), dma((n,)),
        dma((n,)), dma((n,)),
    ]
    turned = pl.pallas_call(
        kernel,
        out_shape=jax.ShapeDtypeStruct((OCC * SUB, OUT_ROWS), bf),
        in_specs=[vmem, vmem, vmem, pl.BlockSpec(memory_space=pl.ANY)],
        out_specs=vmem,
        scratch_shapes=scratch,
        compiler_params=pltpu.CompilerParams(
            collective_id=0, has_side_effects=True, vmem_limit_bytes=58 * 2**20
        ),
        name="ladder",
    )(amplitudes, ab_irrep, cd_irrep, integrals)
    return turned.T


def solution(mesh):
    in_specs = (P("row", "depth"), P("depth", "row", "col"), P("row"), P("depth"))
    out_specs = P(("row", "depth"), "col")
    return jax.shard_map(local, mesh=mesh, in_specs=in_specs, out_specs=out_specs, check_vma=False)
```

```python
import numpy as np

import jax
import jax.numpy as jnp
from jax import lax
from jax.experimental import pallas as pl
from jax.experimental.pallas import tpu as pltpu
from jax.sharding import PartitionSpec as P

OCC = 100
SUB = 25
NZ = 8
LANES = 128
CHUNKS = 10
HALF = 640
PAD = 15
FIRST = 6
LAST = CHUNKS - FIRST
THIN = 3
FULL = FIRST - THIN
CUT = 48
ROWS_T = 80
DEPTH = 1280
OUT_ROWS = 256
WIDE = 2560
MESH = pl.DeviceIdType.MESH


def iota(shape, dim):
    return lax.broadcasted_iota(jnp.int32, shape, dim)


def div25(v):
    return (v * 5243) >> 17


def one_hot(cond):
    return jnp.where(cond, 1.0, 0.0).astype(jnp.bfloat16)


def dot(a, b):
    return jnp.dot(a, b, preferred_element_type=jnp.float32)


def band(n):
    lanes = np.arange(n * LANES, (n + 1) * LANES) - PAD
    lanes = lanes[(lanes >= 0) & (lanes < SUB * SUB)]
    first = 100 * (lanes // SUB) + lanes % SUB
    low = first.min() // LANES * LANES
    high = -(-(first.max() + 76) // LANES) * LANES
    return int(low), int(min(high, WIDE))


def kernel(
    amp_ref, ab_ref, cd_ref, v_hbm, out_ref,
    t_ref, v_ref, vp_ref, pk_ref, pt_ref, x_ref, diag_ref, wsend, wrecv, bq, sc_ref, bhl,
    csend, crecv, ysend, ycode, yrecv, own, r_own, r_recv, tmp_ref, acc_ref,
    v_sem, w_ss, w_rs, h_ss, h_rs, t_ss, t_rs, zr_ss, zr_rs, zl_ss, zl_rs, c_ss, c_rs, y_ss, y_rs, m_ss, m_rs,
):
    row, c, depth = lax.axis_index("row"), lax.axis_index("col"), lax.axis_index("depth")
    z, yh = row // 2, row % 2
    yl, core = depth // 2, depth % 2
    d_right = ((row + 2) % 16, c, depth)
    d_left = ((row + 14) % 16, c, depth)
    d_hi = (2 * z + 1 - yh, c, depth)
    d_core = (row, c, 2 * yl + 1 - core)
    d_lo = (row, c, 2 * (1 - yl) + core)
    x_next = (row, (c + 1) % 4, depth)
    x_opp = (row, (c + 2) % 4, depth)
    x_prev = (row, (c + 3) % 4, depth)

    def copy(src, dst, ss, rs, dev):
        return pltpu.make_async_remote_copy(
            src_ref=src, dst_ref=dst, send_sem=ss, recv_sem=rs, device_id=dev, device_id_type=MESH
        )

    v_copy = pltpu.make_async_copy(v_hbm, v_ref, v_sem)
    v_copy.start()

    barrier = pltpu.get_barrier_semaphore()
    for dev in (d_right, d_left, d_hi, d_core, d_lo, x_next, x_opp, x_prev):
        pl.semaphore_signal(barrier, inc=1, device_id=dev, device_id_type=MESH)

    t_ref[:, 2432:] = jnp.zeros((ROWS_T, LANES), jnp.bfloat16)
    t_ref[:, : OCC * SUB] = amp_ref[...].reshape(ROWS_T, OCC * SUB)

    u = iota((1, HALF), 1) - PAD
    a = div25(u)
    b = u - SUB * a
    flip = jnp.where(u >= 0, PAD + SUB * b + a, -1)
    lower = b <= a
    pt_ref[...] = one_hot(iota((HALF, HALF), 0) == flip)

    for n in range(HALF // LANES):
        low, high = band(n)
        u = iota((1, LANES), 1) + (n * LANES - PAD)
        a = div25(u)
        first = 100 * a + (u - SUB * a)
        r = iota((high - low, LANES), 0) + low
        mats = []
        for g in range(4):
            want = jnp.where((u >= 0), first + SUB * ((c + g) % 4), -1)
            mats.append(one_hot(r == want))
        got = dot(t_ref[:, low:high], jnp.concatenate(mats, axis=1)).astype(jnp.bfloat16)
        for g in range(4):
            x_ref[g, :, n * LANES:(n + 1) * LANES] = got[:, g * LANES:(g + 1) * LANES]

    wsend[1] = dot(x_ref[2], pt_ref[...]).astype(jnp.bfloat16)
    pl.semaphore_wait(barrier, 8)
    w0 = copy(wsend.at[0], wrecv.at[0], w_ss.at[0], w_rs.at[0], x_prev)
    w1 = copy(wsend.at[1], wrecv.at[1], w_ss.at[1], w_rs.at[1], x_opp)
    w1.start()
    wsend[0] = dot(x_ref[3], pt_ref[...]).astype(jnp.bfloat16)
    x0 = x_ref[0]
    diag_ref[...] = x0.astype(jnp.float32) - dot(x0, pt_ref[...])

    k = iota((1, DEPTH), 1)
    zz = (k * 3277) >> 19
    rem = k - 160 * zz
    hh = jnp.where(rem >= 80, 1, 0)
    m = rem - 80 * hh
    from_k = 32 * (m >> 1) + 4 * zz + 2 * hh + (m & 1)

    def make_pk(i, _):
        base = pl.multiple_of(i * 256, 256)
        pk_ref[pl.ds(base, 256), :] = one_hot(iota((256, DEPTH), 0) + base == from_k)
        return 0

    lax.fori_loop(0, DEPTH // 256, make_pk, 0)
    w1.wait_send()
    w0.start()
    v_copy.wait()

    def make_vp(i, _):
        to = 512 * jnp.where(i // 2 % 2 == core, 1, 0) + 256 * jnp.where(i // 4 == yl, 1, 0) + 128 * (i % 2)
        base = pl.multiple_of(i * 128, 128)
        rows = pl.ds(base, 128)
        label = jnp.broadcast_to(ab_ref[rows].reshape(1, 128), (128, 128)).T
        keep = jnp.concatenate([label] * 10, axis=1) == cd_ref[...].reshape(1, DEPTH)
        masked = jnp.where(keep, v_ref[rows, :].astype(jnp.float32), 0.0).astype(jnp.bfloat16)
        vp_ref[pl.ds(pl.multiple_of(to, 128), 128), :] = dot(masked, pk_ref[...]).astype(jnp.bfloat16)
        return 0

    lax.fori_loop(0, 2, make_vp, 0)

    def encode(values, chunk):
        biggest = jnp.max(jnp.abs(values), axis=1, keepdims=True)
        exponent = jnp.ceil(jnp.log2(jnp.maximum(biggest, 1e-30))) - 15.0
        q = jnp.clip(jnp.floor(values * jnp.exp2(-exponent) + 0.5), -32767.0, 32767.0)
        q = jnp.where(iota((ROWS_T, HALF), 1) < PAD, jnp.broadcast_to(exponent, (ROWS_T, HALF)), q)
        for n in range(5):
            part = q[:, n * LANES:(n + 1) * LANES]
            bq[chunk + n, z, yh] = part.astype(jnp.int32).astype(jnp.int16)

    def hi_copy(n):
        return copy(bq.at[n, z, yh], bq.at[n, z, yh], h_ss.at[n], h_rs.at[n], d_hi)

    def first_copies(n, side):
        at = yh if side == 0 else 1 - yh
        ref = bq.at[n, z, at]
        sem = 4 * side
        return (
            copy(ref, ref, zr_ss.at[n, sem], zr_rs.at[n, sem], d_right),
            copy(ref, ref, zl_ss.at[n, sem], zl_rs.at[n, sem], d_left),
        )

    def right_copy(n, s):
        at = (z - s + NZ) % NZ
        return copy(bq.at[n, at], bq.at[n, at], zr_ss.at[n, s], zr_rs.at[n, s], d_right)

    def left_copy(n, s):
        at = (z + s) % NZ
        return copy(bq.at[n, at], bq.at[n, at], zl_ss.at[n, s], zl_rs.at[n, s], d_left)

    def thin_copies(n, s):
        near, far = (z - s + NZ) % NZ, (z + s) % NZ
        right, left = bq.at[n, near, yh], bq.at[n, far, yh]
        if s == 3:
            right, left = right.at[pl.ds(0, CUT)], left.at[pl.ds(CUT, ROWS_T - CUT)]
        return (
            copy(right, right, zr_ss.at[n, s], zr_rs.at[n, s], d_right),
            copy(left, left, zl_ss.at[n, s], zl_rs.at[n, s], d_left),
        )

    def slot_copies(n, s):
        near, far = bq.at[n, (z - s + NZ) % NZ, yh], bq.at[n, (z + s) % NZ, yh]
        first = copy(near, near, t_ss.at[n - FULL, s - 1], t_rs.at[n - FULL, s - 1], d_hi)
        if s == 4:
            return (first,)
        return first, copy(far, far, t_ss.at[n - FULL, s + 3], t_rs.at[n - FULL, s + 3], d_hi)

    def right_last(n):
        at = (z - 3 + NZ) % NZ
        return copy(bq.at[n, at, 0], bq.at[n, at, 0], zr_ss.at[n, 3], zr_rs.at[n, 3], d_right)

    def left_last(n):
        at = (z + 3) % NZ
        return copy(bq.at[n, at, 1], bq.at[n, at, 1], zl_ss.at[n, 3], zl_rs.at[n, 3], d_left)

    def core_copy(n, h):
        return copy(csend.at[n, h], crecv.at[n, h], c_ss.at[n, h], c_rs.at[n, h], d_core)

    def lo_copy(n):
        return copy(ycode.at[n], yrecv.at[n], y_ss.at[n], y_rs.at[n], d_lo)

    def mirror_copy(n):
        to = (row, (c + 2 - n // 5) % 4, depth)
        return copy(r_own.at[n], r_recv.at[n], m_ss.at[n], m_rs.at[n], to)

    def start_both(pair):
        for one in pair:
            one.start()

    def own_start(n, _):
        hi_copy(n).start()
        start_both(first_copies(n, 0))
        return 0

    w1.wait_recv()
    opposite = x_ref[2].astype(jnp.float32) - wrecv[1].astype(jnp.float32)
    encode(jnp.where(lower, opposite, diag_ref[...]), 0)
    lax.fori_loop(0, 5, own_start, 0)
    make_vp(2, 0)
    w0.wait_recv()
    encode(x_ref[1].astype(jnp.float32) - wrecv[0].astype(jnp.float32), 5)
    lax.fori_loop(5, CHUNKS, own_start, 0)
    make_vp(3, 0)

    def products(half):
        both = dot(vp_ref[512 * half:512 * half + 512, :], bhl[...])
        return both[:, :LANES] + both[:, LANES:]

    def part_start(n):
        hi_copy(n).wait_recv()
        start_both(first_copies(n, 1))

    def forward(n, s):
        before = [(right_copy(n, s - 1), left_copy(n, s - 1))] if s > 1 else [first_copies(n, 0), first_copies(n, 1)]
        after = (right_last(n), left_last(n)) if s == 3 else (right_copy(n, s), left_copy(n, s))
        for side in range(2):
            for pair in before:
                pair[side].wait_recv()
            after[side].start()

    def forward_thin(n, s):
        before = thin_copies(n, s - 1) if s > 1 else first_copies(n, 0)
        after = thin_copies(n, s)
        for side in range(2):
            before[side].wait_recv()
            after[side].start()
        start_both(slot_copies(n, s))

    def end_thin(n):
        for one in thin_copies(n, 3):
            one.wait_recv()
        start_both(slot_copies(n, 4))

    def is_thin(n):
        return (n >= FULL) & (n < FIRST)

    def arrive(n):
        @pl.when(is_thin(n))
        def _():
            hi_copy(n).wait_recv()
            for s in range(1, 5):
                for one in slot_copies(n, s):
                    one.wait_recv()

        @pl.when(jnp.logical_not(is_thin(n)))
        def _():
            right_last(n).wait_recv()
            left_last(n).wait_recv()

    def expand(n):
        q = bq[n].reshape(DEPTH, LANES).astype(jnp.int32)

        @pl.when((n == 0) | (n == 5))
        def _():
            sc_ref[...] = jnp.broadcast_to(jnp.exp2(q[:, 0:1].astype(jnp.float32)), (DEPTH, LANES))

        s = sc_ref[...]
        hi = (q + 128) >> 8
        lo = q - (hi << 8)
        bhl[:, :LANES] = (hi.astype(jnp.float32) * (s * 256.0)).astype(jnp.bfloat16)
        bhl[:, LANES:] = (lo.astype(jnp.float32) * s).astype(jnp.bfloat16)

    def to_core(n):
        csend[n] = products(0).reshape(2, OUT_ROWS, LANES)
        core_copy(n, 0).start()
        core_copy(n, 1).start()

    def keep(n):
        both = products(1)
        ysend[n] = both[:OUT_ROWS]
        own[n] = both[OUT_ROWS:]

    def core_arrive(n):
        core_copy(n, 0).wait_recv()
        core_copy(n, 1).wait_recv()

    def core_sum(n):
        part = ysend[n] + crecv[n, 0]
        biggest = jnp.max(jnp.abs(part), axis=0, keepdims=True)
        ex = jnp.ceil(jnp.log2(jnp.maximum(biggest, 1e-30))) - 15.0
        q = jnp.clip(jnp.floor(part * jnp.exp2(-ex) + 0.5), -32767.0, 32767.0)
        ycode[n, :OUT_ROWS] = q.astype(jnp.int32).astype(jnp.int16)
        ycode[n, OUT_ROWS:] = jnp.broadcast_to(ex, (16, LANES)).astype(jnp.int32).astype(jnp.int16)
        own[n] += crecv[n, 1]

    def finish(n):
        lo_copy(n).wait_recv()
        ex = yrecv[n, OUT_ROWS:].astype(jnp.int32).astype(jnp.float32)
        got = yrecv[n, :OUT_ROWS].astype(jnp.int32).astype(jnp.float32) * jnp.exp2(ex[0:1])
        r_own[n] = (own[n] + got).T.astype(jnp.bfloat16)
        mirror_copy(n).start()

    def place(block_ref, group):
        for q in range(4):

            @pl.when((c + group) % 4 == q)
            def _():
                for a in range(SUB):
                    at, to = PAD + SUB * a, OCC * a + SUB * q
                    acc_ref[to:to + SUB, :] = block_ref[at:at + SUB, :]

    def mirror_wait(n, _):
        mirror_copy(n).wait_recv()
        return 0

    def place_opposite():
        rows = iota((HALF, 1), 0) - PAD
        ia = div25(rows)
        ib = rows - SUB * ia
        mine = r_own[0:5].reshape(HALF, OUT_ROWS)
        direct = mine.astype(jnp.float32)
        turned = dot(pt_ref[...], mine)
        tmp_ref[...] = jnp.where(ib > ia, direct, jnp.where(ib < ia, -turned, 0.0))
        place(tmp_ref, 0)
        tmp_ref[...] = jnp.where(ib <= ia, direct, -dot(pt_ref[...], r_recv[0:5].reshape(HALF, OUT_ROWS)))
        place(tmp_ref, 2)

    def place_next():
        tmp_ref[...] = r_own[5:10].reshape(HALF, OUT_ROWS).astype(jnp.float32)
        place(tmp_ref, 1)

    def place_previous():
        tmp_ref[...] = -dot(pt_ref[...], r_recv[5:10].reshape(HALF, OUT_ROWS))
        place(tmp_ref, 3)

    def first_part(n, _):
        part_start(n)
        return 0

    lax.fori_loop(0, FULL, first_part, 0)
    lax.fori_loop(4, 8, make_vp, 0)

    def early(n, _):
        forward(n, 1)
        return 0

    def early_thin(n, _):
        forward_thin(n, 1)
        return 0

    def middle(n, _):
        forward(n, 2)
        return 0

    def middle_thin(n, _):
        forward_thin(n, 2)
        return 0

    def late(n, _):
        forward(n, 3)
        part_start(n + FIRST)
        return 0

    def late_thin(n, _):
        forward_thin(n, 3)
        return 0

    lax.fori_loop(0, FULL, early, 0)
    lax.fori_loop(FULL, FIRST, early_thin, 0)
    lax.fori_loop(0, FULL, middle, 0)
    lax.fori_loop(FULL, FIRST, middle_thin, 0)
    lax.fori_loop(0, FULL, late, 0)
    lax.fori_loop(FULL, FIRST, late_thin, 0)
    part_start(CHUNKS - 1)

    def event(i):
        n = FIRST + i % LAST
        for s in range(1, 4):

            @pl.when(i // LAST == s - 1)
            def _():
                forward(n, s)

    def opening(t, _):
        event(2 * t)
        arrive(t)
        expand(t)
        to_core(t)
        event(2 * t + 1)
        keep(t)

        @pl.when(t == 0)
        def _():
            for n in range(FULL, FIRST):
                end_thin(n)

        return 0

    def body(t, _):
        @pl.when(t < FIRST)
        def _():
            event(2 * t)

        arrive(t)
        expand(t)
        to_core(t)

        @pl.when(t < FIRST)
        def _():
            event(2 * t + 1)

        core_arrive(t - 2)
        core_sum(t - 2)
        keep(t)
        lo_copy(t - 2).start()

        @pl.when(t >= 4)
        def _():
            finish(t - 4)

        return 0

    lax.fori_loop(0, 2, opening, 0)
    lax.fori_loop(2, CHUNKS, body, 0)

    def finish_some(n, _):
        finish(n)
        return 0

    def drain(n, _):
        hi_copy(n).wait_send()
        for one in first_copies(n, 0):
            one.wait_send()

        @pl.when(is_thin(n))
        def _():
            for s in range(1, 4):
                for one in thin_copies(n, s):
                    one.wait_send()
            for s in range(1, 5):
                for one in slot_copies(n, s):
                    one.wait_send()

        @pl.when(jnp.logical_not(is_thin(n)))
        def _():
            for one in first_copies(n, 1):
                one.wait_send()
            for s in range(1, 3):
                right_copy(n, s).wait_send()
                left_copy(n, s).wait_send()
            right_last(n).wait_send()
            left_last(n).wait_send()

        return 0

    def drain_sums(n, _):
        core_copy(n, 0).wait_send()
        core_copy(n, 1).wait_send()
        lo_copy(n).wait_send()
        return 0

    def drain_mirror(n, _):
        mirror_copy(n).wait_send()
        return 0

    def last_sums(n, _):
        core_arrive(n)
        core_sum(n)
        lo_copy(n).start()
        return 0

    lax.fori_loop(8, CHUNKS, last_sums, 0)
    lax.fori_loop(6, 9, finish_some, 0)
    lax.fori_loop(0, CHUNKS, drain, 0)
    lax.fori_loop(0, 5, mirror_wait, 0)
    place_opposite()
    finish(9)
    w0.wait_send()
    lax.fori_loop(0, CHUNKS, drain_sums, 0)
    place_next()
    lax.fori_loop(5, CHUNKS, mirror_wait, 0)
    place_previous()
    out_ref[...] = acc_ref[...].astype(jnp.bfloat16)
    lax.fori_loop(0, CHUNKS, drain_mirror, 0)


def local(integrals, amplitudes, ab_irrep, cd_irrep):
    vmem = pl.BlockSpec(memory_space=pltpu.VMEM)
    bf, f32 = jnp.bfloat16, jnp.float32
    dma = pltpu.SemaphoreType.DMA
    n = CHUNKS
    scratch = [
        pltpu.VMEM((ROWS_T, WIDE), bf),
        pltpu.VMEM((1024, DEPTH), bf),
        pltpu.VMEM((1024, DEPTH), bf),
        pltpu.VMEM((DEPTH, DEPTH), bf),
        pltpu.VMEM((HALF, HALF), bf),
        pltpu.VMEM((4, ROWS_T, HALF), bf),
        pltpu.VMEM((ROWS_T, HALF), f32),
        pltpu.VMEM((2, ROWS_T, HALF), bf),
        pltpu.VMEM((2, ROWS_T, HALF), bf),
        pltpu.VMEM((n, NZ, 2, ROWS_T, LANES), jnp.int16),
        pltpu.VMEM((DEPTH, LANES), f32),
        pltpu.VMEM((DEPTH, 2 * LANES), bf),
        pltpu.VMEM((n, 2, OUT_ROWS, LANES), f32),
        pltpu.VMEM((n, 2, OUT_ROWS, LANES), f32),
        pltpu.VMEM((n, OUT_ROWS, LANES), f32),
        pltpu.VMEM((n, OUT_ROWS + 16, LANES), jnp.int16),
        pltpu.VMEM((n, OUT_ROWS + 16, LANES), jnp.int16),
        pltpu.VMEM((n, OUT_ROWS, LANES), f32),
        pltpu.VMEM((n, LANES, OUT_ROWS), bf),
        pltpu.VMEM((n, LANES, OUT_ROWS), bf),
        pltpu.VMEM((HALF, OUT_ROWS), f32),
        pltpu.VMEM((OCC * SUB, OUT_ROWS), f32),
        dma,
        dma((2,)), dma((2,)),
        dma((n,)), dma((n,)),
        dma((THIN, 7)), dma((THIN, 7)),
        dma((n, 5)), dma((n, 5)),
        dma((n, 5)), dma((n, 5)),
        dma((n, 2)), dma((n, 2)),
        dma((n,)), dma((n,)),
        dma((n,)), dma((n,)),
    ]
    turned = pl.pallas_call(
        kernel,
        out_shape=jax.ShapeDtypeStruct((OCC * SUB, OUT_ROWS), bf),
        in_specs=[vmem, vmem, vmem, pl.BlockSpec(memory_space=pl.ANY)],
        out_specs=vmem,
        scratch_shapes=scratch,
        compiler_params=pltpu.CompilerParams(
            collective_id=0, has_side_effects=True, vmem_limit_bytes=58 * 2**20
        ),
        name="ladder",
    )(amplitudes, ab_irrep, cd_irrep, integrals)
    return turned.T


def solution(mesh):
    in_specs = (P("row", "depth"), P("depth", "row", "col"), P("row"), P("depth"))
    out_specs = P(("row", "depth"), "col")
    return jax.shard_map(local, mesh=mesh, in_specs=in_specs, out_specs=out_specs, check_vma=False)
```

```python
import numpy as np

import jax
import jax.numpy as jnp
from jax import lax
from jax.experimental import pallas as pl
from jax.experimental.pallas import tpu as pltpu
from jax.sharding import PartitionSpec as P

OCC = 100
SUB = 25
NZ = 8
LANES = 128
CHUNKS = 10
HALF = 640
PAD = 15
FIRST = 5
EVENTS = {
    (0, 0): [(5, 1), (6, 1), (7, 1)], (0, 1): [(8, 1), (9, 1)],
    (2, 0): [(5, 2)], (2, 1): [(6, 2)], (2, 2): [(7, 2)],
    (3, 1): [(8, 2)], (3, 2): [(9, 2)],
    (4, 1): [(5, 3)], (4, 2): [(6, 3)],
    (5, 0): [(7, 3)], (5, 1): [(8, 3)], (5, 2): [(9, 3)],
}
THIN = 3
FULL = FIRST - THIN
CUT = 48
ROWS_T = 80
DEPTH = 1280
OUT_ROWS = 256
WIDE = 2560
MESH = pl.DeviceIdType.MESH


def iota(shape, dim):
    return lax.broadcasted_iota(jnp.int32, shape, dim)


def div25(v):
    return (v * 5243) >> 17


def one_hot(cond):
    return jnp.where(cond, 1.0, 0.0).astype(jnp.bfloat16)


def dot(a, b):
    return jnp.dot(a, b, preferred_element_type=jnp.float32)


def band(n):
    lanes = np.arange(n * LANES, (n + 1) * LANES) - PAD
    lanes = lanes[(lanes >= 0) & (lanes < SUB * SUB)]
    first = 100 * (lanes // SUB) + lanes % SUB
    low = first.min() // LANES * LANES
    high = -(-(first.max() + 76) // LANES) * LANES
    return int(low), int(min(high, WIDE))


def kernel(
    amp_ref, ab_ref, cd_ref, v_hbm, out_ref,
    t_ref, v_ref, vp_ref, pk_ref, pt_ref, x_ref, diag_ref, wsend, wrecv, bq, sc_ref, bhl,
    csend, crecv, ysend, ycode, yrecv, own, r_own, r_recv, tmp_ref, acc_ref,
    v_sem, w_ss, w_rs, h_ss, h_rs, t_ss, t_rs, zr_ss, zr_rs, zl_ss, zl_rs, c_ss, c_rs, y_ss, y_rs, m_ss, m_rs,
):
    row, c, depth = lax.axis_index("row"), lax.axis_index("col"), lax.axis_index("depth")
    z, yh = row // 2, row % 2
    yl, core = depth // 2, depth % 2
    d_right = ((row + 2) % 16, c, depth)
    d_left = ((row + 14) % 16, c, depth)
    d_hi = (2 * z + 1 - yh, c, depth)
    d_core = (row, c, 2 * yl + 1 - core)
    d_lo = (row, c, 2 * (1 - yl) + core)
    x_next = (row, (c + 1) % 4, depth)
    x_opp = (row, (c + 2) % 4, depth)
    x_prev = (row, (c + 3) % 4, depth)

    def copy(src, dst, ss, rs, dev):
        return pltpu.make_async_remote_copy(
            src_ref=src, dst_ref=dst, send_sem=ss, recv_sem=rs, device_id=dev, device_id_type=MESH
        )

    v_copy = pltpu.make_async_copy(v_hbm, v_ref, v_sem)
    v_copy.start()

    barrier = pltpu.get_barrier_semaphore()
    for dev in (d_right, d_left, d_hi, d_core, d_lo, x_next, x_opp, x_prev):
        pl.semaphore_signal(barrier, inc=1, device_id=dev, device_id_type=MESH)

    t_ref[:, 2432:] = jnp.zeros((ROWS_T, LANES), jnp.bfloat16)
    t_ref[:, : OCC * SUB] = amp_ref[...].reshape(ROWS_T, OCC * SUB)

    u = iota((1, HALF), 1) - PAD
    a = div25(u)
    b = u - SUB * a
    flip = jnp.where(u >= 0, PAD + SUB * b + a, -1)
    lower = b <= a
    pt_ref[...] = one_hot(iota((HALF, HALF), 0) == flip)

    for n in range(HALF // LANES):
        low, high = band(n)
        u = iota((1, LANES), 1) + (n * LANES - PAD)
        a = div25(u)
        first = 100 * a + (u - SUB * a)
        r = iota((high - low, LANES), 0) + low
        mats = []
        for g in range(4):
            want = jnp.where((u >= 0), first + SUB * ((c + g) % 4), -1)
            mats.append(one_hot(r == want))
        got = dot(t_ref[:, low:high], jnp.concatenate(mats, axis=1)).astype(jnp.bfloat16)
        for g in range(4):
            x_ref[g, :, n * LANES:(n + 1) * LANES] = got[:, g * LANES:(g + 1) * LANES]

    wsend[1] = dot(x_ref[2], pt_ref[...]).astype(jnp.bfloat16)
    pl.semaphore_wait(barrier, 8)
    w0 = copy(wsend.at[0], wrecv.at[0], w_ss.at[0], w_rs.at[0], x_prev)
    w1 = copy(wsend.at[1], wrecv.at[1], w_ss.at[1], w_rs.at[1], x_opp)
    w1.start()
    wsend[0] = dot(x_ref[3], pt_ref[...]).astype(jnp.bfloat16)
    x0 = x_ref[0]
    diag_ref[...] = x0.astype(jnp.float32) - dot(x0, pt_ref[...])

    k = iota((1, DEPTH), 1)
    zz = (k * 3277) >> 19
    rem = k - 160 * zz
    hh = jnp.where(rem >= 80, 1, 0)
    m = rem - 80 * hh
    from_k = 32 * (m >> 1) + 4 * zz + 2 * hh + (m & 1)

    def make_pk(i, _):
        base = pl.multiple_of(i * 256, 256)
        pk_ref[pl.ds(base, 256), :] = one_hot(iota((256, DEPTH), 0) + base == from_k)
        return 0

    lax.fori_loop(0, DEPTH // 256, make_pk, 0)
    w1.wait_send()
    w0.start()
    v_copy.wait()

    def make_vp(i, _):
        to = 512 * jnp.where(i // 2 % 2 == core, 1, 0) + 256 * jnp.where(i // 4 == yl, 1, 0) + 128 * (i % 2)
        base = pl.multiple_of(i * 128, 128)
        rows = pl.ds(base, 128)
        label = jnp.broadcast_to(ab_ref[rows].reshape(1, 128), (128, 128)).T
        keep = jnp.concatenate([label] * 10, axis=1) == cd_ref[...].reshape(1, DEPTH)
        masked = jnp.where(keep, v_ref[rows, :].astype(jnp.float32), 0.0).astype(jnp.bfloat16)
        vp_ref[pl.ds(pl.multiple_of(to, 128), 128), :] = dot(masked, pk_ref[...]).astype(jnp.bfloat16)
        return 0

    lax.fori_loop(0, 2, make_vp, 0)

    def encode(values, chunk):
        biggest = jnp.max(jnp.abs(values), axis=1, keepdims=True)
        exponent = jnp.ceil(jnp.log2(jnp.maximum(biggest, 1e-30))) - 15.0
        q = jnp.clip(jnp.floor(values * jnp.exp2(-exponent) + 0.5), -32767.0, 32767.0)
        q = jnp.where(iota((ROWS_T, HALF), 1) < PAD, jnp.broadcast_to(exponent, (ROWS_T, HALF)), q)
        for n in range(5):
            part = q[:, n * LANES:(n + 1) * LANES]
            bq[chunk + n, z, yh] = part.astype(jnp.int32).astype(jnp.int16)

    def hi_copy(n):
        return copy(bq.at[n, z, yh], bq.at[n, z, yh], h_ss.at[n], h_rs.at[n], d_hi)

    def first_copies(n, side):
        at = yh if side == 0 else 1 - yh
        ref = bq.at[n, z, at]
        sem = 4 * side
        return (
            copy(ref, ref, zr_ss.at[n, sem], zr_rs.at[n, sem], d_right),
            copy(ref, ref, zl_ss.at[n, sem], zl_rs.at[n, sem], d_left),
        )

    def right_copy(n, s):
        at = (z - s + NZ) % NZ
        return copy(bq.at[n, at], bq.at[n, at], zr_ss.at[n, s], zr_rs.at[n, s], d_right)

    def left_copy(n, s):
        at = (z + s) % NZ
        return copy(bq.at[n, at], bq.at[n, at], zl_ss.at[n, s], zl_rs.at[n, s], d_left)

    def thin_copies(n, s):
        near, far = (z - s + NZ) % NZ, (z + s) % NZ
        right, left = bq.at[n, near, yh], bq.at[n, far, yh]
        if s == 3:
            right, left = right.at[pl.ds(0, CUT)], left.at[pl.ds(CUT, ROWS_T - CUT)]
        return (
            copy(right, right, zr_ss.at[n, s], zr_rs.at[n, s], d_right),
            copy(left, left, zl_ss.at[n, s], zl_rs.at[n, s], d_left),
        )

    def slot_copies(n, s):
        near, far = bq.at[n, (z - s + NZ) % NZ, yh], bq.at[n, (z + s) % NZ, yh]
        first = copy(near, near, t_ss.at[n - FULL, s - 1], t_rs.at[n - FULL, s - 1], d_hi)
        if s == 4:
            return (first,)
        return first, copy(far, far, t_ss.at[n - FULL, s + 3], t_rs.at[n - FULL, s + 3], d_hi)

    def right_last(n):
        at = (z - 3 + NZ) % NZ
        return copy(bq.at[n, at, 0], bq.at[n, at, 0], zr_ss.at[n, 3], zr_rs.at[n, 3], d_right)

    def left_last(n):
        at = (z + 3) % NZ
        return copy(bq.at[n, at, 1], bq.at[n, at, 1], zl_ss.at[n, 3], zl_rs.at[n, 3], d_left)

    def core_copy(n, h):
        return copy(csend.at[n, h], crecv.at[n, h], c_ss.at[n, h], c_rs.at[n, h], d_core)

    def lo_copy(n):
        return copy(ycode.at[n], yrecv.at[n], y_ss.at[n], y_rs.at[n], d_lo)

    def mirror_copy(n):
        to = (row, (c + 2 - n // 5) % 4, depth)
        return copy(r_own.at[n], r_recv.at[n], m_ss.at[n], m_rs.at[n], to)

    def start_both(pair):
        for one in pair:
            one.start()

    def own_start(n, _):
        hi_copy(n).start()
        start_both(first_copies(n, 0))
        return 0

    w1.wait_recv()
    opposite = x_ref[2].astype(jnp.float32) - wrecv[1].astype(jnp.float32)
    encode(jnp.where(lower, opposite, diag_ref[...]), 0)
    lax.fori_loop(0, 5, own_start, 0)
    make_vp(2, 0)
    w0.wait_recv()
    encode(x_ref[1].astype(jnp.float32) - wrecv[0].astype(jnp.float32), 5)
    lax.fori_loop(5, CHUNKS, own_start, 0)
    make_vp(3, 0)

    def products(half):
        both = dot(vp_ref[512 * half:512 * half + 512, :], bhl[...])
        return both[:, :LANES] + both[:, LANES:]

    def part_start(n):
        hi_copy(n).wait_recv()
        start_both(first_copies(n, 1))

    def forward(n, s):
        before = [(right_copy(n, s - 1), left_copy(n, s - 1))] if s > 1 else [first_copies(n, 0), first_copies(n, 1)]
        after = (right_last(n), left_last(n)) if s == 3 else (right_copy(n, s), left_copy(n, s))
        for side in range(2):
            for pair in before:
                pair[side].wait_recv()
            after[side].start()

    def forward_thin(n, s):
        before = thin_copies(n, s - 1) if s > 1 else first_copies(n, 0)
        after = thin_copies(n, s)
        for side in range(2):
            before[side].wait_recv()
            after[side].start()
        start_both(slot_copies(n, s))

    def end_thin(n):
        for one in thin_copies(n, 3):
            one.wait_recv()
        start_both(slot_copies(n, 4))

    def is_thin(n):
        return (n >= FULL) & (n < FIRST)

    def arrive(n):
        @pl.when(is_thin(n))
        def _():
            hi_copy(n).wait_recv()
            for s in range(1, 5):
                for one in slot_copies(n, s):
                    one.wait_recv()

        @pl.when(jnp.logical_not(is_thin(n)))
        def _():
            right_last(n).wait_recv()
            left_last(n).wait_recv()

    def expand(n):
        q = bq[n].reshape(DEPTH, LANES).astype(jnp.int32)

        @pl.when((n == 0) | (n == 5))
        def _():
            sc_ref[...] = jnp.broadcast_to(jnp.exp2(q[:, 0:1].astype(jnp.float32)), (DEPTH, LANES))

        s = sc_ref[...]
        hi = (q + 128) >> 8
        lo = q - (hi << 8)
        bhl[:, :LANES] = (hi.astype(jnp.float32) * (s * 256.0)).astype(jnp.bfloat16)
        bhl[:, LANES:] = (lo.astype(jnp.float32) * s).astype(jnp.bfloat16)

    def to_core(n):
        csend[n] = products(0).reshape(2, OUT_ROWS, LANES)
        core_copy(n, 0).start()
        core_copy(n, 1).start()

    def keep(n):
        both = products(1)
        ysend[n] = both[:OUT_ROWS]
        own[n] = both[OUT_ROWS:]

    def core_arrive(n):
        core_copy(n, 0).wait_recv()
        core_copy(n, 1).wait_recv()

    def core_sum(n):
        part = ysend[n] + crecv[n, 0]
        biggest = jnp.max(jnp.abs(part), axis=0, keepdims=True)
        ex = jnp.ceil(jnp.log2(jnp.maximum(biggest, 1e-30))) - 15.0
        q = jnp.clip(jnp.floor(part * jnp.exp2(-ex) + 0.5), -32767.0, 32767.0)
        ycode[n, :OUT_ROWS] = q.astype(jnp.int32).astype(jnp.int16)
        ycode[n, OUT_ROWS:] = jnp.broadcast_to(ex, (16, LANES)).astype(jnp.int32).astype(jnp.int16)
        own[n] += crecv[n, 1]

    def finish(n):
        lo_copy(n).wait_recv()
        ex = yrecv[n, OUT_ROWS:].astype(jnp.int32).astype(jnp.float32)
        got = yrecv[n, :OUT_ROWS].astype(jnp.int32).astype(jnp.float32) * jnp.exp2(ex[0:1])
        r_own[n] = (own[n] + got).T.astype(jnp.bfloat16)
        mirror_copy(n).start()

    def place(block_ref, group):
        for q in range(4):

            @pl.when((c + group) % 4 == q)
            def _():
                for a in range(SUB):
                    at, to = PAD + SUB * a, OCC * a + SUB * q
                    acc_ref[to:to + SUB, :] = block_ref[at:at + SUB, :]

    def mirror_wait(n, _):
        mirror_copy(n).wait_recv()
        return 0

    def place_opposite():
        rows = iota((HALF, 1), 0) - PAD
        ia = div25(rows)
        ib = rows - SUB * ia
        mine = r_own[0:5].reshape(HALF, OUT_ROWS)
        direct = mine.astype(jnp.float32)
        turned = dot(pt_ref[...], mine)
        tmp_ref[...] = jnp.where(ib > ia, direct, -turned)
        place(tmp_ref, 0)
        tmp_ref[...] = jnp.where(ib <= ia, direct, -dot(pt_ref[...], r_recv[0:5].reshape(HALF, OUT_ROWS)))
        place(tmp_ref, 2)

    def place_next():
        tmp_ref[...] = r_own[5:10].reshape(HALF, OUT_ROWS).astype(jnp.float32)
        place(tmp_ref, 1)

    def place_previous():
        tmp_ref[...] = -dot(pt_ref[...], r_recv[5:10].reshape(HALF, OUT_ROWS))
        place(tmp_ref, 3)

    def first_part(n, _):
        part_start(n)
        return 0

    lax.fori_loop(0, FULL, first_part, 0)
    lax.fori_loop(4, 8, make_vp, 0)

    def early(n, _):
        forward(n, 1)
        return 0

    def early_thin(n, _):
        forward_thin(n, 1)
        return 0

    def middle(n, _):
        forward(n, 2)
        return 0

    def middle_thin(n, _):
        forward_thin(n, 2)
        return 0

    def late(n, _):
        forward(n, 3)
        part_start(n + FIRST)
        return 0

    def late_thin(n, _):
        forward_thin(n, 3)
        return 0

    lax.fori_loop(0, FULL, early, 0)
    lax.fori_loop(FULL, FIRST, early_thin, 0)
    lax.fori_loop(0, FULL, middle, 0)
    lax.fori_loop(FULL, FIRST, middle_thin, 0)
    lax.fori_loop(0, FULL, late, 0)
    lax.fori_loop(FULL, FIRST, late_thin, 0)
    lax.fori_loop(FULL + FIRST, CHUNKS, first_part, 0)

    def events(t, place, passes):
        for at in passes:
            if (at, place) in EVENTS:

                @pl.when(t == at)
                def _():
                    for n, s in EVENTS[at, place]:
                        forward(n, s)

    def opening(t, _):
        events(t, 0, (0, 1))
        arrive(t)
        expand(t)
        to_core(t)
        events(t, 1, (0, 1))
        keep(t)

        @pl.when(t == 0)
        def _():
            for n in range(FULL, FIRST):
                end_thin(n)

        return 0

    def body(t, _):
        events(t, 0, range(2, CHUNKS))
        arrive(t)
        expand(t)
        to_core(t)
        events(t, 1, range(2, CHUNKS))
        core_arrive(t - 2)
        core_sum(t - 2)
        keep(t)
        lo_copy(t - 2).start()
        events(t, 2, range(2, CHUNKS))

        @pl.when(t >= 4)
        def _():
            finish(t - 4)

        return 0

    lax.fori_loop(0, 2, opening, 0)
    lax.fori_loop(2, CHUNKS, body, 0)

    def finish_some(n, _):
        finish(n)
        return 0

    def drain(n, _):
        hi_copy(n).wait_send()
        for one in first_copies(n, 0):
            one.wait_send()

        @pl.when(is_thin(n))
        def _():
            for s in range(1, 4):
                for one in thin_copies(n, s):
                    one.wait_send()
            for s in range(1, 5):
                for one in slot_copies(n, s):
                    one.wait_send()

        @pl.when(jnp.logical_not(is_thin(n)))
        def _():
            for one in first_copies(n, 1):
                one.wait_send()
            for s in range(1, 3):
                right_copy(n, s).wait_send()
                left_copy(n, s).wait_send()
            right_last(n).wait_send()
            left_last(n).wait_send()

        return 0

    def drain_sums(n, _):
        core_copy(n, 0).wait_send()
        core_copy(n, 1).wait_send()
        lo_copy(n).wait_send()
        return 0

    def drain_mirror(n, _):
        mirror_copy(n).wait_send()
        return 0

    def last_sums(n, _):
        core_arrive(n)
        core_sum(n)
        lo_copy(n).start()
        return 0

    lax.fori_loop(8, CHUNKS, last_sums, 0)
    lax.fori_loop(6, 9, finish_some, 0)
    lax.fori_loop(0, CHUNKS, drain, 0)
    lax.fori_loop(0, 5, mirror_wait, 0)
    place_opposite()
    finish(9)
    w0.wait_send()
    lax.fori_loop(0, CHUNKS, drain_sums, 0)
    place_next()
    lax.fori_loop(5, CHUNKS, mirror_wait, 0)
    place_previous()
    out_ref[...] = acc_ref[...].astype(jnp.bfloat16)
    lax.fori_loop(0, CHUNKS, drain_mirror, 0)


def local(integrals, amplitudes, ab_irrep, cd_irrep):
    vmem = pl.BlockSpec(memory_space=pltpu.VMEM)
    bf, f32 = jnp.bfloat16, jnp.float32
    dma = pltpu.SemaphoreType.DMA
    n = CHUNKS
    scratch = [
        pltpu.VMEM((ROWS_T, WIDE), bf),
        pltpu.VMEM((1024, DEPTH), bf),
        pltpu.VMEM((1024, DEPTH), bf),
        pltpu.VMEM((DEPTH, DEPTH), bf),
        pltpu.VMEM((HALF, HALF), bf),
        pltpu.VMEM((4, ROWS_T, HALF), bf),
        pltpu.VMEM((ROWS_T, HALF), f32),
        pltpu.VMEM((2, ROWS_T, HALF), bf),
        pltpu.VMEM((2, ROWS_T, HALF), bf),
        pltpu.VMEM((n, NZ, 2, ROWS_T, LANES), jnp.int16),
        pltpu.VMEM((DEPTH, LANES), f32),
        pltpu.VMEM((DEPTH, 2 * LANES), bf),
        pltpu.VMEM((n, 2, OUT_ROWS, LANES), f32),
        pltpu.VMEM((n, 2, OUT_ROWS, LANES), f32),
        pltpu.VMEM((n, OUT_ROWS, LANES), f32),
        pltpu.VMEM((n, OUT_ROWS + 16, LANES), jnp.int16),
        pltpu.VMEM((n, OUT_ROWS + 16, LANES), jnp.int16),
        pltpu.VMEM((n, OUT_ROWS, LANES), f32),
        pltpu.VMEM((n, LANES, OUT_ROWS), bf),
        pltpu.VMEM((n, LANES, OUT_ROWS), bf),
        pltpu.VMEM((HALF, OUT_ROWS), f32),
        pltpu.VMEM((OCC * SUB, OUT_ROWS), f32),
        dma,
        dma((2,)), dma((2,)),
        dma((n,)), dma((n,)),
        dma((THIN, 7)), dma((THIN, 7)),
        dma((n, 5)), dma((n, 5)),
        dma((n, 5)), dma((n, 5)),
        dma((n, 2)), dma((n, 2)),
        dma((n,)), dma((n,)),
        dma((n,)), dma((n,)),
    ]
    turned = pl.pallas_call(
        kernel,
        out_shape=jax.ShapeDtypeStruct((OCC * SUB, OUT_ROWS), bf),
        in_specs=[vmem, vmem, vmem, pl.BlockSpec(memory_space=pl.ANY)],
        out_specs=vmem,
        scratch_shapes=scratch,
        compiler_params=pltpu.CompilerParams(
            collective_id=0, has_side_effects=True, vmem_limit_bytes=58 * 2**20
        ),
        name="ladder",
    )(amplitudes, ab_irrep, cd_irrep, integrals)
    at = lax.broadcasted_iota(jnp.int32, turned.shape, 0)
    i = (at * 5243) >> 19
    same = at - OCC * i == i + SUB * lax.axis_index("col")
    return jnp.where(same, jnp.zeros_like(turned), turned).T


def solution(mesh):
    in_specs = (P("row", "depth"), P("depth", "row", "col"), P("row"), P("depth"))
    out_specs = P(("row", "depth"), "col")
    return jax.shard_map(local, mesh=mesh, in_specs=in_specs, out_specs=out_specs, check_vma=False)
```

```python
import numpy as np

import jax
import jax.numpy as jnp
from jax import lax
from jax.experimental import pallas as pl
from jax.experimental.pallas import tpu as pltpu
from jax.sharding import PartitionSpec as P

OCC = 100
SUB = 25
NZ = 8
LANES = 128
CHUNKS = 10
HALF = 640
PAD = 15
FIRST = 6
LAST = CHUNKS - FIRST
THIN = 3
FULL = FIRST - THIN
CUT = 48
ROWS_T = 80
DEPTH = 1280
OUT_ROWS = 256
WIDE = 2560
MESH = pl.DeviceIdType.MESH


def iota(shape, dim):
    return lax.broadcasted_iota(jnp.int32, shape, dim)


def div25(v):
    return (v * 5243) >> 17


def one_hot(cond):
    return jnp.where(cond, 1.0, 0.0).astype(jnp.bfloat16)


def dot(a, b):
    return jnp.dot(a, b, preferred_element_type=jnp.float32)


def band(n):
    lanes = np.arange(n * LANES, (n + 1) * LANES) - PAD
    lanes = lanes[(lanes >= 0) & (lanes < SUB * SUB)]
    first = 100 * (lanes // SUB) + lanes % SUB
    low = first.min() // LANES * LANES
    high = -(-(first.max() + 76) // LANES) * LANES
    return int(low), int(min(high, WIDE))


def kernel(
    amp_ref, ab_ref, cd_ref, v_hbm, out_ref,
    t_ref, v_ref, vp_ref, pk_ref, pt_ref, x_ref, diag_ref, wsend, wrecv, bq, sc_ref, bhl,
    csend, crecv, ysend, ycode, yrecv, own, r_own, r_recv, tmp_ref, acc_ref,
    v_sem, w_ss, w_rs, h_ss, h_rs, t_ss, t_rs, zr_ss, zr_rs, zl_ss, zl_rs, c_ss, c_rs, y_ss, y_rs, m_ss, m_rs,
):
    row, c, depth = lax.axis_index("row"), lax.axis_index("col"), lax.axis_index("depth")
    z, yh = row // 2, row % 2
    yl, core = depth // 2, depth % 2
    d_right = ((row + 2) % 16, c, depth)
    d_left = ((row + 14) % 16, c, depth)
    d_hi = (2 * z + 1 - yh, c, depth)
    d_core = (row, c, 2 * yl + 1 - core)
    d_lo = (row, c, 2 * (1 - yl) + core)
    x_next = (row, (c + 1) % 4, depth)
    x_opp = (row, (c + 2) % 4, depth)
    x_prev = (row, (c + 3) % 4, depth)

    def copy(src, dst, ss, rs, dev):
        return pltpu.make_async_remote_copy(
            src_ref=src, dst_ref=dst, send_sem=ss, recv_sem=rs, device_id=dev, device_id_type=MESH
        )

    v_copy = pltpu.make_async_copy(v_hbm, v_ref, v_sem)
    v_copy.start()

    barrier = pltpu.get_barrier_semaphore()
    for dev in (d_right, d_left, d_hi, d_core, d_lo, x_next, x_opp, x_prev):
        pl.semaphore_signal(barrier, inc=1, device_id=dev, device_id_type=MESH)

    t_ref[:, 2432:] = jnp.zeros((ROWS_T, LANES), jnp.bfloat16)
    t_ref[:, : OCC * SUB] = amp_ref[...].reshape(ROWS_T, OCC * SUB)

    u = iota((1, HALF), 1) - PAD
    a = div25(u)
    b = u - SUB * a
    flip = jnp.where(u >= 0, PAD + SUB * b + a, -1)
    lower = b <= a
    pt_ref[...] = one_hot(iota((HALF, HALF), 0) == flip)

    for n in range(HALF // LANES):
        low, high = band(n)
        u = iota((1, LANES), 1) + (n * LANES - PAD)
        a = div25(u)
        first = 100 * a + (u - SUB * a)
        r = iota((high - low, LANES), 0) + low
        mats = []
        for g in range(4):
            want = jnp.where((u >= 0), first + SUB * ((c + g) % 4), -1)
            mats.append(one_hot(r == want))
        got = dot(t_ref[:, low:high], jnp.concatenate(mats, axis=1)).astype(jnp.bfloat16)
        for g in range(4):
            x_ref[g, :, n * LANES:(n + 1) * LANES] = got[:, g * LANES:(g + 1) * LANES]

    wsend[1] = dot(x_ref[2], pt_ref[...]).astype(jnp.bfloat16)
    pl.semaphore_wait(barrier, 8)
    w0 = copy(wsend.at[0], wrecv.at[0], w_ss.at[0], w_rs.at[0], x_prev)
    w1 = copy(wsend.at[1], wrecv.at[1], w_ss.at[1], w_rs.at[1], x_opp)
    w1.start()
    wsend[0] = dot(x_ref[3], pt_ref[...]).astype(jnp.bfloat16)
    x0 = x_ref[0]
    diag_ref[...] = x0.astype(jnp.float32) - dot(x0, pt_ref[...])

    k = iota((1, DEPTH), 1)
    zz = (k * 3277) >> 19
    rem = k - 160 * zz
    hh = jnp.where(rem >= 80, 1, 0)
    m = rem - 80 * hh
    from_k = 32 * (m >> 1) + 4 * zz + 2 * hh + (m & 1)

    def make_pk(i, _):
        base = pl.multiple_of(i * 256, 256)
        pk_ref[pl.ds(base, 256), :] = one_hot(iota((256, DEPTH), 0) + base == from_k)
        return 0

    lax.fori_loop(0, DEPTH // 256, make_pk, 0)
    w1.wait_send()
    w0.start()
    v_copy.wait()

    def make_vp(i, _):
        to = 512 * jnp.where(i // 2 % 2 == core, 1, 0) + 256 * jnp.where(i // 4 == yl, 1, 0) + 128 * (i % 2)
        base = pl.multiple_of(i * 128, 128)
        rows = pl.ds(base, 128)
        label = jnp.broadcast_to(ab_ref[rows].reshape(1, 128), (128, 128)).T
        keep = jnp.concatenate([label] * 10, axis=1) == cd_ref[...].reshape(1, DEPTH)
        masked = jnp.where(keep, v_ref[rows, :].astype(jnp.float32), 0.0).astype(jnp.bfloat16)
        vp_ref[pl.ds(pl.multiple_of(to, 128), 128), :] = dot(masked, pk_ref[...]).astype(jnp.bfloat16)
        return 0

    lax.fori_loop(0, 2, make_vp, 0)

    def encode(values, chunk):
        biggest = jnp.max(jnp.abs(values), axis=1, keepdims=True)
        exponent = jnp.ceil(jnp.log2(jnp.maximum(biggest, 1e-30))) - 15.0
        q = jnp.clip(jnp.floor(values * jnp.exp2(-exponent) + 0.5), -32767.0, 32767.0)
        q = jnp.where(iota((ROWS_T, HALF), 1) < PAD, jnp.broadcast_to(exponent, (ROWS_T, HALF)), q)
        for n in range(5):
            part = q[:, n * LANES:(n + 1) * LANES]
            bq[chunk + n, z, yh] = part.astype(jnp.int32).astype(jnp.int16)

    def hi_copy(n):
        return copy(bq.at[n, z, yh], bq.at[n, z, yh], h_ss.at[n], h_rs.at[n], d_hi)

    def first_copies(n, side):
        at = yh if side == 0 else 1 - yh
        ref = bq.at[n, z, at]
        sem = 4 * side
        return (
            copy(ref, ref, zr_ss.at[n, sem], zr_rs.at[n, sem], d_right),
            copy(ref, ref, zl_ss.at[n, sem], zl_rs.at[n, sem], d_left),
        )

    def right_copy(n, s):
        at = (z - s + NZ) % NZ
        return copy(bq.at[n, at], bq.at[n, at], zr_ss.at[n, s], zr_rs.at[n, s], d_right)

    def left_copy(n, s):
        at = (z + s) % NZ
        return copy(bq.at[n, at], bq.at[n, at], zl_ss.at[n, s], zl_rs.at[n, s], d_left)

    def thin_copies(n, s):
        near, far = (z - s + NZ) % NZ, (z + s) % NZ
        right, left = bq.at[n, near, yh], bq.at[n, far, yh]
        if s == 3:
            right, left = right.at[pl.ds(0, CUT)], left.at[pl.ds(CUT, ROWS_T - CUT)]
        return (
            copy(right, right, zr_ss.at[n, s], zr_rs.at[n, s], d_right),
            copy(left, left, zl_ss.at[n, s], zl_rs.at[n, s], d_left),
        )

    def slot_copies(n, s):
        near, far = bq.at[n, (z - s + NZ) % NZ, yh], bq.at[n, (z + s) % NZ, yh]
        first = copy(near, near, t_ss.at[n - FULL, s - 1], t_rs.at[n - FULL, s - 1], d_hi)
        if s == 4:
            return (first,)
        return first, copy(far, far, t_ss.at[n - FULL, s + 3], t_rs.at[n - FULL, s + 3], d_hi)

    def right_last(n):
        at = (z - 3 + NZ) % NZ
        return copy(bq.at[n, at, 0], bq.at[n, at, 0], zr_ss.at[n, 3], zr_rs.at[n, 3], d_right)

    def left_last(n):
        at = (z + 3) % NZ
        return copy(bq.at[n, at, 1], bq.at[n, at, 1], zl_ss.at[n, 3], zl_rs.at[n, 3], d_left)

    def core_copy(n, h):
        return copy(csend.at[n, h], crecv.at[n, h], c_ss.at[n, h], c_rs.at[n, h], d_core)

    def lo_copy(n):
        return copy(ycode.at[n], yrecv.at[n], y_ss.at[n], y_rs.at[n], d_lo)

    def mirror_copy(n):
        to = (row, (c + 2 - n // 5) % 4, depth)
        return copy(r_own.at[n], r_recv.at[n], m_ss.at[n], m_rs.at[n], to)

    def start_both(pair):
        for one in pair:
            one.start()

    def own_start(n, _):
        hi_copy(n).start()
        start_both(first_copies(n, 0))
        return 0

    w1.wait_recv()
    opposite = x_ref[2].astype(jnp.float32) - wrecv[1].astype(jnp.float32)
    encode(jnp.where(lower, opposite, diag_ref[...]), 0)
    lax.fori_loop(0, 5, own_start, 0)
    make_vp(2, 0)
    w0.wait_recv()
    encode(x_ref[1].astype(jnp.float32) - wrecv[0].astype(jnp.float32), 5)
    lax.fori_loop(5, CHUNKS, own_start, 0)
    make_vp(3, 0)

    def part_start(n):
        hi_copy(n).wait_recv()
        start_both(first_copies(n, 1))

    def forward(n, s):
        before = [(right_copy(n, s - 1), left_copy(n, s - 1))] if s > 1 else [first_copies(n, 0), first_copies(n, 1)]
        after = (right_last(n), left_last(n)) if s == 3 else (right_copy(n, s), left_copy(n, s))
        for side in range(2):
            for pair in before:
                pair[side].wait_recv()
            after[side].start()

    def forward_thin(n, s):
        before = thin_copies(n, s - 1) if s > 1 else first_copies(n, 0)
        after = thin_copies(n, s)
        for side in range(2):
            before[side].wait_recv()
            after[side].start()
        start_both(slot_copies(n, s))

    def end_thin(n):
        for one in thin_copies(n, 3):
            one.wait_recv()
        start_both(slot_copies(n, 4))

    def is_thin(n):
        return (n >= FULL) & (n < FIRST)

    def arrive(n):
        @pl.when(is_thin(n))
        def _():
            hi_copy(n).wait_recv()
            for s in range(1, 5):
                for one in slot_copies(n, s):
                    one.wait_recv()

        @pl.when(jnp.logical_not(is_thin(n)))
        def _():
            right_last(n).wait_recv()
            left_last(n).wait_recv()

    def expand(n):
        q = bq[n].reshape(DEPTH, LANES).astype(jnp.int32)

        @pl.when((n == 0) | (n == 5))
        def _():
            sc_ref[...] = jnp.broadcast_to(jnp.exp2(q[:, 0:1].astype(jnp.float32)), (DEPTH, LANES))

        s = sc_ref[...]
        hi = (q + 128) >> 8
        lo = q - (hi << 8)
        bhl[:, :LANES] = (hi.astype(jnp.float32) * (s * 256.0)).astype(jnp.bfloat16)
        bhl[:, LANES:] = (lo.astype(jnp.float32) * s).astype(jnp.bfloat16)

    def multiply(n):
        both = dot(vp_ref[...], bhl[...])
        both = both[:, :LANES] + both[:, LANES:]
        csend[n] = both[:2 * OUT_ROWS].reshape(2, OUT_ROWS, LANES)
        core_copy(n, 0).start()
        core_copy(n, 1).start()
        ysend[n] = both[2 * OUT_ROWS:3 * OUT_ROWS]
        own[n] = both[3 * OUT_ROWS:]

    def core_arrive(n):
        core_copy(n, 0).wait_recv()
        core_copy(n, 1).wait_recv()

    def core_sum(n):
        part = ysend[n] + crecv[n, 0]
        biggest = jnp.max(jnp.abs(part), axis=0, keepdims=True)
        ex = jnp.ceil(jnp.log2(jnp.maximum(biggest, 1e-30))) - 15.0
        q = jnp.clip(jnp.floor(part * jnp.exp2(-ex) + 0.5), -32767.0, 32767.0)
        ycode[n, :OUT_ROWS] = q.astype(jnp.int32).astype(jnp.int16)
        ycode[n, OUT_ROWS:] = jnp.broadcast_to(ex, (16, LANES)).astype(jnp.int32).astype(jnp.int16)
        own[n] += crecv[n, 1]

    def finish(n):
        lo_copy(n).wait_recv()
        ex = yrecv[n, OUT_ROWS:].astype(jnp.int32).astype(jnp.float32)
        got = yrecv[n, :OUT_ROWS].astype(jnp.int32).astype(jnp.float32) * jnp.exp2(ex[0:1])
        r_own[n] = (own[n] + got).T.astype(jnp.bfloat16)
        mirror_copy(n).start()

    def place(block_ref, group):
        for q in range(4):

            @pl.when((c + group) % 4 == q)
            def _():
                for a in range(SUB):
                    at, to = PAD + SUB * a, OCC * a + SUB * q
                    acc_ref[to:to + SUB, :] = block_ref[at:at + SUB, :]

    def mirror_wait(n, _):
        mirror_copy(n).wait_recv()
        return 0

    def place_opposite():
        rows = iota((HALF, 1), 0) - PAD
        ia = div25(rows)
        ib = rows - SUB * ia
        mine = r_own[0:5].reshape(HALF, OUT_ROWS)
        direct = mine.astype(jnp.float32)
        turned = dot(pt_ref[...], mine)
        tmp_ref[...] = jnp.where(ib > ia, direct, jnp.where(ib < ia, -turned, 0.0))
        place(tmp_ref, 0)
        tmp_ref[...] = jnp.where(ib <= ia, direct, -dot(pt_ref[...], r_recv[0:5].reshape(HALF, OUT_ROWS)))
        place(tmp_ref, 2)

    def place_next():
        tmp_ref[...] = r_own[5:10].reshape(HALF, OUT_ROWS).astype(jnp.float32)
        place(tmp_ref, 1)

    def place_previous():
        tmp_ref[...] = -dot(pt_ref[...], r_recv[5:10].reshape(HALF, OUT_ROWS))
        place(tmp_ref, 3)

    def first_part(n, _):
        part_start(n)
        return 0

    lax.fori_loop(0, FULL, first_part, 0)
    lax.fori_loop(4, 8, make_vp, 0)

    def early(n, _):
        forward(n, 1)
        return 0

    def early_thin(n, _):
        forward_thin(n, 1)
        return 0

    def middle(n, _):
        forward(n, 2)
        return 0

    def middle_thin(n, _):
        forward_thin(n, 2)
        return 0

    def late(n, _):
        forward(n, 3)
        part_start(n + FIRST)
        return 0

    def late_thin(n, _):
        forward_thin(n, 3)
        return 0

    lax.fori_loop(0, FULL, early, 0)
    lax.fori_loop(FULL, FIRST, early_thin, 0)
    lax.fori_loop(0, FULL, middle, 0)
    lax.fori_loop(FULL, FIRST, middle_thin, 0)
    lax.fori_loop(0, FULL, late, 0)
    lax.fori_loop(FULL, FIRST, late_thin, 0)
    part_start(CHUNKS - 1)

    def event(i):
        n = FIRST + i % LAST
        for s in range(1, 4):

            @pl.when(i // LAST == s - 1)
            def _():
                forward(n, s)

    def opening(t, _):
        event(2 * t)
        arrive(t)
        expand(t)
        multiply(t)
        event(2 * t + 1)

        @pl.when(t == 0)
        def _():
            for n in range(FULL, FIRST):
                end_thin(n)

        return 0

    def body(t, _):
        @pl.when(t < FIRST)
        def _():
            event(2 * t)

        arrive(t)
        expand(t)
        multiply(t)

        @pl.when(t < FIRST)
        def _():
            event(2 * t + 1)

        core_arrive(t - 2)
        core_sum(t - 2)
        lo_copy(t - 2).start()

        @pl.when(t >= 4)
        def _():
            finish(t - 4)

        return 0

    lax.fori_loop(0, 2, opening, 0)
    lax.fori_loop(2, CHUNKS, body, 0)

    def finish_some(n, _):
        finish(n)
        return 0

    def drain(n, _):
        hi_copy(n).wait_send()
        for one in first_copies(n, 0):
            one.wait_send()

        @pl.when(is_thin(n))
        def _():
            for s in range(1, 4):
                for one in thin_copies(n, s):
                    one.wait_send()
            for s in range(1, 5):
                for one in slot_copies(n, s):
                    one.wait_send()

        @pl.when(jnp.logical_not(is_thin(n)))
        def _():
            for one in first_copies(n, 1):
                one.wait_send()
            for s in range(1, 3):
                right_copy(n, s).wait_send()
                left_copy(n, s).wait_send()
            right_last(n).wait_send()
            left_last(n).wait_send()

        return 0

    def drain_sums(n, _):
        core_copy(n, 0).wait_send()
        core_copy(n, 1).wait_send()
        lo_copy(n).wait_send()
        return 0

    def drain_mirror(n, _):
        mirror_copy(n).wait_send()
        return 0

    def last_sums(n, _):
        core_arrive(n)
        core_sum(n)
        lo_copy(n).start()
        return 0

    lax.fori_loop(8, CHUNKS, last_sums, 0)
    lax.fori_loop(6, 9, finish_some, 0)
    lax.fori_loop(0, CHUNKS, drain, 0)
    lax.fori_loop(0, 5, mirror_wait, 0)
    place_opposite()
    finish(9)
    w0.wait_send()
    lax.fori_loop(0, CHUNKS, drain_sums, 0)
    place_next()
    lax.fori_loop(5, CHUNKS, mirror_wait, 0)
    place_previous()
    out_ref[...] = acc_ref[...].astype(jnp.bfloat16)
    lax.fori_loop(0, CHUNKS, drain_mirror, 0)


def local(integrals, amplitudes, ab_irrep, cd_irrep):
    vmem = pl.BlockSpec(memory_space=pltpu.VMEM)
    bf, f32 = jnp.bfloat16, jnp.float32
    dma = pltpu.SemaphoreType.DMA
    n = CHUNKS
    scratch = [
        pltpu.VMEM((ROWS_T, WIDE), bf),
        pltpu.VMEM((1024, DEPTH), bf),
        pltpu.VMEM((1024, DEPTH), bf),
        pltpu.VMEM((DEPTH, DEPTH), bf),
        pltpu.VMEM((HALF, HALF), bf),
        pltpu.VMEM((4, ROWS_T, HALF), bf),
        pltpu.VMEM((ROWS_T, HALF), f32),
        pltpu.VMEM((2, ROWS_T, HALF), bf),
        pltpu.VMEM((2, ROWS_T, HALF), bf),
        pltpu.VMEM((n, NZ, 2, ROWS_T, LANES), jnp.int16),
        pltpu.VMEM((DEPTH, LANES), f32),
        pltpu.VMEM((DEPTH, 2 * LANES), bf),
        pltpu.VMEM((n, 2, OUT_ROWS, LANES), f32),
        pltpu.VMEM((n, 2, OUT_ROWS, LANES), f32),
        pltpu.VMEM((n, OUT_ROWS, LANES), f32),
        pltpu.VMEM((n, OUT_ROWS + 16, LANES), jnp.int16),
        pltpu.VMEM((n, OUT_ROWS + 16, LANES), jnp.int16),
        pltpu.VMEM((n, OUT_ROWS, LANES), f32),
        pltpu.VMEM((n, LANES, OUT_ROWS), bf),
        pltpu.VMEM((n, LANES, OUT_ROWS), bf),
        pltpu.VMEM((HALF, OUT_ROWS), f32),
        pltpu.VMEM((OCC * SUB, OUT_ROWS), f32),
        dma,
        dma((2,)), dma((2,)),
        dma((n,)), dma((n,)),
        dma((THIN, 7)), dma((THIN, 7)),
        dma((n, 5)), dma((n, 5)),
        dma((n, 5)), dma((n, 5)),
        dma((n, 2)), dma((n, 2)),
        dma((n,)), dma((n,)),
        dma((n,)), dma((n,)),
    ]
    turned = pl.pallas_call(
        kernel,
        out_shape=jax.ShapeDtypeStruct((OCC * SUB, OUT_ROWS), bf),
        in_specs=[vmem, vmem, vmem, pl.BlockSpec(memory_space=pl.ANY)],
        out_specs=vmem,
        scratch_shapes=scratch,
        compiler_params=pltpu.CompilerParams(
            collective_id=0, has_side_effects=True, vmem_limit_bytes=58 * 2**20
        ),
        name="ladder",
    )(amplitudes, ab_irrep, cd_irrep, integrals)
    return turned.T


def solution(mesh):
    in_specs = (P("row", "depth"), P("depth", "row", "col"), P("row"), P("depth"))
    out_specs = P(("row", "depth"), "col")
    return jax.shard_map(local, mesh=mesh, in_specs=in_specs, out_specs=out_specs, check_vma=False)
```

```python
import numpy as np

import jax
import jax.numpy as jnp
from jax import lax
from jax.experimental import pallas as pl
from jax.experimental.pallas import tpu as pltpu
from jax.sharding import PartitionSpec as P

OCC = 100
SUB = 25
NZ = 8
LANES = 128
CHUNKS = 10
HALF = 640
PAD = 15
FIRST = 6
LAST = CHUNKS - FIRST
THIN = 3
FULL = FIRST - THIN
CUT = 48
ROWS_T = 80
DEPTH = 1280
OUT_ROWS = 256
WIDE = 2560
MESH = pl.DeviceIdType.MESH


def iota(shape, dim):
    return lax.broadcasted_iota(jnp.int32, shape, dim)


def div25(v):
    return (v * 5243) >> 17


def one_hot(cond):
    return jnp.where(cond, 1.0, 0.0).astype(jnp.bfloat16)


def dot(a, b):
    return jnp.dot(a, b, preferred_element_type=jnp.float32)


def band(n):
    lanes = np.arange(n * LANES, (n + 1) * LANES) - PAD
    lanes = lanes[(lanes >= 0) & (lanes < SUB * SUB)]
    first = 100 * (lanes // SUB) + lanes % SUB
    low = first.min() // LANES * LANES
    high = -(-(first.max() + 76) // LANES) * LANES
    return int(low), int(min(high, WIDE))


def kernel(
    amp_hbm, ab_ref, cd_ref, v_hbm, out_ref,
    amp_ref, t_ref, v_ref, vp_ref, pk_ref, pt_ref, x_ref, diag_ref, wsend, wrecv, bq, sc_ref, bhl,
    csend, crecv, ysend, ycode, yrecv, own, r_own, r_recv, tmp_ref, acc_ref,
    a_sem, v_sem, w_ss, w_rs, h_ss, h_rs, t_ss, t_rs, zr_ss, zr_rs, zl_ss, zl_rs, c_ss, c_rs, y_ss, y_rs, m_ss, m_rs,
):
    row, c, depth = lax.axis_index("row"), lax.axis_index("col"), lax.axis_index("depth")
    z, yh = row // 2, row % 2
    yl, core = depth // 2, depth % 2
    d_right = ((row + 2) % 16, c, depth)
    d_left = ((row + 14) % 16, c, depth)
    d_hi = (2 * z + 1 - yh, c, depth)
    d_core = (row, c, 2 * yl + 1 - core)
    d_lo = (row, c, 2 * (1 - yl) + core)
    x_next = (row, (c + 1) % 4, depth)
    x_opp = (row, (c + 2) % 4, depth)
    x_prev = (row, (c + 3) % 4, depth)

    def copy(src, dst, ss, rs, dev):
        return pltpu.make_async_remote_copy(
            src_ref=src, dst_ref=dst, send_sem=ss, recv_sem=rs, device_id=dev, device_id_type=MESH
        )

    a_copy = pltpu.make_async_copy(amp_hbm, amp_ref, a_sem)
    a_copy.start()

    barrier = pltpu.get_barrier_semaphore()
    for dev in (d_right, d_left, d_hi, d_core, d_lo, x_next, x_opp, x_prev):
        pl.semaphore_signal(barrier, inc=1, device_id=dev, device_id_type=MESH)

    u = iota((1, HALF), 1) - PAD
    a = div25(u)
    b = u - SUB * a
    flip = jnp.where(u >= 0, PAD + SUB * b + a, -1)
    lower = b <= a
    pt_ref[...] = one_hot(iota((HALF, HALF), 0) == flip)

    a_copy.wait()
    v_copy = pltpu.make_async_copy(v_hbm, v_ref, v_sem)
    v_copy.start()
    t_ref[:, 2432:] = jnp.zeros((ROWS_T, LANES), jnp.bfloat16)
    t_ref[:, : OCC * SUB] = amp_ref[...].reshape(ROWS_T, OCC * SUB)

    for n in range(HALF // LANES):
        low, high = band(n)
        u = iota((1, LANES), 1) + (n * LANES - PAD)
        a = div25(u)
        first = 100 * a + (u - SUB * a)
        r = iota((high - low, LANES), 0) + low
        mats = []
        for g in range(4):
            want = jnp.where((u >= 0), first + SUB * ((c + g) % 4), -1)
            mats.append(one_hot(r == want))
        got = dot(t_ref[:, low:high], jnp.concatenate(mats, axis=1)).astype(jnp.bfloat16)
        for g in range(4):
            x_ref[g, :, n * LANES:(n + 1) * LANES] = got[:, g * LANES:(g + 1) * LANES]

    wsend[1] = dot(x_ref[2], pt_ref[...]).astype(jnp.bfloat16)
    wsend[0] = dot(x_ref[3], pt_ref[...]).astype(jnp.bfloat16)
    pl.semaphore_wait(barrier, 8)
    w0 = copy(wsend.at[0], wrecv.at[0], w_ss.at[0], w_rs.at[0], x_prev)
    w1 = copy(wsend.at[1], wrecv.at[1], w_ss.at[1], w_rs.at[1], x_opp)
    w1.start()
    w0.start()
    x0 = x_ref[0]
    diag_ref[...] = x0.astype(jnp.float32) - dot(x0, pt_ref[...])

    k = iota((1, DEPTH), 1)
    zz = (k * 3277) >> 19
    rem = k - 160 * zz
    hh = jnp.where(rem >= 80, 1, 0)
    m = rem - 80 * hh
    from_k = 32 * (m >> 1) + 4 * zz + 2 * hh + (m & 1)

    def make_pk(i, _):
        base = pl.multiple_of(i * 256, 256)
        pk_ref[pl.ds(base, 256), :] = one_hot(iota((256, DEPTH), 0) + base == from_k)
        return 0

    lax.fori_loop(0, DEPTH // 256, make_pk, 0)
    v_copy.wait()

    def make_vp(i, _):
        to = 512 * jnp.where(i // 2 % 2 == core, 1, 0) + 256 * jnp.where(i // 4 == yl, 1, 0) + 128 * (i % 2)
        base = pl.multiple_of(i * 128, 128)
        rows = pl.ds(base, 128)
        label = jnp.broadcast_to(ab_ref[rows].reshape(1, 128), (128, 128)).T
        keep = jnp.concatenate([label] * 10, axis=1) == cd_ref[...].reshape(1, DEPTH)
        masked = jnp.where(keep, v_ref[rows, :].astype(jnp.float32), 0.0).astype(jnp.bfloat16)
        vp_ref[pl.ds(pl.multiple_of(to, 128), 128), :] = dot(masked, pk_ref[...]).astype(jnp.bfloat16)
        return 0


    def encode(values, chunk):
        biggest = jnp.max(jnp.abs(values), axis=1, keepdims=True)
        exponent = jnp.ceil(jnp.log2(jnp.maximum(biggest, 1e-30))) - 15.0
        q = jnp.clip(jnp.floor(values * jnp.exp2(-exponent) + 0.5), -32767.0, 32767.0)
        q = jnp.where(iota((ROWS_T, HALF), 1) < PAD, jnp.broadcast_to(exponent, (ROWS_T, HALF)), q)
        for n in range(5):
            part = q[:, n * LANES:(n + 1) * LANES]
            bq[chunk + n, z, yh] = part.astype(jnp.int32).astype(jnp.int16)

    def hi_copy(n):
        return copy(bq.at[n, z, yh], bq.at[n, z, yh], h_ss.at[n], h_rs.at[n], d_hi)

    def first_copies(n, side):
        at = yh if side == 0 else 1 - yh
        ref = bq.at[n, z, at]
        sem = 4 * side
        return (
            copy(ref, ref, zr_ss.at[n, sem], zr_rs.at[n, sem], d_right),
            copy(ref, ref, zl_ss.at[n, sem], zl_rs.at[n, sem], d_left),
        )

    def right_copy(n, s):
        at = (z - s + NZ) % NZ
        return copy(bq.at[n, at], bq.at[n, at], zr_ss.at[n, s], zr_rs.at[n, s], d_right)

    def left_copy(n, s):
        at = (z + s) % NZ
        return copy(bq.at[n, at], bq.at[n, at], zl_ss.at[n, s], zl_rs.at[n, s], d_left)

    def thin_copies(n, s):
        near, far = (z - s + NZ) % NZ, (z + s) % NZ
        right, left = bq.at[n, near, yh], bq.at[n, far, yh]
        if s == 3:
            right, left = right.at[pl.ds(0, CUT)], left.at[pl.ds(CUT, ROWS_T - CUT)]
        return (
            copy(right, right, zr_ss.at[n, s], zr_rs.at[n, s], d_right),
            copy(left, left, zl_ss.at[n, s], zl_rs.at[n, s], d_left),
        )

    def slot_copies(n, s):
        near, far = bq.at[n, (z - s + NZ) % NZ, yh], bq.at[n, (z + s) % NZ, yh]
        first = copy(near, near, t_ss.at[n - FULL, s - 1], t_rs.at[n - FULL, s - 1], d_hi)
        if s == 4:
            return (first,)
        return first, copy(far, far, t_ss.at[n - FULL, s + 3], t_rs.at[n - FULL, s + 3], d_hi)

    def right_last(n):
        at = (z - 3 + NZ) % NZ
        return copy(bq.at[n, at, 0], bq.at[n, at, 0], zr_ss.at[n, 3], zr_rs.at[n, 3], d_right)

    def left_last(n):
        at = (z + 3) % NZ
        return copy(bq.at[n, at, 1], bq.at[n, at, 1], zl_ss.at[n, 3], zl_rs.at[n, 3], d_left)

    def core_copy(n, h):
        return copy(csend.at[n, h], crecv.at[n, h], c_ss.at[n, h], c_rs.at[n, h], d_core)

    def lo_copy(n):
        return copy(ycode.at[n], yrecv.at[n], y_ss.at[n], y_rs.at[n], d_lo)

    def mirror_copy(n):
        to = (row, (c + 2 - n // 5) % 4, depth)
        return copy(r_own.at[n], r_recv.at[n], m_ss.at[n], m_rs.at[n], to)

    def start_both(pair):
        for one in pair:
            one.start()

    def own_start(n, _):
        hi_copy(n).start()
        start_both(first_copies(n, 0))
        return 0

    w1.wait_recv()
    opposite = x_ref[2].astype(jnp.float32) - wrecv[1].astype(jnp.float32)
    encode(jnp.where(lower, opposite, diag_ref[...]), 0)
    lax.fori_loop(0, 5, own_start, 0)
    lax.fori_loop(0, 3, make_vp, 0)
    w0.wait_recv()
    encode(x_ref[1].astype(jnp.float32) - wrecv[0].astype(jnp.float32), 5)
    lax.fori_loop(5, CHUNKS, own_start, 0)
    make_vp(3, 0)

    def part_start(n):
        hi_copy(n).wait_recv()
        start_both(first_copies(n, 1))

    def forward(n, s):
        before = [(right_copy(n, s - 1), left_copy(n, s - 1))] if s > 1 else [first_copies(n, 0), first_copies(n, 1)]
        after = (right_last(n), left_last(n)) if s == 3 else (right_copy(n, s), left_copy(n, s))
        for side in range(2):
            for pair in before:
                pair[side].wait_recv()
            after[side].start()

    def forward_thin(n, s):
        before = thin_copies(n, s - 1) if s > 1 else first_copies(n, 0)
        after = thin_copies(n, s)
        for side in range(2):
            before[side].wait_recv()
            after[side].start()
        start_both(slot_copies(n, s))

    def end_thin(n):
        for one in thin_copies(n, 3):
            one.wait_recv()
        start_both(slot_copies(n, 4))

    def is_thin(n):
        return (n >= FULL) & (n < FIRST)

    def arrive(n):
        @pl.when(is_thin(n))
        def _():
            hi_copy(n).wait_recv()
            for s in range(1, 5):
                for one in slot_copies(n, s):
                    one.wait_recv()

        @pl.when(jnp.logical_not(is_thin(n)))
        def _():
            right_last(n).wait_recv()
            left_last(n).wait_recv()

    def expand(n):
        q = bq[n].reshape(DEPTH, LANES).astype(jnp.int32)

        @pl.when((n == 0) | (n == 5))
        def _():
            sc_ref[...] = jnp.broadcast_to(jnp.exp2(q[:, 0:1].astype(jnp.float32)), (DEPTH, LANES))

        s = sc_ref[...]
        hi = (q + 128) >> 8
        lo = q - (hi << 8)
        bhl[:, :LANES] = (hi.astype(jnp.float32) * (s * 256.0)).astype(jnp.bfloat16)
        bhl[:, LANES:] = (lo.astype(jnp.float32) * s).astype(jnp.bfloat16)

    def multiply(n):
        both = dot(vp_ref[...], bhl[...])
        both = both[:, :LANES] + both[:, LANES:]
        csend[n] = both[:2 * OUT_ROWS].reshape(2, OUT_ROWS, LANES)
        core_copy(n, 0).start()
        core_copy(n, 1).start()
        ysend[n] = both[2 * OUT_ROWS:3 * OUT_ROWS]
        own[n] = both[3 * OUT_ROWS:]

    def core_arrive(n):
        core_copy(n, 0).wait_recv()
        core_copy(n, 1).wait_recv()

    def core_sum(n):
        part = ysend[n] + crecv[n, 0]
        biggest = jnp.max(jnp.abs(part), axis=0, keepdims=True)
        ex = jnp.ceil(jnp.log2(jnp.maximum(biggest, 1e-30))) - 15.0
        q = jnp.clip(jnp.floor(part * jnp.exp2(-ex) + 0.5), -32767.0, 32767.0)
        ycode[n, :OUT_ROWS] = q.astype(jnp.int32).astype(jnp.int16)
        ycode[n, OUT_ROWS:] = jnp.broadcast_to(ex, (16, LANES)).astype(jnp.int32).astype(jnp.int16)
        own[n] += crecv[n, 1]

    def finish(n):
        lo_copy(n).wait_recv()
        ex = yrecv[n, OUT_ROWS:].astype(jnp.int32).astype(jnp.float32)
        got = yrecv[n, :OUT_ROWS].astype(jnp.int32).astype(jnp.float32) * jnp.exp2(ex[0:1])
        r_own[n] = (own[n] + got).T.astype(jnp.bfloat16)
        mirror_copy(n).start()

    def place(block_ref, group):
        for q in range(4):

            @pl.when((c + group) % 4 == q)
            def _():
                for a in range(SUB):
                    at, to = PAD + SUB * a, OCC * a + SUB * q
                    acc_ref[to:to + SUB, :] = block_ref[at:at + SUB, :]

    def mirror_wait(n, _):
        mirror_copy(n).wait_recv()
        return 0

    def place_opposite():
        rows = iota((HALF, 1), 0) - PAD
        ia = div25(rows)
        ib = rows - SUB * ia
        mine = r_own[0:5].reshape(HALF, OUT_ROWS)
        direct = mine.astype(jnp.float32)
        turned = dot(pt_ref[...], mine)
        tmp_ref[...] = jnp.where(ib > ia, direct, jnp.where(ib < ia, -turned, 0.0))
        place(tmp_ref, 0)
        tmp_ref[...] = jnp.where(ib <= ia, direct, -dot(pt_ref[...], r_recv[0:5].reshape(HALF, OUT_ROWS)))
        place(tmp_ref, 2)

    def place_next():
        tmp_ref[...] = r_own[5:10].reshape(HALF, OUT_ROWS).astype(jnp.float32)
        place(tmp_ref, 1)

    def place_previous():
        tmp_ref[...] = -dot(pt_ref[...], r_recv[5:10].reshape(HALF, OUT_ROWS))
        place(tmp_ref, 3)

    def first_part(n, _):
        part_start(n)
        return 0

    lax.fori_loop(0, FULL, first_part, 0)
    lax.fori_loop(4, 8, make_vp, 0)

    def early(n, _):
        forward(n, 1)
        return 0

    def early_thin(n, _):
        forward_thin(n, 1)
        return 0

    def middle(n, _):
        forward(n, 2)
        return 0

    def middle_thin(n, _):
        forward_thin(n, 2)
        return 0

    def late(n, _):
        forward(n, 3)
        part_start(n + FIRST)
        return 0

    def late_thin(n, _):
        forward_thin(n, 3)
        return 0

    lax.fori_loop(0, FULL, early, 0)
    lax.fori_loop(FULL, FIRST, early_thin, 0)
    lax.fori_loop(0, FULL, middle, 0)
    lax.fori_loop(FULL, FIRST, middle_thin, 0)
    lax.fori_loop(0, FULL, late, 0)
    lax.fori_loop(FULL, FIRST, late_thin, 0)
    part_start(CHUNKS - 1)

    def event(i):
        n = FIRST + i % LAST
        for s in range(1, 4):

            @pl.when(i // LAST == s - 1)
            def _():
                forward(n, s)

    def opening(t, _):
        event(2 * t)
        arrive(t)
        expand(t)
        multiply(t)
        event(2 * t + 1)

        @pl.when(t == 0)
        def _():
            for n in range(FULL, FIRST):
                end_thin(n)

        return 0

    def body(t, _):
        @pl.when(t < FIRST)
        def _():
            event(2 * t)

        arrive(t)
        expand(t)
        multiply(t)

        @pl.when(t < FIRST)
        def _():
            event(2 * t + 1)

        core_arrive(t - 2)
        core_sum(t - 2)
        lo_copy(t - 2).start()

        @pl.when(t >= 5)
        def _():
            finish(t - 5)

        return 0

    lax.fori_loop(0, 2, opening, 0)
    lax.fori_loop(2, CHUNKS, body, 0)

    def finish_some(n, _):
        finish(n)
        return 0

    def drain(n, _):
        hi_copy(n).wait_send()
        for one in first_copies(n, 0):
            one.wait_send()

        @pl.when(is_thin(n))
        def _():
            for s in range(1, 4):
                for one in thin_copies(n, s):
                    one.wait_send()
            for s in range(1, 5):
                for one in slot_copies(n, s):
                    one.wait_send()

        @pl.when(jnp.logical_not(is_thin(n)))
        def _():
            for one in first_copies(n, 1):
                one.wait_send()
            for s in range(1, 3):
                right_copy(n, s).wait_send()
                left_copy(n, s).wait_send()
            right_last(n).wait_send()
            left_last(n).wait_send()

        return 0

    def drain_sums(n, _):
        core_copy(n, 0).wait_send()
        core_copy(n, 1).wait_send()
        lo_copy(n).wait_send()
        return 0

    def drain_mirror(n, _):
        mirror_copy(n).wait_send()
        return 0

    def last_sums(n, _):
        core_arrive(n)
        core_sum(n)
        lo_copy(n).start()
        return 0

    lax.fori_loop(8, CHUNKS, last_sums, 0)
    lax.fori_loop(5, 9, finish_some, 0)
    lax.fori_loop(0, CHUNKS, drain, 0)
    lax.fori_loop(0, 5, mirror_wait, 0)
    place_opposite()
    finish(9)
    w0.wait_send()
    w1.wait_send()
    lax.fori_loop(0, CHUNKS, drain_sums, 0)
    place_next()
    lax.fori_loop(5, CHUNKS, mirror_wait, 0)
    place_previous()
    out_ref[...] = acc_ref[...].astype(jnp.bfloat16)
    lax.fori_loop(0, CHUNKS, drain_mirror, 0)


def local(integrals, amplitudes, ab_irrep, cd_irrep):
    vmem = pl.BlockSpec(memory_space=pltpu.VMEM)
    bf, f32 = jnp.bfloat16, jnp.float32
    dma = pltpu.SemaphoreType.DMA
    n = CHUNKS
    scratch = [
        pltpu.VMEM((40, 2, OCC * SUB), bf),
        pltpu.VMEM((ROWS_T, WIDE), bf),
        pltpu.VMEM((1024, DEPTH), bf),
        pltpu.VMEM((1024, DEPTH), bf),
        pltpu.VMEM((DEPTH, DEPTH), bf),
        pltpu.VMEM((HALF, HALF), bf),
        pltpu.VMEM((4, ROWS_T, HALF), bf),
        pltpu.VMEM((ROWS_T, HALF), f32),
        pltpu.VMEM((2, ROWS_T, HALF), bf),
        pltpu.VMEM((2, ROWS_T, HALF), bf),
        pltpu.VMEM((n, NZ, 2, ROWS_T, LANES), jnp.int16),
        pltpu.VMEM((DEPTH, LANES), f32),
        pltpu.VMEM((DEPTH, 2 * LANES), bf),
        pltpu.VMEM((n, 2, OUT_ROWS, LANES), f32),
        pltpu.VMEM((n, 2, OUT_ROWS, LANES), f32),
        pltpu.VMEM((n, OUT_ROWS, LANES), f32),
        pltpu.VMEM((n, OUT_ROWS + 16, LANES), jnp.int16),
        pltpu.VMEM((n, OUT_ROWS + 16, LANES), jnp.int16),
        pltpu.VMEM((n, OUT_ROWS, LANES), f32),
        pltpu.VMEM((n, LANES, OUT_ROWS), bf),
        pltpu.VMEM((n, LANES, OUT_ROWS), bf),
        pltpu.VMEM((HALF, OUT_ROWS), f32),
        pltpu.VMEM((OCC * SUB, OUT_ROWS), f32),
        dma,
        dma,
        dma((2,)), dma((2,)),
        dma((n,)), dma((n,)),
        dma((THIN, 7)), dma((THIN, 7)),
        dma((n, 5)), dma((n, 5)),
        dma((n, 5)), dma((n, 5)),
        dma((n, 2)), dma((n, 2)),
        dma((n,)), dma((n,)),
        dma((n,)), dma((n,)),
    ]
    turned = pl.pallas_call(
        kernel,
        out_shape=jax.ShapeDtypeStruct((OCC * SUB, OUT_ROWS), bf),
        in_specs=[pl.BlockSpec(memory_space=pl.ANY), vmem, vmem, pl.BlockSpec(memory_space=pl.ANY)],
        out_specs=vmem,
        scratch_shapes=scratch,
        compiler_params=pltpu.CompilerParams(
            collective_id=0, has_side_effects=True, vmem_limit_bytes=58 * 2**20
        ),
        name="ladder",
    )(amplitudes, ab_irrep, cd_irrep, integrals)
    return turned.T


def solution(mesh):
    in_specs = (P("row", "depth"), P("depth", "row", "col"), P("row"), P("depth"))
    out_specs = P(("row", "depth"), "col")
    return jax.shard_map(local, mesh=mesh, in_specs=in_specs, out_specs=out_specs, check_vma=False)
```

```python
import numpy as np

import jax
import jax.numpy as jnp
from jax import lax
from jax.experimental import pallas as pl
from jax.experimental.pallas import tpu as pltpu
from jax.sharding import PartitionSpec as P

OCC = 100
SUB = 25
NZ = 8
LANES = 128
CHUNKS = 10
HALF = 640
PAD = 15
FIRST = 6
LAST = CHUNKS - FIRST
THIN = 3
FULL = FIRST - THIN
CUT = 48
ROWS_T = 80
DEPTH = 1280
OUT_ROWS = 256
WIDE = 2560
MESH = pl.DeviceIdType.MESH


def iota(shape, dim):
    return lax.broadcasted_iota(jnp.int32, shape, dim)


def div25(v):
    return (v * 5243) >> 17


def one_hot(cond):
    return jnp.where(cond, 1.0, 0.0).astype(jnp.bfloat16)


def dot(a, b):
    return jnp.dot(a, b, preferred_element_type=jnp.float32)


def band(n):
    lanes = np.arange(n * LANES, (n + 1) * LANES) - PAD
    lanes = lanes[(lanes >= 0) & (lanes < SUB * SUB)]
    first = 100 * (lanes // SUB) + lanes % SUB
    low = first.min() // LANES * LANES
    high = -(-(first.max() + 76) // LANES) * LANES
    return int(low), int(min(high, WIDE))


def kernel(
    amp_ref, ab_ref, cd_ref, v_hbm, out_ref,
    t_ref, v_ref, vp_ref, pk_ref, pt_ref, x_ref, diag_ref, wsend, wrecv, bq, sc_ref, bhl,
    csend, crecv, ysend, ycode, yrecv, own, r_own, r_recv, tmp_ref, acc_ref,
    v_sem, w_ss, w_rs, h_ss, h_rs, t_ss, t_rs, zr_ss, zr_rs, zl_ss, zl_rs, c_ss, c_rs, y_ss, y_rs, m_ss, m_rs,
):
    row, c, depth = lax.axis_index("row"), lax.axis_index("col"), lax.axis_index("depth")
    z, yh = row // 2, row % 2
    yl, core = depth // 2, depth % 2
    d_right = ((row + 2) % 16, c, depth)
    d_left = ((row + 14) % 16, c, depth)
    d_hi = (2 * z + 1 - yh, c, depth)
    d_core = (row, c, 2 * yl + 1 - core)
    d_lo = (row, c, 2 * (1 - yl) + core)
    x_next = (row, (c + 1) % 4, depth)
    x_opp = (row, (c + 2) % 4, depth)
    x_prev = (row, (c + 3) % 4, depth)

    def copy(src, dst, ss, rs, dev):
        return pltpu.make_async_remote_copy(
            src_ref=src, dst_ref=dst, send_sem=ss, recv_sem=rs, device_id=dev, device_id_type=MESH
        )

    v_copy = pltpu.make_async_copy(v_hbm, v_ref, v_sem)
    v_copy.start()

    barrier = pltpu.get_barrier_semaphore()
    for dev in (d_right, d_left, d_hi, d_core, d_lo, x_next, x_opp, x_prev):
        pl.semaphore_signal(barrier, inc=1, device_id=dev, device_id_type=MESH)

    t_ref[:, 2432:] = jnp.zeros((ROWS_T, LANES), jnp.bfloat16)
    t_ref[:, : OCC * SUB] = amp_ref[...].reshape(ROWS_T, OCC * SUB)

    u = iota((1, HALF), 1) - PAD
    a = div25(u)
    b = u - SUB * a
    flip = jnp.where(u >= 0, PAD + SUB * b + a, -1)
    lower = b <= a
    pt_ref[...] = one_hot(iota((HALF, HALF), 0) == flip)

    for n in range(HALF // LANES):
        low, high = band(n)
        u = iota((1, LANES), 1) + (n * LANES - PAD)
        a = div25(u)
        first = 100 * a + (u - SUB * a)
        r = iota((high - low, LANES), 0) + low
        mats = []
        for g in range(4):
            want = jnp.where((u >= 0), first + SUB * ((c + g) % 4), -1)
            mats.append(one_hot(r == want))
        got = dot(t_ref[:, low:high], jnp.concatenate(mats, axis=1)).astype(jnp.bfloat16)
        for g in range(4):
            x_ref[g, :, n * LANES:(n + 1) * LANES] = got[:, g * LANES:(g + 1) * LANES]

    wsend[1] = dot(x_ref[2], pt_ref[...]).astype(jnp.bfloat16)
    pl.semaphore_wait(barrier, 8)
    w0 = copy(wsend.at[0], wrecv.at[0], w_ss.at[0], w_rs.at[0], x_prev)
    w1 = copy(wsend.at[1], wrecv.at[1], w_ss.at[1], w_rs.at[1], x_opp)
    w1.start()
    wsend[0] = dot(x_ref[3], pt_ref[...]).astype(jnp.bfloat16)
    x0 = x_ref[0]
    diag_ref[...] = x0.astype(jnp.float32) - dot(x0, pt_ref[...])

    k = iota((1, DEPTH), 1)
    zz = (k * 3277) >> 19
    rem = k - 160 * zz
    hh = jnp.where(rem >= 80, 1, 0)
    m = rem - 80 * hh
    from_k = 32 * (m >> 1) + 4 * zz + 2 * hh + (m & 1)

    def make_pk(i, _):
        base = pl.multiple_of(i * 256, 256)
        pk_ref[pl.ds(base, 256), :] = one_hot(iota((256, DEPTH), 0) + base == from_k)
        return 0

    lax.fori_loop(0, DEPTH // 256, make_pk, 0)
    w1.wait_send()
    w0.start()
    v_copy.wait()

    def make_vp(i, _):
        to = 512 * jnp.where(i // 2 % 2 == core, 1, 0) + 256 * jnp.where(i // 4 == yl, 1, 0) + 128 * (i % 2)
        base = pl.multiple_of(i * 128, 128)
        rows = pl.ds(base, 128)
        label = jnp.broadcast_to(ab_ref[rows].reshape(1, 128), (128, 128)).T
        keep = jnp.concatenate([label] * 10, axis=1) == cd_ref[...].reshape(1, DEPTH)
        masked = jnp.where(keep, v_ref[rows, :].astype(jnp.float32), 0.0).astype(jnp.bfloat16)
        vp_ref[pl.ds(pl.multiple_of(to, 128), 128), :] = dot(masked, pk_ref[...]).astype(jnp.bfloat16)
        return 0

    lax.fori_loop(0, 2, make_vp, 0)

    def encode(values, chunk):
        biggest = jnp.max(jnp.abs(values), axis=1, keepdims=True)
        exponent = jnp.ceil(jnp.log2(jnp.maximum(biggest, 1e-30))) - 15.0
        q = jnp.clip(jnp.floor(values * jnp.exp2(-exponent) + 0.5), -32767.0, 32767.0)
        q = jnp.where(iota((ROWS_T, HALF), 1) < PAD, jnp.broadcast_to(exponent, (ROWS_T, HALF)), q)
        for n in range(5):
            part = q[:, n * LANES:(n + 1) * LANES]
            bq[chunk + n, z, yh] = part.astype(jnp.int32).astype(jnp.int16)

    def hi_copy(n):
        return copy(bq.at[n, z, yh], bq.at[n, z, yh], h_ss.at[n], h_rs.at[n], d_hi)

    def first_copies(n, side):
        at = yh if side == 0 else 1 - yh
        ref = bq.at[n, z, at]
        sem = 4 * side
        return (
            copy(ref, ref, zr_ss.at[n, sem], zr_rs.at[n, sem], d_right),
            copy(ref, ref, zl_ss.at[n, sem], zl_rs.at[n, sem], d_left),
        )

    def right_copy(n, s):
        at = (z - s + NZ) % NZ
        return copy(bq.at[n, at], bq.at[n, at], zr_ss.at[n, s], zr_rs.at[n, s], d_right)

    def left_copy(n, s):
        at = (z + s) % NZ
        return copy(bq.at[n, at], bq.at[n, at], zl_ss.at[n, s], zl_rs.at[n, s], d_left)

    def thin_copies(n, s):
        near, far = (z - s + NZ) % NZ, (z + s) % NZ
        right, left = bq.at[n, near, yh], bq.at[n, far, yh]
        if s == 3:
            right, left = right.at[pl.ds(0, CUT)], left.at[pl.ds(CUT, ROWS_T - CUT)]
        return (
            copy(right, right, zr_ss.at[n, s], zr_rs.at[n, s], d_right),
            copy(left, left, zl_ss.at[n, s], zl_rs.at[n, s], d_left),
        )

    def slot_copies(n, s):
        near, far = bq.at[n, (z - s + NZ) % NZ, yh], bq.at[n, (z + s) % NZ, yh]
        first = copy(near, near, t_ss.at[n - FULL, s - 1], t_rs.at[n - FULL, s - 1], d_hi)
        if s == 4:
            return (first,)
        return first, copy(far, far, t_ss.at[n - FULL, s + 3], t_rs.at[n - FULL, s + 3], d_hi)

    def right_last(n):
        at = (z - 3 + NZ) % NZ
        return copy(bq.at[n, at, 0], bq.at[n, at, 0], zr_ss.at[n, 3], zr_rs.at[n, 3], d_right)

    def left_last(n):
        at = (z + 3) % NZ
        return copy(bq.at[n, at, 1], bq.at[n, at, 1], zl_ss.at[n, 3], zl_rs.at[n, 3], d_left)

    def core_copy(n, h):
        return copy(csend.at[n, h], crecv.at[n, h], c_ss.at[n, h], c_rs.at[n, h], d_core)

    def lo_copy(n):
        return copy(ycode.at[n], yrecv.at[n], y_ss.at[n], y_rs.at[n], d_lo)

    def mirror_copy(n):
        to = (row, (c + 2 - n // 5) % 4, depth)
        return copy(r_own.at[n], r_recv.at[n], m_ss.at[n], m_rs.at[n], to)

    def start_both(pair):
        for one in pair:
            one.start()

    def own_start(n, _):
        hi_copy(n).start()
        start_both(first_copies(n, 0))
        return 0

    w1.wait_recv()
    opposite = x_ref[2].astype(jnp.float32) - wrecv[1].astype(jnp.float32)
    encode(jnp.where(lower, opposite, diag_ref[...]), 0)
    lax.fori_loop(0, 5, own_start, 0)
    make_vp(2, 0)
    w0.wait_recv()
    encode(x_ref[1].astype(jnp.float32) - wrecv[0].astype(jnp.float32), 5)
    lax.fori_loop(5, CHUNKS, own_start, 0)
    make_vp(3, 0)

    def part_start(n):
        hi_copy(n).wait_recv()
        start_both(first_copies(n, 1))

    def forward(n, s):
        before = [(right_copy(n, s - 1), left_copy(n, s - 1))] if s > 1 else [first_copies(n, 0), first_copies(n, 1)]
        after = (right_last(n), left_last(n)) if s == 3 else (right_copy(n, s), left_copy(n, s))
        for side in range(2):
            for pair in before:
                pair[side].wait_recv()
            after[side].start()

    def forward_thin(n, s):
        before = thin_copies(n, s - 1) if s > 1 else first_copies(n, 0)
        after = thin_copies(n, s)
        for side in range(2):
            before[side].wait_recv()
            after[side].start()
        start_both(slot_copies(n, s))

    def end_thin(n):
        for one in thin_copies(n, 3):
            one.wait_recv()
        start_both(slot_copies(n, 4))

    def is_thin(n):
        return (n >= FULL) & (n < FIRST)

    def arrive(n):
        @pl.when(is_thin(n))
        def _():
            hi_copy(n).wait_recv()
            for s in range(1, 5):
                for one in slot_copies(n, s):
                    one.wait_recv()

        @pl.when(jnp.logical_not(is_thin(n)))
        def _():
            right_last(n).wait_recv()
            left_last(n).wait_recv()

    def expand(n):
        q = bq[n].reshape(DEPTH, LANES).astype(jnp.int32)

        @pl.when((n == 0) | (n == 5))
        def _():
            sc_ref[...] = jnp.broadcast_to(jnp.exp2(q[:, 0:1].astype(jnp.float32)), (DEPTH, LANES))

        s = sc_ref[...]
        hi = (q + 128) >> 8
        lo = q - (hi << 8)
        bhl[:, :LANES] = (hi.astype(jnp.float32) * (s * 256.0)).astype(jnp.bfloat16)
        bhl[:, LANES:] = (lo.astype(jnp.float32) * s).astype(jnp.bfloat16)

    def multiply(n):
        both = dot(vp_ref[...], bhl[...])
        both = both[:, :LANES] + both[:, LANES:]
        csend[n] = both[:2 * OUT_ROWS].reshape(2, OUT_ROWS, LANES)
        core_copy(n, 0).start()
        core_copy(n, 1).start()
        ysend[n] = both[2 * OUT_ROWS:3 * OUT_ROWS]
        own[n] = both[3 * OUT_ROWS:]

    def core_arrive(n):
        core_copy(n, 0).wait_recv()
        core_copy(n, 1).wait_recv()

    def core_sum(n):
        part = ysend[n] + crecv[n, 0]
        biggest = jnp.max(jnp.abs(part), axis=0, keepdims=True)
        ex = jnp.ceil(jnp.log2(jnp.maximum(biggest, 1e-30))) - 15.0
        q = jnp.clip(jnp.floor(part * jnp.exp2(-ex) + 0.5), -32767.0, 32767.0)
        ycode[n, :OUT_ROWS] = q.astype(jnp.int32).astype(jnp.int16)
        ycode[n, OUT_ROWS:] = jnp.broadcast_to(ex, (16, LANES)).astype(jnp.int32).astype(jnp.int16)
        own[n] += crecv[n, 1]

    def finish(n):
        lo_copy(n).wait_recv()
        ex = yrecv[n, OUT_ROWS:].astype(jnp.int32).astype(jnp.float32)
        got = yrecv[n, :OUT_ROWS].astype(jnp.int32).astype(jnp.float32) * jnp.exp2(ex[0:1])
        r_own[n] = (own[n] + got).T.astype(jnp.bfloat16)
        mirror_copy(n).start()

    def place(block_ref, group):
        for q in range(4):

            @pl.when((c + group) % 4 == q)
            def _():
                for a in range(SUB):
                    at, to = PAD + SUB * a, OCC * a + SUB * q
                    acc_ref[to:to + SUB, :] = block_ref[at:at + SUB, :]

    def mirror_wait(n, _):
        mirror_copy(n).wait_recv()
        return 0

    def place_opposite():
        rows = iota((HALF, 1), 0) - PAD
        ia = div25(rows)
        ib = rows - SUB * ia
        mine = r_own[0:5].reshape(HALF, OUT_ROWS)
        direct = mine.astype(jnp.float32)
        turned = dot(pt_ref[...], mine)
        tmp_ref[...] = jnp.where(ib > ia, direct, jnp.where(ib < ia, -turned, 0.0))
        place(tmp_ref, 0)
        tmp_ref[...] = jnp.where(ib <= ia, direct, -dot(pt_ref[...], r_recv[0:5].reshape(HALF, OUT_ROWS)))
        place(tmp_ref, 2)

    def place_next():
        tmp_ref[...] = r_own[5:10].reshape(HALF, OUT_ROWS).astype(jnp.float32)
        place(tmp_ref, 1)

    def place_previous():
        tmp_ref[...] = -dot(pt_ref[...], r_recv[5:10].reshape(HALF, OUT_ROWS))
        place(tmp_ref, 3)

    def first_part(n, _):
        part_start(n)
        return 0

    lax.fori_loop(0, FULL, first_part, 0)
    lax.fori_loop(4, 8, make_vp, 0)

    def early(n, _):
        forward(n, 1)
        return 0

    def early_thin(n, _):
        forward_thin(n, 1)
        return 0

    def middle(n, _):
        forward(n, 2)
        return 0

    def middle_thin(n, _):
        forward_thin(n, 2)
        return 0

    def late(n, _):
        forward(n, 3)
        part_start(n + FIRST)
        return 0

    def late_thin(n, _):
        forward_thin(n, 3)
        return 0

    lax.fori_loop(0, FULL, early, 0)
    lax.fori_loop(FULL, FIRST, early_thin, 0)
    lax.fori_loop(0, FULL, middle, 0)
    lax.fori_loop(FULL, FIRST, middle_thin, 0)
    lax.fori_loop(0, FULL, late, 0)
    lax.fori_loop(FULL, FIRST, late_thin, 0)
    part_start(CHUNKS - 1)

    def event(i):
        n = FIRST + i % LAST
        for s in range(1, 4):

            @pl.when(i // LAST == s - 1)
            def _():
                forward(n, s)

    def opening(t, _):
        event(2 * t)
        arrive(t)
        expand(t)
        multiply(t)
        event(2 * t + 1)

        @pl.when(t == 0)
        def _():
            for n in range(FULL, FIRST):
                end_thin(n)

        return 0

    def body(t, _):
        @pl.when(t < FIRST)
        def _():
            event(2 * t)

        arrive(t)
        expand(t)
        multiply(t)

        @pl.when(t < FIRST)
        def _():
            event(2 * t + 1)

        core_arrive(t - 2)
        core_sum(t - 2)
        lo_copy(t - 2).start()

        @pl.when(t >= 5)
        def _():
            finish(t - 5)

        return 0

    lax.fori_loop(0, 2, opening, 0)
    lax.fori_loop(2, CHUNKS, body, 0)

    def finish_some(n, _):
        finish(n)
        return 0

    def drain(n, _):
        hi_copy(n).wait_send()
        for one in first_copies(n, 0):
            one.wait_send()

        @pl.when(is_thin(n))
        def _():
            for s in range(1, 4):
                for one in thin_copies(n, s):
                    one.wait_send()
            for s in range(1, 5):
                for one in slot_copies(n, s):
                    one.wait_send()

        @pl.when(jnp.logical_not(is_thin(n)))
        def _():
            for one in first_copies(n, 1):
                one.wait_send()
            for s in range(1, 3):
                right_copy(n, s).wait_send()
                left_copy(n, s).wait_send()
            right_last(n).wait_send()
            left_last(n).wait_send()

        return 0

    def drain_sums(n, _):
        core_copy(n, 0).wait_send()
        core_copy(n, 1).wait_send()
        lo_copy(n).wait_send()
        return 0

    def drain_mirror(n, _):
        mirror_copy(n).wait_send()
        return 0

    def last_sums(n, _):
        core_arrive(n)
        core_sum(n)
        lo_copy(n).start()
        return 0

    lax.fori_loop(8, CHUNKS, last_sums, 0)
    lax.fori_loop(5, 9, finish_some, 0)
    lax.fori_loop(0, CHUNKS, drain, 0)
    lax.fori_loop(0, 5, mirror_wait, 0)
    place_opposite()
    finish(9)
    w0.wait_send()
    lax.fori_loop(0, CHUNKS, drain_sums, 0)
    place_next()
    lax.fori_loop(5, CHUNKS, mirror_wait, 0)
    place_previous()
    out_ref[...] = acc_ref[...].astype(jnp.bfloat16)
    lax.fori_loop(0, CHUNKS, drain_mirror, 0)


def local(integrals, amplitudes, ab_irrep, cd_irrep):
    vmem = pl.BlockSpec(memory_space=pltpu.VMEM)
    bf, f32 = jnp.bfloat16, jnp.float32
    dma = pltpu.SemaphoreType.DMA
    n = CHUNKS
    scratch = [
        pltpu.VMEM((ROWS_T, WIDE), bf),
        pltpu.VMEM((1024, DEPTH), bf),
        pltpu.VMEM((1024, DEPTH), bf),
        pltpu.VMEM((DEPTH, DEPTH), bf),
        pltpu.VMEM((HALF, HALF), bf),
        pltpu.VMEM((4, ROWS_T, HALF), bf),
        pltpu.VMEM((ROWS_T, HALF), f32),
        pltpu.VMEM((2, ROWS_T, HALF), bf),
        pltpu.VMEM((2, ROWS_T, HALF), bf),
        pltpu.VMEM((n, NZ, 2, ROWS_T, LANES), jnp.int16),
        pltpu.VMEM((DEPTH, LANES), f32),
        pltpu.VMEM((DEPTH, 2 * LANES), bf),
        pltpu.VMEM((n, 2, OUT_ROWS, LANES), f32),
        pltpu.VMEM((n, 2, OUT_ROWS, LANES), f32),
        pltpu.VMEM((n, OUT_ROWS, LANES), f32),
        pltpu.VMEM((n, OUT_ROWS + 16, LANES), jnp.int16),
        pltpu.VMEM((n, OUT_ROWS + 16, LANES), jnp.int16),
        pltpu.VMEM((n, OUT_ROWS, LANES), f32),
        pltpu.VMEM((n, LANES, OUT_ROWS), bf),
        pltpu.VMEM((n, LANES, OUT_ROWS), bf),
        pltpu.VMEM((HALF, OUT_ROWS), f32),
        pltpu.VMEM((OCC * SUB, OUT_ROWS), f32),
        dma,
        dma((2,)), dma((2,)),
        dma((n,)), dma((n,)),
        dma((THIN, 7)), dma((THIN, 7)),
        dma((n, 5)), dma((n, 5)),
        dma((n, 5)), dma((n, 5)),
        dma((n, 2)), dma((n, 2)),
        dma((n,)), dma((n,)),
        dma((n,)), dma((n,)),
    ]
    turned = pl.pallas_call(
        kernel,
        out_shape=jax.ShapeDtypeStruct((OCC * SUB, OUT_ROWS), bf),
        in_specs=[vmem, vmem, vmem, pl.BlockSpec(memory_space=pl.ANY)],
        out_specs=vmem,
        scratch_shapes=scratch,
        compiler_params=pltpu.CompilerParams(
            collective_id=0, has_side_effects=True, vmem_limit_bytes=58 * 2**20
        ),
        name="ladder",
    )(amplitudes, ab_irrep, cd_irrep, integrals)
    return turned.T


def solution(mesh):
    in_specs = (P("row", "depth"), P("depth", "row", "col"), P("row"), P("depth"))
    out_specs = P(("row", "depth"), "col")
    return jax.shard_map(local, mesh=mesh, in_specs=in_specs, out_specs=out_specs, check_vma=False)
```
